32 devices in a mesh: chan: 8 (over y, x, core), batch: 4 (over z).
Axes of the slice: x: 2, y: 2, z: 4, core: 2. Of those that a mesh axis runs over, the one named last changes fastest.
Arguments:
- images: bfloat16 [256, 2, 13, 13, 384], P(('batch', 'chan')), may hold values from -6 to 6
- conv_weight: float32 [2, 3, 3, 384, 256], P(None, None, None, None, 'chan'), may hold values from -0.109375 to 0.109375
- conv_bias: float32 [2, 256], P(None, 'chan'), may hold values from -3 to 3
- stitch_conv: float32 [2, 2, 256], P(None, None, 'chan'), may hold values from 0.1 to 1
- fc_weight: float32 [2, 9216, 4096], P(None, 'batch', 'chan'), may hold values from -0.0625 to 0.0625
- fc_bias: float32 [2, 4096], P(None, 'chan'), may hold values from -3 to 3
- stitch_fc: float32 [2, 2, 4096], P(None, None, 'chan'), may hold values from 0.1 to 1
- conv_moment: float32 [2, 3, 3, 384, 256], P(None, None, None, None, 'chan'), may hold values from -6 to 6
- bias_moment: float32 [2, 256], P(None, 'chan'), may hold values from -6 to 6
- stitch_conv_moment: float32 [2, 2, 256], P(None, None, 'chan'), may hold values from -6 to 6
- fc_moment: float32 [2, 9216, 4096], P(None, 'batch', 'chan'), may hold values from -6 to 6
- fc_bias_moment: float32 [2, 4096], P(None, 'chan'), may hold values from -6 to 6
- stitch_fc_moment: float32 [2, 2, 4096], P(None, None, 'chan'), may hold values from -6 to 6
- cotangent: bfloat16 [256, 2, 4096], P('batch', None, 'chan'), may hold values from -6 to 6
- task_mask: int32 [256, 2], P('batch'), may hold values 0 or 1
Outputs:
- features_out: bfloat16 [256, 2, 4096], P('batch', None, 'chan')
- images_grad: bfloat16 [256, 2, 13, 13, 384], P(('batch', 'chan'))
- new_conv_weight: float32 [2, 3, 3, 384, 256], P(None, None, None, None, 'chan')
- new_conv_bias: float32 [2, 256], P(None, 'chan')
- new_stitch_conv: float32 [2, 2, 256], P(None, None, 'chan')
- new_fc_weight: float32 [2, 9216, 4096], P(None, 'batch', 'chan')
- new_fc_bias: float32 [2, 4096], P(None, 'chan')
- new_stitch_fc: float32 [2, 2, 4096], P(None, None, 'chan')
- new_conv_moment: float32 [2, 3, 3, 384, 256], P(None, None, None, None, 'chan')
- new_bias_moment: float32 [2, 256], P(None, 'chan')
- new_stitch_conv_moment: float32 [2, 2, 256], P(None, None, 'chan')
- new_fc_moment: float32 [2, 9216, 4096], P(None, 'batch', 'chan')
- new_fc_bias_moment: float32 [2, 4096], P(None, 'chan')
- new_stitch_fc_moment: float32 [2, 2, 4096], P(None, None, 'chan')
The draws below stay inside these ranges and needn't reach their ends.
All inputs are finite; a program needn't handle non-finite values. No bound on the sum of `task_mask` on one device may be relied on, other than what follows from the above.
Results may differ from the reference program's by a relative error of at most 0.015.
Values may be sent and summed in bfloat16 or wider, within the bound.
No kernel may reach another device: no remote copies, remote signals or barrier semaphores. Data moves between devices by JAX's collectives and lax.ppermute only.
A program may use at most 128 MiB of HBM per device.

```python
import jax
import jax.numpy as jnp
from jax import lax

CIN = 384
C5 = 256
FF = 4096
SIDE = 13
FEAT = 9216
IMAGES = 256


def with_ends(array, own_key, low, high):
    spot = [jax.random.randint(jax.random.fold_in(own_key, axis), (), 0, length) for axis, length in enumerate(array.shape)]
    widest = array.shape.index(max(array.shape))
    neighbour = spot[:widest] + [(spot[widest] + 1) % array.shape[widest]] + spot[widest + 1:]
    return array.at[tuple(spot)].set(low).at[tuple(neighbour)].set(high)


def shard_levels(key, dims, cuts, least, top_value):
    factor_of, own = 1.0, jax.random.fold_in(key, 6)
    for dim, parts in cuts:
        heights = jnp.exp(jax.random.uniform(jax.random.fold_in(own, dim), (parts,), jnp.float32, least / len(cuts), top_value / len(cuts)))
        factor_of = factor_of * jnp.repeat(heights, dims[dim] // parts).reshape([-1 if axis == dim else 1 for axis in range(len(dims))])
    return factor_of


def scatter_about(own_key, extent, deviation, reach, shards=(), held_as=jnp.bfloat16):
    array = deviation * jax.random.normal(own_key, extent, jnp.float32)
    if shards:
        array = array * shard_levels(own_key, extent, shards, -0.22, 0.18)
    return jnp.clip(array, -reach, reach).astype(held_as)


def setup_inputs(seed: int = 0) -> dict:
    key_list = jax.random.split(jax.random.key(seed), 16)
    images = scatter_about(key_list[0], (IMAGES, 2, SIDE, SIDE, CIN), 1.0, 6.0, ((0, 32),))
    conv_weight = scatter_about(key_list[1], (2, 3, 3, CIN, C5), (9 * CIN) ** -0.5, 0.109375, ((4, 8),), jnp.float32)
    conv_bias = scatter_about(key_list[2], (2, C5), 0.5, 3.0, ((1, 8),), jnp.float32)
    stitch_conv = jnp.clip(0.1 + 0.9 * jax.random.uniform(key_list[3], (2, 2, C5), jnp.float32) ** shard_levels(key_list[3], (2, 2, C5), ((2, 8),), -0.2, 0.2), 0.1, 1.0)
    fc_weight = scatter_about(key_list[4], (2, FEAT, FF), FEAT ** -0.5, 0.0625, ((1, 4), (2, 8)), jnp.float32)
    fc_bias = scatter_about(key_list[5], (2, FF), 0.5, 3.0, ((1, 8),), jnp.float32)
    stitch_fc = jnp.clip(0.1 + 0.9 * jax.random.uniform(key_list[6], (2, 2, FF), jnp.float32) ** shard_levels(key_list[6], (2, 2, FF), ((2, 8),), -0.2, 0.2), 0.1, 1.0)
    conv_moment = scatter_about(key_list[7], (2, 3, 3, CIN, C5), 1.0, 6.0, ((4, 8),), jnp.float32)
    bias_moment = scatter_about(key_list[8], (2, C5), 1.0, 6.0, ((1, 8),), jnp.float32)
    stitch_conv_moment = scatter_about(key_list[9], (2, 2, C5), 1.0, 6.0, ((2, 8),), jnp.float32)
    fc_moment = scatter_about(key_list[10], (2, FEAT, FF), 1.0, 6.0, ((1, 4), (2, 8)), jnp.float32)
    fc_bias_moment = scatter_about(key_list[11], (2, FF), 1.0, 6.0, ((1, 8),), jnp.float32)
    stitch_fc_moment = scatter_about(key_list[12], (2, 2, FF), 1.0, 6.0, ((2, 8),), jnp.float32)
    cotangent = scatter_about(key_list[13], (IMAGES, 2, FF), 1.0, 6.0, ((0, 4), (2, 8)))
    task_mask = with_ends((jax.random.randint(key_list[14], (IMAGES, 2), 0, 4) < 3).astype(jnp.int32), jax.random.fold_in(key_list[14], 1), 0, 1)
    return dict(images=images, conv_weight=conv_weight, conv_bias=conv_bias, stitch_conv=stitch_conv, fc_weight=fc_weight, fc_bias=fc_bias, stitch_fc=stitch_fc, conv_moment=conv_moment, bias_moment=bias_moment, stitch_conv_moment=stitch_conv_moment, fc_moment=fc_moment, fc_bias_moment=fc_bias_moment, stitch_fc_moment=stitch_fc_moment, cotangent=cotangent, task_mask=task_mask)


MOMENTUM = 0.9
LEARN_RATE = 0.002
BIAS_RATE = 0.02
STITCH_RATE = 0.02

@jax.custom_vjp
def low(v):
    return lax.optimization_barrier(v.astype(jnp.bfloat16)).astype(jnp.float32)

@jax.custom_vjp
def low_back(v):
    return v

def low_keep(v):
    return (low(v), None)

def low_pass(kept, grad):
    return (grad,)

def back_keep(v):
    return (v, None)

def back_low(kept, grad):
    return (low(grad),)
low.defvjp(low_keep, low_pass)
low_back.defvjp(back_keep, back_low)

def pool_axis(values, dimension):
    steps_out = (values.shape[dimension] - 1) // 2
    total = 0.0
    for offset in range(3):
        total = total + lax.slice_in_dim(values, offset, offset + 2 * steps_out - 1, 2, dimension)
    return total / 3.0

def stitch(mixing, values):
    first = mixing[0, 0] * values[:, 0] + mixing[0, 1] * values[:, 1]
    second = mixing[1, 0] * values[:, 0] + mixing[1, 1] * values[:, 1]
    return jnp.stack([first, second], axis=1)

def forward(images, conv_weight, conv_bias, stitch_conv, fc_weight, fc_bias, stitch_fc):
    kernel = low(conv_weight)
    bias_low = low(conv_bias)
    mixing = low(stitch_conv)
    fc_low = low(fc_weight)
    conv_out = jnp.stack([lax.conv_general_dilated(images[:, member], kernel[member], (1, 1), 'SAME', dimension_numbers=('NHWC', 'HWIO', 'NHWC'), precision=lax.Precision.HIGHEST) for member in range(2)], axis=1)
    conv_out = low_back(conv_out + bias_low[None, :, None, None, :])
    pooled = pool_axis(pool_axis(jax.nn.silu(conv_out), 2), 3)
    mixed = stitch(mixing, pooled)
    flattened = low(jnp.transpose(mixed, (0, 1, 4, 2, 3)).reshape(mixed.shape[0], 2, -1))
    fc_out = jnp.einsum('ntf,tfu->ntu', flattened, fc_low, precision=lax.Precision.HIGHEST) + fc_bias[None]
    fc_out = low_back(fc_out)
    return stitch(stitch_fc, jax.nn.silu(fc_out))

def reference(images, conv_weight, conv_bias, stitch_conv, fc_weight, fc_bias, stitch_fc, conv_moment, bias_moment, stitch_conv_moment, fc_moment, fc_bias_moment, stitch_fc_moment, cotangent, task_mask):
    result, pullback = jax.vjp(forward, images.astype(jnp.float32), conv_weight, conv_bias, stitch_conv, fc_weight, fc_bias, stitch_fc)
    out_grad = cotangent.astype(jnp.float32) * task_mask.astype(jnp.float32)[:, :, None]
    grads = pullback(out_grad)
    params = (conv_weight, conv_bias, stitch_conv, fc_weight, fc_bias, stitch_fc)
    moments = (conv_moment, bias_moment, stitch_conv_moment, fc_moment, fc_bias_moment, stitch_fc_moment)
    rates = (LEARN_RATE, BIAS_RATE, STITCH_RATE, LEARN_RATE, BIAS_RATE, STITCH_RATE)
    fresh = [MOMENTUM * moments[place] + grads[place + 1] for place in range(6)]
    updated = [params[place] - rates[place] * fresh[place] for place in range(6)]
    return (result.astype(jnp.bfloat16), grads[0].astype(jnp.bfloat16), updated[0], updated[1], updated[2], updated[3], updated[4], updated[5], fresh[0], fresh[1], fresh[2], fresh[3], fresh[4], fresh[5])
```

```python
import jax
import jax.numpy as jnp
from jax import lax
from jax.sharding import PartitionSpec as P

MOMENTUM = 0.9
LEARN_RATE = 0.002
BIAS_RATE = 0.02
STITCH_RATE = 0.02
LOW = jnp.bfloat16
WIDE = jnp.float32


def trade(value, axis, bit):
    size = lax.axis_size(axis)
    return lax.ppermute(value, axis, [(i, i ^ bit) for i in range(size)])


def reorder(parts, place):
    bit = 1
    while bit < len(parts):
        flip = (place & bit) != 0
        parts = [
            jax.tree.map(lambda a, b: jnp.where(flip, b, a), parts[j], parts[j ^ bit])
            for j in range(len(parts))
        ]
        bit *= 2
    return parts


def pick(stacked, place, count):
    return [lax.dynamic_index_in_dim(stacked, place ^ j, 0, keepdims=False) for j in range(count)]


def gather_chips(first, second, chips):
    if chips == 4:
        second_x = trade(second, "chan", 2)
        first_y = trade(first, "chan", 4)
        first_x = trade(first, "chan", 2)
        second_y = trade(second, "chan", 4)
        first_d = trade(first_y, "chan", 2)
        second_d = trade(second_x, "chan", 4)
        return [(first, second), (first_x, second_x), (first_y, second_y), (first_d, second_d)]
    return [(first, second)] + [
        (trade(first, "chan", 2 * j), trade(second, "chan", 2 * j)) for j in range(1, chips)
    ]


def scatter_chips(parts, chips):
    if chips == 4:
        from_x = trade(parts[3][0], "chan", 2)
        from_y = trade(parts[3][1], "chan", 4)
        first_x = trade(parts[1][0], "chan", 2)
        second_y = trade(parts[2][1], "chan", 4)
        first_y = trade(add_low(parts[2][0], from_x), "chan", 4)
        second_x = trade(add_low(parts[1][1], from_y), "chan", 2)
        return (parts[0][0], first_x, first_y), (parts[0][1], second_x, second_y)
    got = [(trade(parts[j][0], "chan", 2 * j), trade(parts[j][1], "chan", 2 * j)) for j in range(1, chips)]
    return (
        (parts[0][0],) + tuple(pair[0] for pair in got),
        (parts[0][1],) + tuple(pair[1] for pair in got),
    )


def add_low(a, b):
    return (a.astype(WIDE) + b.astype(WIDE)).astype(LOW)


def total(values):
    out = values[0].astype(WIDE)
    for value in values[1:]:
        out = out + value.astype(WIDE)
    return out


def exchange_planes(parts):
    got = {k: trade(parts[k], "batch", k) for k in range(len(parts) - 1, 0, -1)}
    return [parts[0]] + [got[k] for k in range(1, len(parts))]


def silu_and_slope(value):
    gate = jax.nn.sigmoid(value)
    act = value * gate
    return act, gate + act * (1.0 - gate)


def pool(values):
    rows = values[0:11:2] + values[1:12:2] + values[2:13:2]
    return (rows[:, 0:11:2] + rows[:, 1:12:2] + rows[:, 2:13:2]) * (1.0 / 9.0)


def spread(values, axis):
    values = jnp.moveaxis(values, axis, 0)
    zero = jnp.zeros_like(values[:1])
    even = jnp.concatenate([values, zero]) + jnp.concatenate([zero, values])
    inter = jnp.stack([even[:-1], values], axis=1).reshape((12,) + values.shape[1:])
    return jnp.moveaxis(jnp.concatenate([inter, even[-1:]]), 0, axis)


def body(
    images,
    conv_weight,
    conv_bias,
    stitch_conv,
    fc_weight,
    fc_bias,
    stitch_fc,
    conv_moment,
    bias_moment,
    stitch_conv_moment,
    fc_moment,
    fc_bias_moment,
    stitch_fc_moment,
    cotangent,
    task_mask,
):
    chan_size, planes = lax.axis_size("chan"), lax.axis_size("batch")
    chips = chan_size // 2
    me, plane = lax.axis_index("chan"), lax.axis_index("batch")
    core, chip = me % 2, me // 2
    swap = lambda value: trade(value, "chan", 1)
    mine = lambda a, b: jnp.where(core == 0, a, b)
    per_core, side, width_in = images.shape[0], images.shape[2], images.shape[-1]
    chan_width = conv_weight.shape[-1]
    full_chan = chan_width * chan_size
    units = fc_weight.shape[-1]
    rows = fc_weight.shape[1]
    cells = 36
    plane_chan = rows // cells
    group = 2 * per_core

    kernel_rows = jnp.transpose(conv_weight, (0, 1, 2, 4, 3)).astype(LOW)
    kernel_rows = kernel_rows.reshape(2, 9 * chan_width, width_in)
    cross = stitch_conv[:, ::-1]
    small = jnp.stack(
        [
            conv_bias,
            jnp.stack([stitch_conv[0, 0], stitch_conv[1, 1]]),
            jnp.stack([stitch_conv[0, 1], stitch_conv[1, 0]]),
            jnp.stack([stitch_conv[1, 0], stitch_conv[0, 1]]),
        ],
        axis=1,
    ).astype(LOW)
    small = jnp.pad(small, ((0, 0), (0, 12), (0, width_in - chan_width)))
    kernel_rows = jnp.concatenate([kernel_rows, small], axis=1)
    keep = mine(kernel_rows[0], kernel_rows[1])
    got = swap(mine(kernel_rows[1], kernel_rows[0]))
    halves = mine(keep, got), mine(got, keep)
    kernel_parts = gather_chips(halves[0], halves[1], chips)

    keep = mine(images[:, 0], images[:, 1])
    got = swap(mine(images[:, 1], images[:, 0]))
    tower_images = jnp.concatenate([mine(keep, got), mine(got, keep)], axis=0)
    tower_images = jnp.transpose(tower_images, (1, 2, 0, 3))

    fc_low = fc_weight.astype(LOW).reshape(2, plane_chan, cells, units)
    fc_low = jnp.swapaxes(fc_low, 1, 2).reshape(2, rows, units)
    fc_keep = mine(fc_low[0], fc_low[1])
    fc_got = swap(mine(fc_low[1], fc_low[0]))
    fc_halves = mine(fc_keep, fc_got), mine(fc_got, fc_keep)

    ordered = reorder(kernel_parts, chip)
    kernel = jnp.concatenate(
        [half[: 9 * chan_width].reshape(9, chan_width, width_in) for pair in ordered for half in pair],
        axis=1,
    )
    small_all = jnp.concatenate(
        [half[9 * chan_width :, :chan_width] for pair in ordered for half in pair], axis=1
    ).astype(WIDE)
    bias_all, self_mix, cross_mix, back_mix = (small_all[i] for i in range(4))

    conv_out = lax.conv_general_dilated(
        tower_images,
        kernel.reshape(3, 3, full_chan, width_in),
        (1, 1),
        "SAME",
        dimension_numbers=("HWNC", "HWOI", "HWNC"),
        preferred_element_type=WIDE,
    )
    act, slope = silu_and_slope(conv_out + bias_all)
    pooled = pool(act)
    pooled_other = swap(pooled)
    mixed = (self_mix * pooled + cross_mix * pooled_other).astype(LOW)
    mixed = mixed.reshape(cells, group, planes, plane_chan)
    pieces = jnp.transpose(mixed, (2, 1, 0, 3)).reshape(planes, group, rows)
    got = exchange_planes(pick(pieces, plane, planes))
    half = planes // 2
    gathered = reorder(
        gather_chips(jnp.stack(got[:half]), jnp.stack(got[half:]), chips), chip
    )
    tower_rows = jnp.concatenate(
        [jnp.stack([pair[h] for pair in gathered], axis=1) for h in range(2)], axis=0
    )
    tower_rows = tower_rows.reshape(planes * chips * group, rows)
    other_rows = swap(tower_rows)

    fc_tower = jnp.concatenate(fc_halves, axis=1)
    partial = jnp.dot(tower_rows, fc_tower, preferred_element_type=WIDE).astype(LOW)
    partial = partial.reshape(planes, chips * group, 2 * units)
    fc_sum = total(exchange_planes([partial[k] for k in range(planes)]))
    fc_keep = mine(fc_sum[:, :units], fc_sum[:, units:])
    fc_got = swap(mine(fc_sum[:, units:], fc_sum[:, :units]))
    fc_out = [mine(fc_keep, fc_got) + fc_bias[0], mine(fc_got, fc_keep) + fc_bias[1]]

    acts, slopes = zip(*[silu_and_slope(value) for value in fc_out])
    features_out = jnp.stack(
        [stitch_fc[t, 0] * acts[0] + stitch_fc[t, 1] * acts[1] for t in range(2)], axis=1
    ).astype(LOW)
    out_grad = [
        cotangent[:, t].astype(WIDE) * task_mask[:, t].astype(WIDE)[:, None] for t in range(2)
    ]
    stitch_fc_grad = jnp.stack(
        [jnp.stack([jnp.sum(out_grad[t] * acts[s], axis=0) for s in range(2)]) for t in range(2)]
    )
    grad_low = jnp.stack(
        [
            (slopes[s] * (stitch_fc[0, s] * out_grad[0] + stitch_fc[1, s] * out_grad[1])).astype(LOW)
            for s in range(2)
        ]
    )
    grad_all = exchange_planes([grad_low] * planes)
    grad_all = jnp.stack(grad_all, axis=1).reshape(2, planes * chips * group, units)
    grad_keep = mine(grad_all[0], grad_all[1])
    grad_got = swap(mine(grad_all[1], grad_all[0]))
    grad_tower = jnp.concatenate([mine(grad_keep, grad_got), mine(grad_got, grad_keep)], axis=1)

    flat_grad = lax.dot_general(
        grad_tower, fc_tower, (((1,), (1,)), ((), ())), preferred_element_type=WIDE
    ).astype(LOW)
    flat_grad = flat_grad.reshape(2, half, chips, group, rows)
    by_chip = reorder([(flat_grad[0, :, m], flat_grad[1, :, m]) for m in range(chips)], chip)
    first, second = scatter_chips(by_chip, chips)
    sums = jnp.concatenate([total(first), total(second)]).astype(LOW)
    got = reorder(exchange_planes([sums[k] for k in range(planes)]), plane)
    mixed_grad = jnp.stack(got)
    mixed_grad_other = swap(mixed_grad)

    def unflatten(value):
        value = value.astype(WIDE).reshape(planes, group, cells, plane_chan)
        return jnp.transpose(value, (2, 1, 0, 3)).reshape(6, 6, group, full_chan)

    own_grad, other_grad = unflatten(mixed_grad), unflatten(mixed_grad_other)
    self_stitch = jnp.sum(own_grad * pooled, axis=(0, 1, 2))
    cross_stitch = jnp.sum(own_grad * pooled_other, axis=(0, 1, 2))
    pooled_grad = (self_mix * own_grad + back_mix * other_grad) * (1.0 / 9.0)
    conv_grad = (slope * spread(spread(pooled_grad, 0), 1)).astype(LOW)
    bias_grad = jnp.sum(conv_grad.astype(WIDE), axis=(0, 1, 2))

    padded = jnp.pad(tower_images, ((1, 1), (1, 1), (0, 0), (0, 0)))
    taps = []
    for down in range(3):
        for right in range(3):
            window = padded[down : down + side, right : right + side]
            taps.append(
                lax.dot_general(
                    conv_grad.reshape(-1, full_chan),
                    window.reshape(-1, width_in),
                    (((0,), (0,)), ((), ())),
                    preferred_element_type=WIDE,
                ).astype(LOW)
            )
    kernel_grad = jnp.stack(taps).reshape(9, chips, 2, chan_width, width_in)
    smalls = jnp.stack([bias_grad, self_stitch, cross_stitch]).astype(LOW)
    smalls = jnp.pad(
        smalls.reshape(3, chips, 2, chan_width), ((0, 13), (0, 0), (0, 0), (0, width_in - chan_width))
    )
    blocks = [
        tuple(
            jnp.concatenate([kernel_grad[:, m, c].reshape(9 * chan_width, width_in), smalls[:, m, c]])
            for c in range(2)
        )
        for m in range(chips)
    ]
    first, second = scatter_chips(reorder(blocks, chip), chips)
    sums = [total(first).astype(LOW), total(second).astype(LOW)]
    keep = mine(sums[0], sums[1])
    got = swap(mine(sums[1], sums[0]))
    towers = jnp.stack([mine(keep, got), mine(got, keep)])
    towers = lax.psum(towers, "batch").astype(WIDE)
    stitch_fc_grad = lax.psum(stitch_fc_grad.astype(LOW), "batch").astype(WIDE)

    images_grad = lax.conv_general_dilated(
        conv_grad,
        kernel.reshape(3, 3, full_chan, width_in)[::-1, ::-1],
        (1, 1),
        "SAME",
        dimension_numbers=("HWNC", "HWIO", "HWNC"),
        preferred_element_type=WIDE,
    ).astype(LOW)
    images_grad = jnp.transpose(images_grad, (2, 0, 1, 3))
    keep = mine(images_grad[:per_core], images_grad[per_core:])
    got = swap(mine(images_grad[per_core:], images_grad[:per_core]))
    images_grad = jnp.stack([mine(keep, got), mine(got, keep)], axis=1)

    both_rows = [mine(tower_rows, other_rows), mine(other_rows, tower_rows)]
    fc_weight_grad = jnp.stack(
        [
            lax.dot_general(
                jnp.swapaxes(both_rows[t].reshape(-1, cells, plane_chan), 1, 2).reshape(-1, rows),
                grad_all[t],
                (((0,), (0,)), ((), ())),
                preferred_element_type=WIDE,
            )
            for t in range(2)
        ]
    )
    fc_bias_grad = jnp.sum(grad_all.astype(WIDE), axis=1)

    conv_weight_grad = jnp.swapaxes(
        towers[:, : 9 * chan_width].reshape(2, 3, 3, chan_width, width_in), 3, 4
    )
    conv_bias_grad = towers[:, 9 * chan_width, :chan_width]
    straight = towers[:, 9 * chan_width + 1, :chan_width]
    crossed = towers[:, 9 * chan_width + 2, :chan_width]
    stitch_conv_grad = jnp.stack(
        [jnp.stack([straight[0], crossed[0]]), jnp.stack([crossed[1], straight[1]])]
    )
    grads = (
        conv_weight_grad,
        conv_bias_grad,
        stitch_conv_grad,
        fc_weight_grad,
        fc_bias_grad,
        stitch_fc_grad,
    )
    params = (conv_weight, conv_bias, stitch_conv, fc_weight, fc_bias, stitch_fc)
    moments = (
        conv_moment,
        bias_moment,
        stitch_conv_moment,
        fc_moment,
        fc_bias_moment,
        stitch_fc_moment,
    )
    rates = (LEARN_RATE, BIAS_RATE, STITCH_RATE, LEARN_RATE, BIAS_RATE, STITCH_RATE)
    fresh = [MOMENTUM * moments[place] + grads[place] for place in range(6)]
    updated = [params[place] - rates[place] * fresh[place] for place in range(6)]
    return (features_out, images_grad, *updated, *fresh)


def solution(mesh):
    chan_last = P(None, None, None, None, "chan")
    fc_spec = P(None, "batch", "chan")
    params = (chan_last, P(None, "chan"), P(None, None, "chan"), fc_spec, P(None, "chan"), P(None, None, "chan"))
    image_spec = P(("batch", "chan"), None, None, None, None)
    feature_spec = P("batch", None, "chan")
    in_specs = (image_spec, *params, *params, feature_spec, P("batch", None))
    out_specs = (feature_spec, image_spec, *params, *params)
    return jax.shard_map(body, mesh=mesh, in_specs=in_specs, out_specs=out_specs, check_vma=False)
```

```python
import functools

import jax
import jax.numpy as jnp
from jax import lax
from jax.experimental import pallas as pl
from jax.experimental.pallas import tpu as pltpu
from jax.sharding import PartitionSpec as P

MOMENTUM = 0.9
LEARN_RATE = 0.002
BIAS_RATE = 0.02
STITCH_RATE = 0.02
LOW = jnp.bfloat16
WIDE = jnp.float32
TAPS = 9
CELLS = 36
EXTRA = 16
LANES = 128
WHOLE = pl.BlockSpec(memory_space=pltpu.VMEM)
SCALARS = pl.BlockSpec(memory_space=pltpu.SMEM)
NN = (((1,), (0,)), ((), ()))
NT = (((1,), (1,)), ((), ()))
TN = (((0,), (0,)), ((), ()))


def like(shape, dtype):
    return jax.ShapeDtypeStruct(shape, dtype)


def dot(a, b, dims):
    return lax.dot_general(a, b, dims, preferred_element_type=WIDE)


def trade(value, axis, bit):
    size = lax.axis_size(axis)
    return lax.ppermute(value, axis, [(i, i ^ bit) for i in range(size)])


def gather_chips(first, second, chips):
    if chips == 4:
        second_x = trade(second, "chan", 2)
        first_y = trade(first, "chan", 4)
        first_x = trade(first, "chan", 2)
        second_y = trade(second, "chan", 4)
        first_d = trade(first_y, "chan", 2)
        second_d = trade(second_x, "chan", 4)
        return [(first, second), (first_x, second_x), (first_y, second_y), (first_d, second_d)]
    return [(first, second)] + [
        (trade(first, "chan", 2 * j), trade(second, "chan", 2 * j)) for j in range(1, chips)
    ]


def add_low(a, b):
    return (a.astype(WIDE) + b.astype(WIDE)).astype(LOW)


def scatter_chips(parts, chips):
    if chips == 4:
        from_x = trade(parts[3][0], "chan", 2)
        from_y = trade(parts[3][1], "chan", 4)
        first_x = trade(parts[1][0], "chan", 2)
        second_y = trade(parts[2][1], "chan", 4)
        first_y = trade(add_low(parts[2][0], from_x), "chan", 4)
        second_x = trade(add_low(parts[1][1], from_y), "chan", 2)
        return (parts[0][0], first_x, first_y), (parts[0][1], second_x, second_y)
    got = [(trade(parts[j][0], "chan", 2 * j), trade(parts[j][1], "chan", 2 * j)) for j in range(1, chips)]
    return (
        (parts[0][0],) + tuple(pair[0] for pair in got),
        (parts[0][1],) + tuple(pair[1] for pair in got),
    )


def total(values):
    out = values[0].astype(WIDE)
    for value in values[1:]:
        out = out + value.astype(WIDE)
    return out


def exchange_planes(parts):
    got = {k: trade(parts[k], "batch", k) for k in range(len(parts) - 1, 0, -1)}
    return [parts[0]] + [got[k] for k in range(1, len(parts))]


def gate_of(value):
    return 1.0 / (1.0 + jnp.exp(-value))


def silu_and_slope(value):
    gate = gate_of(value)
    act = value * gate
    return act, gate + act * (1.0 - gate)


def lane_place(width):
    return lax.broadcasted_iota(jnp.int32, (1, LANES), 1) // width


def shift_slots(value, width, source, target):
    if source == target:
        return value
    return pltpu.roll(value, ((target - source) * width) % LANES, 1)


def fc_prepare(fc_weight, core):
    towers, rows, units = fc_weight.shape
    width = rows // CELLS

    def kernel(core_ref, w_ref, o_ref):
        for cell in range(CELLS):
            o_ref[0, pl.ds(cell * width, width), :] = w_ref[
                0, pl.ds(cell, width, stride=CELLS), :
            ].astype(LOW)

    return pl.pallas_call(
        kernel,
        grid_spec=pltpu.PrefetchScalarGridSpec(
            num_scalar_prefetch=1,
            grid=(towers, units // LANES),
            in_specs=[pl.BlockSpec((1, rows, LANES), lambda i, j, core: (core[0] ^ i, 0, j))],
            out_specs=pl.BlockSpec((1, rows, LANES), lambda i, j, core: (i, 0, j)),
        ),
        out_shape=like(fc_weight.shape, LOW),
        compiler_params=pltpu.CompilerParams(vmem_limit_bytes=8 << 20),
        cost_estimate=pl.CostEstimate(flops=0, bytes_accessed=6 * fc_weight.size, transcendentals=0),
    )(core, fc_weight)


def conv_forward(images, parts, core, chip):
    high, wide, group, width_in = images.shape
    side = high - 2
    count = len(parts)
    shard = (parts[0].shape[0] - EXTRA) // TAPS
    full = shard * count
    slots = LANES // shard

    def kernel(core_ref, chip_ref, x_ref, *refs):
        pieces = refs[:count]
        pooled_ref, slope_ref, small_ref = refs[count : count + 3]
        joined, weights, acc, act = refs[count + 3 :]
        lane = lax.broadcasted_iota(jnp.int32, (EXTRA, LANES), 1) // shard
        smalls = [jnp.zeros((EXTRA, LANES), WIDE) for _ in range(full // LANES)]
        for j in range(count // 2):
            for r in range(2):
                piece = pieces[2 * j + r]
                where = (chip_ref[0] ^ j) * 2 + (core_ref[0] ^ r)
                at = pl.ds(pl.multiple_of(where * shard, shard), shard)
                for tap in range(TAPS):
                    weights[tap // 3, at, (tap % 3) * width_in : (tap % 3 + 1) * width_in] = piece[
                        tap * shard : (tap + 1) * shard, :
                    ]
                row = piece[TAPS * shard :, :LANES].astype(WIDE)
                copies = row
                for s in range(1, slots):
                    copies = copies + pltpu.roll(row, s * shard, 1)
                for v in range(len(smalls)):
                    smalls[v] = jnp.where(lane + v * slots == where, copies, smalls[v])
        for v, value in enumerate(smalls):
            small_ref[:, v * LANES : (v + 1) * LANES] = value
        for right in range(3):
            joined[:, :, :, right * width_in : (right + 1) * width_in] = x_ref[:, right : right + side]
        for down in range(3):
            part = dot(
                joined[down : down + side].reshape(side * side * group, 3 * width_in),
                weights[down],
                NT,
            )
            if down == 0:
                acc[...] = part
            else:
                acc[...] += part
        bias = small_ref[0:1, :]
        line = side * group
        for h in range(side):
            value, slope = silu_and_slope(acc[h * line : (h + 1) * line, :] + bias)
            slope_ref[h] = slope.reshape(side, group, full).astype(LOW)
            act[h] = value.reshape(side, group, full)
        for r in range(6):
            rows = act[2 * r] + act[2 * r + 1] + act[2 * r + 2]
            for c in range(6):
                pooled_ref[6 * r + c] = (rows[2 * c] + rows[2 * c + 1] + rows[2 * c + 2]) * (1.0 / 9.0)

    area = side * side * group
    return pl.pallas_call(
        kernel,
        in_specs=[SCALARS] * 2 + [WHOLE] * (1 + count),
        out_specs=[WHOLE] * 3,
        out_shape=[
            like((CELLS, group, full), WIDE),
            like((side, side, group, full), LOW),
            like((EXTRA, full), WIDE),
        ],
        scratch_shapes=[
            pltpu.VMEM((high, side, group, 3 * width_in), LOW),
            pltpu.VMEM((3, full, 3 * width_in), LOW),
            pltpu.VMEM((area, full), WIDE),
            pltpu.VMEM((side, side, group, full), WIDE),
        ],
        compiler_params=pltpu.CompilerParams(vmem_limit_bytes=28 << 20),
        cost_estimate=pl.CostEstimate(
            flops=2 * area * TAPS * width_in * full,
            bytes_accessed=2 * images.size + 2 * area * full,
            transcendentals=0,
        ),
    )(core, chip, images, *parts)


def mix_pieces(pooled, other, small, plane, planes):
    cells, group, full = pooled.shape
    width = full // planes
    per = LANES // width

    def kernel(plane_ref, a_ref, b_ref, small_ref, *refs):
        outs, held = refs[:planes], refs[planes]
        place = lane_place(width)
        one, two = small_ref[1:2, :], small_ref[2:3, :]
        for start in range(0, cells, per):
            mixed = [
                one * a_ref[start + i] + two * b_ref[start + i] for i in range(per)
            ]
            for p in range(planes):
                column, source = divmod(p * width, LANES)
                out = None
                for i in range(per):
                    moved = shift_slots(
                        mixed[i][:, column * LANES : (column + 1) * LANES], width, source // width, i
                    )
                    out = moved if out is None else jnp.where(place == i, moved, out)
                held[p, :, start * width : (start + per) * width] = out.astype(LOW)
        for k in range(planes):
            outs[k][...] = held[plane_ref[0] ^ k]

    rows = cells * width
    return pl.pallas_call(
        kernel,
        in_specs=[SCALARS] + [WHOLE] * 3,
        out_specs=[WHOLE] * planes,
        out_shape=[like((group, rows), LOW)] * planes,
        scratch_shapes=[pltpu.VMEM((planes, group, rows), LOW)],
        compiler_params=pltpu.CompilerParams(vmem_limit_bytes=8 << 20),
        cost_estimate=pl.CostEstimate(flops=4 * pooled.size, bytes_accessed=8 * pooled.size, transcendentals=0),
    )(plane, pooled, other, small)


def fc_forward(gathered, weights, chip, chips, planes):
    half, group, rows = gathered[0].shape
    units = weights[0].shape[-1]
    count = 2 * chips
    block = chips * group

    def kernel(chip_ref, *refs):
        pieces, (own, cross) = refs[:count], refs[count : count + 2]
        rows_ref, outs = refs[count + 2], refs[count + 3 :]
        for j in range(chips):
            for h in range(2):
                for i in range(half):
                    start = ((h * half + i) * chips + (chip_ref[0] ^ j)) * group
                    rows_ref[pl.ds(pl.multiple_of(start, group), group), :] = pieces[2 * j + h][i]
        for n, weight in enumerate((own, cross)):
            part = dot(rows_ref[...], weight[...], NN)
            for k in range(planes):
                outs[k][:, n * units : (n + 1) * units] = part[k * block : (k + 1) * block].astype(
                    outs[k].dtype
                )

    n_images = planes * block
    return pl.pallas_call(
        kernel,
        in_specs=[SCALARS] + [WHOLE] * (count + 2),
        out_specs=[WHOLE] * (1 + planes),
        out_shape=[like((n_images, rows), LOW)]
        + [like((block, 2 * units), LOW if k else WIDE) for k in range(planes)],
        compiler_params=pltpu.CompilerParams(vmem_limit_bytes=16 << 20),
        cost_estimate=pl.CostEstimate(
            flops=4 * n_images * rows * units, bytes_accessed=4 * rows * units, transcendentals=0
        ),
    )(chip, *gathered, *weights)


def fc_backward(grads, crossed, weights, chip, chips, planes):
    _, block, units = grads[0].shape
    rows = weights[0].shape[0]
    group = block // chips
    half = planes // 2
    n_images = planes * block

    def kernel(chip_ref, *refs):
        pieces, got = refs[:planes], refs[planes]
        own, cross = refs[planes + 1 : planes + 3]
        outs = refs[planes + 3 : planes + 3 + 2 * chips]
        held_own, held_cross, held = refs[planes + 3 + 2 * chips :]
        for k in range(planes):
            held_own[pl.ds(k * block, block), :] = pieces[k][0]
            held_cross[pl.ds(k * block, block), :] = got[k]
        step = rows // 3
        for s in range(3):
            at = pl.ds(s * step, step)
            value = dot(held_own[...], own[at, :], NT) + dot(held_cross[...], cross[at, :], NT)
            held[:, at] = value.astype(LOW)
        for j in range(chips):
            for h in range(2):
                for i in range(half):
                    start = ((h * half + i) * chips + (chip_ref[0] ^ j)) * group
                    outs[2 * j + h][i] = held[pl.ds(pl.multiple_of(start, group), group), :]

    return pl.pallas_call(
        kernel,
        in_specs=[SCALARS] + [WHOLE] * (planes + 3),
        out_specs=[WHOLE] * (2 * chips),
        out_shape=[like((half, group, rows), LOW)] * (2 * chips),
        scratch_shapes=[
            pltpu.VMEM((n_images, units), LOW),
            pltpu.VMEM((n_images, units), LOW),
            pltpu.VMEM((n_images, rows), LOW),
        ],
        compiler_params=pltpu.CompilerParams(vmem_limit_bytes=20 << 20),
        cost_estimate=pl.CostEstimate(
            flops=4 * n_images * rows * units, bytes_accessed=4 * rows * units, transcendentals=0
        ),
    )(chip, *grads, crossed, *weights)


def conv_backward(own, other, pooled, pooled_other, slope, images, small, core, chip, plane):
    planes = len(own)
    cells, group, full = pooled.shape
    high, _, _, width_in = images.shape
    side = high - 2
    width = full // planes
    per = LANES // width
    columns = full // LANES
    shards = lax.axis_size("chan")
    shard = full // shards
    slots = LANES // shard
    area = side * side * group

    def covering(h):
        return [r for r in range(6) if 2 * r <= h <= 2 * r + 2]

    def kernel(core_ref, chip_ref, plane_ref, *refs):
        own_refs, other_ref = refs[:planes], refs[planes]
        a_ref, b_ref, slope_ref, x_ref, small_ref = refs[planes + 1 : planes + 6]
        outs = refs[planes + 6 : planes + 6 + shards]
        grad_ref = refs[planes + 6 + shards]
        flat, pool_grad, turned, taps, smalls = refs[planes + 7 + shards :]
        place = lane_place(width)
        for k in range(planes):
            flat[0, plane_ref[0] ^ k] = own_refs[k][...].astype(WIDE)
            flat[1, plane_ref[0] ^ k] = other_ref[k].astype(WIDE)
        one, back = small_ref[1:2, :] * (1.0 / 9.0), small_ref[3:4, :] * (1.0 / 9.0)
        sum_one = jnp.zeros((group, full), WIDE)
        sum_two = jnp.zeros((group, full), WIDE)
        for cell in range(cells):
            column, source = divmod(cell * width, LANES)
            both = []
            for t in range(2):
                blocks = []
                for v in range(columns):
                    out = None
                    for i in range(per):
                        piece = flat[t, v * per + i, :, column * LANES : (column + 1) * LANES]
                        moved = shift_slots(piece, width, source // width, i)
                        out = moved if out is None else jnp.where(place == i, moved, out)
                    blocks.append(out)
                both.append(jnp.concatenate(blocks, axis=1))
            sum_one += both[0] * a_ref[cell]
            sum_two += both[0] * b_ref[cell]
            pool_grad[cell] = one * both[0] + back * both[1]
        sum_bias = jnp.zeros((group, full), WIDE)
        for h in range(side):
            line = [sum(pool_grad[6 * r + c] for r in covering(h)) for c in range(6)]
            for w in range(side):
                value = sum(line[c] for c in covering(w))
                value = (value * slope_ref[h, w].astype(WIDE)).astype(LOW)
                grad_ref[h, w] = value
                sum_bias += value.astype(WIDE)
        turned[...] = grad_ref[...].reshape(area, full).T
        for tap in range(TAPS):
            window = x_ref[tap // 3 : tap // 3 + side, tap % 3 : tap % 3 + side]
            taps[tap] = dot(turned[...], window.reshape(area, width_in), NN).astype(LOW)
        sums = [jnp.sum(value, axis=0, keepdims=True) for value in (sum_bias, sum_one, sum_two)]
        sums = jnp.concatenate(sums + [jnp.zeros((EXTRA - 3, full), WIDE)], axis=0)
        for v in range(columns):
            smalls[v] = sums[:, v * LANES : (v + 1) * LANES]
        lane = lax.broadcasted_iota(jnp.int32, (EXTRA, LANES), 1)
        for j in range(shards // 2):
            for r in range(2):
                where = (chip_ref[0] ^ j) * 2 + (core_ref[0] ^ r)
                at = pl.ds(pl.multiple_of(where * shard, shard), shard)
                out = outs[2 * j + r]
                for tap in range(TAPS):
                    out[tap * shard : (tap + 1) * shard, :] = taps[tap, at, :]
                row = smalls[where // slots]
                value = jnp.zeros((EXTRA, LANES), WIDE)
                for s in range(slots):
                    moved = row if s == 0 else pltpu.roll(row, LANES - s * shard, 1)
                    value = jnp.where(where % slots == s, moved, value)
                out[TAPS * shard :, :] = jnp.zeros((EXTRA, width_in), LOW)
                out[TAPS * shard :, :LANES] = jnp.where(lane < shard, value, 0.0).astype(LOW)

    return pl.pallas_call(
        kernel,
        in_specs=[SCALARS] * 3 + [WHOLE] * (planes + 6),
        out_specs=[WHOLE] * (shards + 1),
        out_shape=[like((TAPS * shard + EXTRA, width_in), LOW)] * shards
        + [like((side, side, group, full), LOW)],
        scratch_shapes=[
            pltpu.VMEM((2, planes, group, cells * width), WIDE),
            pltpu.VMEM((cells, group, full), WIDE),
            pltpu.VMEM((full, area), LOW),
            pltpu.VMEM((TAPS, full, width_in), LOW),
            pltpu.VMEM((columns, EXTRA, LANES), WIDE),
        ],
        compiler_params=pltpu.CompilerParams(vmem_limit_bytes=28 << 20),
        cost_estimate=pl.CostEstimate(
            flops=2 * area * TAPS * width_in * full,
            bytes_accessed=2 * images.size + 6 * area * full,
            transcendentals=0,
        ),
    )(core, chip, plane, *own, other, pooled, pooled_other, slope, images, small)


def fc_update(weight, moment, rows, grads, core, which, previous):
    towers, depth, units = weight.shape
    width = depth // CELLS
    n_images = rows.shape[0]
    planes = len(grads)
    block = n_images // planes

    def kernel(core_ref, w_ref, m_ref, rows_ref, *refs):
        grad_refs = refs[:planes]
        new_w, new_m, product, joined = refs[-4:]
        for k in range(planes):
            joined[pl.ds(k * block, block), :] = grad_refs[k][0]
        product[...] = dot(rows_ref[...], joined[...], TN)
        for cell in range(CELLS):
            at = pl.ds(cell, width, stride=CELLS)
            fresh = MOMENTUM * m_ref[0, at, :] + product[pl.ds(cell * width, width), :]
            new_m[0, at, :] = fresh
            new_w[0, at, :] = w_ref[0, at, :] - LEARN_RATE * fresh

    big = pl.BlockSpec((1, depth, LANES), lambda j, core: (core[0] ^ which, 0, j))
    grad_spec = pl.BlockSpec((1, block, LANES), lambda j, core: (which, 0, j))
    extra = [] if previous is None else list(previous)
    return pl.pallas_call(
        kernel,
        grid_spec=pltpu.PrefetchScalarGridSpec(
            num_scalar_prefetch=1,
            grid=(units // LANES,),
            in_specs=[big, big, pl.BlockSpec((n_images, depth), lambda j, core: (0, 0))]
            + [grad_spec] * planes
            + [pl.BlockSpec(memory_space=pl.ANY)] * len(extra),
            out_specs=[big, big],
            scratch_shapes=[pltpu.VMEM((depth, LANES), WIDE), pltpu.VMEM((n_images, LANES), LOW)],
        ),
        out_shape=[like(weight.shape, WIDE)] * 2,
        input_output_aliases={} if previous is None else {4 + planes: 0, 5 + planes: 1},
        compiler_params=pltpu.CompilerParams(vmem_limit_bytes=20 << 20),
        cost_estimate=pl.CostEstimate(
            flops=2 * n_images * depth * units, bytes_accessed=16 * depth * units, transcendentals=0
        ),
    )(core, weight, moment, rows, *grads, *extra)


def reorder(parts, place):
    bit = 1
    while bit < len(parts):
        flip = (place & bit) != 0
        parts = [
            jax.tree.map(lambda a, b: jnp.where(flip, b, a), parts[j], parts[j ^ bit])
            for j in range(len(parts))
        ]
        bit *= 2
    return parts


def pick(stacked, place, count):
    return [lax.dynamic_index_in_dim(stacked, place ^ j, 0, keepdims=False) for j in range(count)]


def pool(values):
    rows = values[0:11:2] + values[1:12:2] + values[2:13:2]
    return (rows[:, 0:11:2] + rows[:, 1:12:2] + rows[:, 2:13:2]) * (1.0 / 9.0)


def spread(values, axis):
    values = jnp.moveaxis(values, axis, 0)
    zero = jnp.zeros_like(values[:1])
    even = jnp.concatenate([values, zero]) + jnp.concatenate([zero, values])
    inter = jnp.stack([even[:-1], values], axis=1).reshape((12,) + values.shape[1:])
    return jnp.moveaxis(jnp.concatenate([inter, even[-1:]]), 0, axis)


def any_mesh(
    images,
    conv_weight,
    conv_bias,
    stitch_conv,
    fc_weight,
    fc_bias,
    stitch_fc,
    conv_moment,
    bias_moment,
    stitch_conv_moment,
    fc_moment,
    fc_bias_moment,
    stitch_fc_moment,
    cotangent,
    task_mask,
):
    chan_size, planes = lax.axis_size("chan"), lax.axis_size("batch")
    chips = chan_size // 2
    me, plane = lax.axis_index("chan"), lax.axis_index("batch")
    core, chip = me % 2, me // 2
    swap = lambda value: trade(value, "chan", 1)
    mine = lambda a, b: jnp.where(core == 0, a, b)
    per_core, side, width_in = images.shape[0], images.shape[2], images.shape[-1]
    chan_width = conv_weight.shape[-1]
    full_chan = chan_width * chan_size
    units = fc_weight.shape[-1]
    rows = fc_weight.shape[1]
    cells = 36
    plane_chan = rows // cells
    group = 2 * per_core

    kernel_rows = jnp.transpose(conv_weight, (0, 1, 2, 4, 3)).astype(LOW)
    kernel_rows = kernel_rows.reshape(2, 9 * chan_width, width_in)
    cross = stitch_conv[:, ::-1]
    small = jnp.stack(
        [
            conv_bias,
            jnp.stack([stitch_conv[0, 0], stitch_conv[1, 1]]),
            jnp.stack([stitch_conv[0, 1], stitch_conv[1, 0]]),
            jnp.stack([stitch_conv[1, 0], stitch_conv[0, 1]]),
        ],
        axis=1,
    ).astype(LOW)
    small = jnp.pad(small, ((0, 0), (0, 12), (0, width_in - chan_width)))
    kernel_rows = jnp.concatenate([kernel_rows, small], axis=1)
    keep = mine(kernel_rows[0], kernel_rows[1])
    got = swap(mine(kernel_rows[1], kernel_rows[0]))
    halves = mine(keep, got), mine(got, keep)
    kernel_parts = gather_chips(halves[0], halves[1], chips)

    keep = mine(images[:, 0], images[:, 1])
    got = swap(mine(images[:, 1], images[:, 0]))
    tower_images = jnp.concatenate([mine(keep, got), mine(got, keep)], axis=0)
    tower_images = jnp.transpose(tower_images, (1, 2, 0, 3))

    fc_low = fc_weight.astype(LOW).reshape(2, plane_chan, cells, units)
    fc_low = jnp.swapaxes(fc_low, 1, 2).reshape(2, rows, units)
    fc_keep = mine(fc_low[0], fc_low[1])
    fc_got = swap(mine(fc_low[1], fc_low[0]))
    fc_halves = mine(fc_keep, fc_got), mine(fc_got, fc_keep)

    ordered = reorder(kernel_parts, chip)
    kernel = jnp.concatenate(
        [half[: 9 * chan_width].reshape(9, chan_width, width_in) for pair in ordered for half in pair],
        axis=1,
    )
    small_all = jnp.concatenate(
        [half[9 * chan_width :, :chan_width] for pair in ordered for half in pair], axis=1
    ).astype(WIDE)
    bias_all, self_mix, cross_mix, back_mix = (small_all[i] for i in range(4))

    conv_out = lax.conv_general_dilated(
        tower_images,
        kernel.reshape(3, 3, full_chan, width_in),
        (1, 1),
        "SAME",
        dimension_numbers=("HWNC", "HWOI", "HWNC"),
        preferred_element_type=WIDE,
    )
    act, slope = silu_and_slope(conv_out + bias_all)
    pooled = pool(act)
    pooled_other = swap(pooled)
    mixed = (self_mix * pooled + cross_mix * pooled_other).astype(LOW)
    mixed = mixed.reshape(cells, group, planes, plane_chan)
    pieces = jnp.transpose(mixed, (2, 1, 0, 3)).reshape(planes, group, rows)
    got = exchange_planes(pick(pieces, plane, planes))
    half = planes // 2
    gathered = reorder(
        gather_chips(jnp.stack(got[:half]), jnp.stack(got[half:]), chips), chip
    )
    tower_rows = jnp.concatenate(
        [jnp.stack([pair[h] for pair in gathered], axis=1) for h in range(2)], axis=0
    )
    tower_rows = tower_rows.reshape(planes * chips * group, rows)
    other_rows = swap(tower_rows)

    fc_tower = jnp.concatenate(fc_halves, axis=1)
    partial = jnp.dot(tower_rows, fc_tower, preferred_element_type=WIDE).astype(LOW)
    partial = partial.reshape(planes, chips * group, 2 * units)
    fc_sum = total(exchange_planes([partial[k] for k in range(planes)]))
    fc_keep = mine(fc_sum[:, :units], fc_sum[:, units:])
    fc_got = swap(mine(fc_sum[:, units:], fc_sum[:, :units]))
    fc_out = [mine(fc_keep, fc_got) + fc_bias[0], mine(fc_got, fc_keep) + fc_bias[1]]

    acts, slopes = zip(*[silu_and_slope(value) for value in fc_out])
    features_out = jnp.stack(
        [stitch_fc[t, 0] * acts[0] + stitch_fc[t, 1] * acts[1] for t in range(2)], axis=1
    ).astype(LOW)
    out_grad = [
        cotangent[:, t].astype(WIDE) * task_mask[:, t].astype(WIDE)[:, None] for t in range(2)
    ]
    stitch_fc_grad = jnp.stack(
        [jnp.stack([jnp.sum(out_grad[t] * acts[s], axis=0) for s in range(2)]) for t in range(2)]
    )
    grad_low = jnp.stack(
        [
            (slopes[s] * (stitch_fc[0, s] * out_grad[0] + stitch_fc[1, s] * out_grad[1])).astype(LOW)
            for s in range(2)
        ]
    )
    grad_all = exchange_planes([grad_low] * planes)
    grad_all = jnp.stack(grad_all, axis=1).reshape(2, planes * chips * group, units)
    grad_keep = mine(grad_all[0], grad_all[1])
    grad_got = swap(mine(grad_all[1], grad_all[0]))
    grad_tower = jnp.concatenate([mine(grad_keep, grad_got), mine(grad_got, grad_keep)], axis=1)

    flat_grad = lax.dot_general(
        grad_tower, fc_tower, (((1,), (1,)), ((), ())), preferred_element_type=WIDE
    ).astype(LOW)
    flat_grad = flat_grad.reshape(2, half, chips, group, rows)
    by_chip = reorder([(flat_grad[0, :, m], flat_grad[1, :, m]) for m in range(chips)], chip)
    first, second = scatter_chips(by_chip, chips)
    sums = jnp.concatenate([total(first), total(second)]).astype(LOW)
    got = reorder(exchange_planes([sums[k] for k in range(planes)]), plane)
    mixed_grad = jnp.stack(got)
    mixed_grad_other = swap(mixed_grad)

    def unflatten(value):
        value = value.astype(WIDE).reshape(planes, group, cells, plane_chan)
        return jnp.transpose(value, (2, 1, 0, 3)).reshape(6, 6, group, full_chan)

    own_grad, other_grad = unflatten(mixed_grad), unflatten(mixed_grad_other)
    self_stitch = jnp.sum(own_grad * pooled, axis=(0, 1, 2))
    cross_stitch = jnp.sum(own_grad * pooled_other, axis=(0, 1, 2))
    pooled_grad = (self_mix * own_grad + back_mix * other_grad) * (1.0 / 9.0)
    conv_grad = (slope * spread(spread(pooled_grad, 0), 1)).astype(LOW)
    bias_grad = jnp.sum(conv_grad.astype(WIDE), axis=(0, 1, 2))

    padded = jnp.pad(tower_images, ((1, 1), (1, 1), (0, 0), (0, 0)))
    taps = []
    for down in range(3):
        for right in range(3):
            window = padded[down : down + side, right : right + side]
            taps.append(
                lax.dot_general(
                    conv_grad.reshape(-1, full_chan),
                    window.reshape(-1, width_in),
                    (((0,), (0,)), ((), ())),
                    preferred_element_type=WIDE,
                ).astype(LOW)
            )
    kernel_grad = jnp.stack(taps).reshape(9, chips, 2, chan_width, width_in)
    smalls = jnp.stack([bias_grad, self_stitch, cross_stitch]).astype(LOW)
    smalls = jnp.pad(
        smalls.reshape(3, chips, 2, chan_width), ((0, 13), (0, 0), (0, 0), (0, width_in - chan_width))
    )
    blocks = [
        tuple(
            jnp.concatenate([kernel_grad[:, m, c].reshape(9 * chan_width, width_in), smalls[:, m, c]])
            for c in range(2)
        )
        for m in range(chips)
    ]
    first, second = scatter_chips(reorder(blocks, chip), chips)
    sums = [total(first).astype(LOW), total(second).astype(LOW)]
    keep = mine(sums[0], sums[1])
    got = swap(mine(sums[1], sums[0]))
    towers = jnp.stack([mine(keep, got), mine(got, keep)])
    towers = lax.psum(towers, "batch").astype(WIDE)
    stitch_fc_grad = lax.psum(stitch_fc_grad.astype(LOW), "batch").astype(WIDE)

    images_grad = lax.conv_general_dilated(
        conv_grad,
        kernel.reshape(3, 3, full_chan, width_in)[::-1, ::-1],
        (1, 1),
        "SAME",
        dimension_numbers=("HWNC", "HWIO", "HWNC"),
        preferred_element_type=WIDE,
    ).astype(LOW)
    images_grad = jnp.transpose(images_grad, (2, 0, 1, 3))
    keep = mine(images_grad[:per_core], images_grad[per_core:])
    got = swap(mine(images_grad[per_core:], images_grad[:per_core]))
    images_grad = jnp.stack([mine(keep, got), mine(got, keep)], axis=1)

    both_rows = [mine(tower_rows, other_rows), mine(other_rows, tower_rows)]
    fc_weight_grad = jnp.stack(
        [
            lax.dot_general(
                jnp.swapaxes(both_rows[t].reshape(-1, cells, plane_chan), 1, 2).reshape(-1, rows),
                grad_all[t],
                (((0,), (0,)), ((), ())),
                preferred_element_type=WIDE,
            )
            for t in range(2)
        ]
    )
    fc_bias_grad = jnp.sum(grad_all.astype(WIDE), axis=1)

    conv_weight_grad = jnp.swapaxes(
        towers[:, : 9 * chan_width].reshape(2, 3, 3, chan_width, width_in), 3, 4
    )
    conv_bias_grad = towers[:, 9 * chan_width, :chan_width]
    straight = towers[:, 9 * chan_width + 1, :chan_width]
    crossed = towers[:, 9 * chan_width + 2, :chan_width]
    stitch_conv_grad = jnp.stack(
        [jnp.stack([straight[0], crossed[0]]), jnp.stack([crossed[1], straight[1]])]
    )
    grads = (
        conv_weight_grad,
        conv_bias_grad,
        stitch_conv_grad,
        fc_weight_grad,
        fc_bias_grad,
        stitch_fc_grad,
    )
    params = (conv_weight, conv_bias, stitch_conv, fc_weight, fc_bias, stitch_fc)
    moments = (
        conv_moment,
        bias_moment,
        stitch_conv_moment,
        fc_moment,
        fc_bias_moment,
        stitch_fc_moment,
    )
    rates = (LEARN_RATE, BIAS_RATE, STITCH_RATE, LEARN_RATE, BIAS_RATE, STITCH_RATE)
    fresh = [MOMENTUM * moments[place] + grads[place] for place in range(6)]
    updated = [params[place] - rates[place] * fresh[place] for place in range(6)]
    return (features_out, images_grad, *updated, *fresh)


def four_by_four(
    images,
    conv_weight,
    conv_bias,
    stitch_conv,
    fc_weight,
    fc_bias,
    stitch_fc,
    conv_moment,
    bias_moment,
    stitch_conv_moment,
    fc_moment,
    fc_bias_moment,
    stitch_fc_moment,
    cotangent,
    task_mask,
):
    chips, planes = lax.axis_size("chan") // 2, lax.axis_size("batch")
    me, plane = lax.axis_index("chan"), lax.axis_index("batch")
    core, chip = me % 2, me // 2
    as_scalar = lambda value: value.reshape(1).astype(jnp.int32)
    core_at, chip_at, plane_at = as_scalar(core), as_scalar(chip), as_scalar(plane)
    swap = lambda value: trade(value, "chan", 1)
    mine = lambda a, b: jnp.where(core == 0, a, b)
    per_core, side, width_in = images.shape[0], images.shape[2], images.shape[-1]
    shard = conv_weight.shape[-1]
    units = fc_weight.shape[-1]
    half = planes // 2

    kernel_rows = jnp.transpose(conv_weight, (0, 1, 2, 4, 3)).astype(LOW)
    kernel_rows = kernel_rows.reshape(2, TAPS * shard, width_in)
    straight = jnp.stack([stitch_conv[0, 0], stitch_conv[1, 1]])
    crossed = jnp.stack([stitch_conv[0, 1], stitch_conv[1, 0]])
    small = jnp.stack([conv_bias, straight, crossed, crossed[::-1]], axis=1).astype(LOW)
    small = jnp.pad(small, ((0, 0), (0, EXTRA - 4), (0, width_in - shard)))
    kernel_rows = jnp.concatenate([kernel_rows, small], axis=1)
    keep = mine(kernel_rows[0], kernel_rows[1])
    got = swap(mine(kernel_rows[1], kernel_rows[0]))
    kernel_parts = [part for pair in gather_chips(keep, got, chips) for part in pair]

    keep = mine(images[:, 0], images[:, 1])
    got = swap(mine(images[:, 1], images[:, 0]))
    tower_images = jnp.concatenate([mine(keep, got), mine(got, keep)], axis=0)
    tower_images = jnp.transpose(tower_images, (1, 2, 0, 3))
    tower_images = jnp.pad(tower_images, ((1, 1), (1, 1), (0, 0), (0, 0)))

    fc_low = fc_prepare(fc_weight, core_at)
    fc_own, fc_cross = fc_low[0], swap(fc_low[1])

    pooled, slope, small_all = conv_forward(tower_images, kernel_parts, core_at, chip_at)
    pooled_other = swap(pooled)
    got = exchange_planes(mix_pieces(pooled, pooled_other, small_all, plane_at, planes))
    gathered = gather_chips(jnp.stack(got[:half]), jnp.stack(got[half:]), chips)
    tower_rows, *partial = fc_forward(
        [part for pair in gathered for part in pair], (fc_own, fc_cross), chip_at, chips, planes
    )
    other_rows = swap(tower_rows)

    fc_sum = total(exchange_planes(partial))
    fc_out = [fc_sum[:, :units], swap(fc_sum[:, units:])]
    fc_out = [fc_out[a] + mine(fc_bias[a], fc_bias[1 - a]) for a in range(2)]
    acts, slopes = zip(*[silu_and_slope(value) for value in fc_out])
    mix = [[mine(stitch_fc[a, b], stitch_fc[1 - a, 1 - b]) for b in range(2)] for a in range(2)]
    features = [mix[a][0] * acts[0] + mix[a][1] * acts[1] for a in range(2)]
    features_out = jnp.stack([mine(features[0], features[1]), mine(features[1], features[0])], axis=1)
    masked = [cotangent[:, t].astype(WIDE) * task_mask[:, t].astype(WIDE)[:, None] for t in range(2)]
    out_grad = [mine(masked[a], masked[1 - a]) for a in range(2)]
    grad_low = jnp.stack(
        [(slopes[b] * (mix[0][b] * out_grad[0] + mix[1][b] * out_grad[1])).astype(LOW) for b in range(2)]
    )
    stitch_fc_grad = jnp.stack(
        [jnp.stack([jnp.sum(out_grad[a] * acts[b], axis=0) for b in range(2)]) for a in range(2)]
    )
    grads = exchange_planes([grad_low] * planes)
    grads_cross = swap(jnp.stack([value[1] for value in grads]))

    blocks = fc_backward(grads, grads_cross, (fc_own, fc_cross), chip_at, chips, planes)
    first, second = scatter_chips([blocks[2 * j : 2 * j + 2] for j in range(chips)], chips)
    sums = [total([value[i] for value in part]).astype(LOW) for part in (first, second) for i in range(half)]
    mixed_grad = exchange_planes(sums)
    mixed_grad_other = swap(jnp.stack(mixed_grad))

    *blocks, conv_grad = conv_backward(
        mixed_grad, mixed_grad_other, pooled, pooled_other, slope, tower_images, small_all, core_at, chip_at, plane_at
    )
    first, second = scatter_chips([blocks[2 * j : 2 * j + 2] for j in range(chips)], chips)
    towers = jnp.stack([total(first).astype(LOW), swap(total(second).astype(LOW))])
    lines = towers.shape[1]

    packed = jnp.concatenate([stitch_fc_grad.reshape(-1), jnp.zeros((-4 * units) % width_in)])
    packed = packed.astype(LOW).reshape(-1, width_in)
    tail = (-(2 * lines + packed.shape[0])) % (planes * 16)
    flat = jnp.concatenate([towers.reshape(-1, width_in), jnp.pad(packed, ((0, tail), (0, 0)))])
    flat = flat.reshape(planes, -1, width_in)
    quarters = [lax.dynamic_index_in_dim(flat, plane ^ k, 0, keepdims=False) for k in range(planes)]
    quarter = total(exchange_planes(quarters)).astype(LOW)
    whole = exchange_planes([quarter] * planes)
    whole = jnp.concatenate(reorder(whole, plane)).astype(WIDE)
    towers = whole[: 2 * lines].reshape(2, lines, width_in)
    stitch_fc_grad = whole[2 * lines :].reshape(-1)[: 4 * units].reshape(2, 2, units)
    stitch_fc_grad = mine(stitch_fc_grad, stitch_fc_grad[::-1, ::-1])
    towers = mine(towers, towers[::-1])

    full_chan = conv_grad.shape[-1]
    ordered = reorder([(kernel_parts[2 * j], kernel_parts[2 * j + 1]) for j in range(chips)], chip)
    ordered = [part for a, b in ordered for part in (mine(a, b), mine(b, a))]
    kernel = jnp.concatenate(
        [part[: TAPS * shard].reshape(3, 3, shard, width_in) for part in ordered], axis=2
    )
    images_grad = lax.conv_general_dilated(
        conv_grad,
        kernel[::-1, ::-1],
        (1, 1),
        "SAME",
        dimension_numbers=("HWNC", "HWIO", "HWNC"),
        preferred_element_type=WIDE,
    ).astype(LOW)
    images_grad = jnp.transpose(images_grad, (2, 0, 1, 3))
    keep = mine(images_grad[:per_core], images_grad[per_core:])
    got = swap(mine(images_grad[per_core:], images_grad[:per_core]))
    images_grad = jnp.stack([mine(keep, got), mine(got, keep)], axis=1)

    step = fc_update(fc_weight, fc_moment, tower_rows, grads, core_at, 0, None)
    new_fc_weight, new_fc_moment = fc_update(fc_weight, fc_moment, other_rows, grads, core_at, 1, step)
    fc_bias_grad = sum(jnp.sum(value.astype(WIDE), axis=1) for value in grads)
    fc_bias_grad = mine(fc_bias_grad, fc_bias_grad[::-1])

    conv_weight_grad = towers[:, : TAPS * shard].reshape(2, 3, 3, shard, width_in)
    conv_weight_grad = jnp.swapaxes(conv_weight_grad, 3, 4)
    conv_bias_grad = towers[:, TAPS * shard, :shard]
    straight = towers[:, TAPS * shard + 1, :shard]
    crossed = towers[:, TAPS * shard + 2, :shard]
    stitch_conv_grad = jnp.stack(
        [jnp.stack([straight[0], crossed[0]]), jnp.stack([crossed[1], straight[1]])]
    )

    def step_of(param, moment, grad, rate):
        fresh = MOMENTUM * moment + grad
        return param - rate * fresh, fresh

    kernel_step = step_of(conv_weight, conv_moment, conv_weight_grad, LEARN_RATE)
    bias_step = step_of(conv_bias, bias_moment, conv_bias_grad, BIAS_RATE)
    stitch_step = step_of(stitch_conv, stitch_conv_moment, stitch_conv_grad, STITCH_RATE)
    fc_bias_step = step_of(fc_bias, fc_bias_moment, fc_bias_grad, BIAS_RATE)
    fc_stitch_step = step_of(stitch_fc, stitch_fc_moment, stitch_fc_grad, STITCH_RATE)
    params, fresh = zip(
        kernel_step, bias_step, stitch_step, (new_fc_weight, new_fc_moment), fc_bias_step, fc_stitch_step
    )
    return (features_out.astype(LOW), images_grad, *params, *fresh)


def solution(mesh):
    chan_last = P(None, None, None, None, "chan")
    fc_spec = P(None, "batch", "chan")
    params = (chan_last, P(None, "chan"), P(None, None, "chan"), fc_spec, P(None, "chan"), P(None, None, "chan"))
    image_spec = P(("batch", "chan"), None, None, None, None)
    feature_spec = P("batch", None, "chan")
    in_specs = (image_spec, *params, *params, feature_spec, P("batch", None))
    out_specs = (feature_spec, image_spec, *params, *params)
    body = four_by_four if dict(mesh.shape) == {"chan": 8, "batch": 4} else any_mesh
    return jax.shard_map(body, mesh=mesh, in_specs=in_specs, out_specs=out_specs, check_vma=False)
```

```python
import functools

import jax
import jax.numpy as jnp
from jax import lax
from jax.experimental import pallas as pl
from jax.experimental.pallas import tpu as pltpu
from jax.sharding import PartitionSpec as P

MOMENTUM = 0.9
LEARN_RATE = 0.002
BIAS_RATE = 0.02
STITCH_RATE = 0.02
LOW = jnp.bfloat16
WIDE = jnp.float32
TAPS = 9
CELLS = 36
EXTRA = 16
LANES = 128
WHOLE = pl.BlockSpec(memory_space=pltpu.VMEM)
SCALARS = pl.BlockSpec(memory_space=pltpu.SMEM)
NN = (((1,), (0,)), ((), ()))
NT = (((1,), (1,)), ((), ()))
TN = (((0,), (0,)), ((), ()))


def like(shape, dtype):
    return jax.ShapeDtypeStruct(shape, dtype)


def dot(a, b, dims):
    return lax.dot_general(a, b, dims, preferred_element_type=WIDE)


def trade(value, axis, bit):
    size = lax.axis_size(axis)
    return lax.ppermute(value, axis, [(i, i ^ bit) for i in range(size)])


def tie(*values):
    return lax.optimization_barrier(values)


def gather_chips(first, second, chips):
    if chips == 4:
        first_y = trade(first, "chan", 4)
        second_x = trade(second, "chan", 2)
        first_x = trade(first, "chan", 2)
        second_y = trade(second, "chan", 4)
        first_d = trade(first_y, "chan", 2)
        second_d = trade(second_x, "chan", 4)
        return [(first, second), (first_x, second_x), (first_y, second_y), (first_d, second_d)]
    return [(first, second)] + [
        (trade(first, "chan", 2 * j), trade(second, "chan", 2 * j)) for j in range(1, chips)
    ]


def add_low(a, b):
    return (a.astype(WIDE) + b.astype(WIDE)).astype(LOW)


def scatter_chips(parts, chips, later=lambda gate, value: (gate, value)):
    if chips == 4:
        from_x = trade(parts[3][0], "chan", 2)
        from_y = trade(parts[3][1], "chan", 4)
        first_x = trade(parts[1][0], "chan", 2)
        second_y = trade(parts[2][1], "chan", 4)
        to_y = add_low(parts[2][0], from_x)
        first_y = trade(to_y, "chan", 4)
        to_x = add_low(parts[1][1], from_y)
        to_x, first_y = later(to_x, first_y)
        second_x = trade(to_x, "chan", 2)
        return (parts[0][0], first_x, first_y), (parts[0][1], second_x, second_y)
    got = [(trade(parts[j][0], "chan", 2 * j), trade(parts[j][1], "chan", 2 * j)) for j in range(1, chips)]
    return (
        (parts[0][0],) + tuple(pair[0] for pair in got),
        (parts[0][1],) + tuple(pair[1] for pair in got),
    )


def total(values):
    out = values[0].astype(WIDE)
    for value in values[1:]:
        out = out + value.astype(WIDE)
    return out


def exchange_planes(parts):
    got = {k: trade(parts[k], "batch", k) for k in range(len(parts) - 1, 0, -1)}
    return [parts[0]] + [got[k] for k in range(1, len(parts))]


def gate_of(value):
    return 1.0 / (1.0 + jnp.exp(-value))


def silu_and_slope(value):
    gate = gate_of(value)
    act = value * gate
    return act, gate + act * (1.0 - gate)


def lane_place(width):
    return lax.broadcasted_iota(jnp.int32, (1, LANES), 1) // width


def shift_slots(value, width, source, target):
    if source == target:
        return value
    return pltpu.roll(value, ((target - source) * width) % LANES, 1)


def pack_kernels(conv_weight, conv_bias, stitch_conv, core):
    _, lines, width_in = conv_weight.shape
    shard = conv_bias.shape[-1]

    def kernel(core_ref, w_ref, bias_ref, mix_ref, keep_ref, give_ref):
        first = core_ref[0] == 0
        for a, out in enumerate((keep_ref, give_ref)):
            out[:lines, :] = w_ref[core_ref[0] ^ a].astype(LOW)
            choose = lambda p, q: jnp.where(first, *((q, p) if a else (p, q)))
            rows = [
                choose(bias_ref[0:1, :], bias_ref[1:2, :]),
                choose(mix_ref[0, 0:1, :], mix_ref[1, 1:2, :]),
                choose(mix_ref[0, 1:2, :], mix_ref[1, 0:1, :]),
                choose(mix_ref[1, 0:1, :], mix_ref[0, 1:2, :]),
                jnp.zeros((EXTRA - 4, shard), WIDE),
            ]
            out[lines:, :] = jnp.zeros((EXTRA, width_in), LOW)
            out[lines:, :shard] = jnp.concatenate(rows, axis=0).astype(LOW)

    return pl.pallas_call(
        kernel,
        in_specs=[SCALARS] + [WHOLE] * 3,
        out_specs=[WHOLE] * 2,
        out_shape=[like((lines + EXTRA, width_in), LOW)] * 2,
        compiler_params=pltpu.CompilerParams(vmem_limit_bytes=8 << 20),
        cost_estimate=pl.CostEstimate(flops=0, bytes_accessed=8 * lines * width_in, transcendentals=0),
    )(core, conv_weight, conv_bias, stitch_conv)


def fc_prepare(fc_weight, core, gate):
    _, rows, units = fc_weight.shape
    width = rows // CELLS
    fc_weight = pltpu.with_memory_space_constraint(fc_weight, pltpu.HBM)

    def kernel(core_ref, own_ref, other_ref, _, keep_ref, give_ref):
        for source, out in ((own_ref, keep_ref), (other_ref, give_ref)):
            for cell in range(CELLS):
                out[pl.ds(cell * width, width), :] = source[
                    0, pl.ds(cell, width, stride=CELLS), :
                ].astype(LOW)

    return pl.pallas_call(
        kernel,
        grid_spec=pltpu.PrefetchScalarGridSpec(
            num_scalar_prefetch=1,
            grid=(units // LANES,),
            in_specs=[
                pl.BlockSpec((1, rows, LANES), lambda j, core: (core[0], 0, j)),
                pl.BlockSpec((1, rows, LANES), lambda j, core: (core[0] ^ 1, 0, j)),
                pl.BlockSpec(memory_space=pl.ANY),
            ],
            out_specs=[pl.BlockSpec((rows, LANES), lambda j, core: (0, j))] * 2,
        ),
        out_shape=[like((rows, units), LOW)] * 2,
        compiler_params=pltpu.CompilerParams(vmem_limit_bytes=12 << 20),
        cost_estimate=pl.CostEstimate(flops=0, bytes_accessed=6 * fc_weight.size, transcendentals=0),
    )(core, fc_weight, fc_weight, gate)


def conv_forward(images, parts, core, chip):
    high, wide, group, width_in = images.shape
    side = high - 2
    count = len(parts)
    shard = (parts[0].shape[0] - EXTRA) // TAPS
    full = shard * count
    slots = LANES // shard

    def kernel(core_ref, chip_ref, x_ref, *refs):
        pieces = refs[:count]
        pooled_ref, slope_out, small_ref = refs[count : count + 3]
        weights, acc, slope_ref, sems = refs[count + 3 :]
        copies = [pltpu.make_async_copy(slope_ref.at[h], slope_out.at[h], sems.at[h]) for h in range(side)]
        lane = lax.broadcasted_iota(jnp.int32, (EXTRA, LANES), 1) // shard
        smalls = [jnp.zeros((EXTRA, LANES), WIDE) for _ in range(full // LANES)]
        for j in range(count // 2):
            for r in range(2):
                piece = pieces[2 * j + r]
                where = (chip_ref[0] ^ j) * 2 + (core_ref[0] ^ r)
                at = pl.ds(pl.multiple_of(where * shard, shard), shard)
                for tap in range(TAPS):
                    weights[at, tap * width_in : (tap + 1) * width_in] = piece[tap * shard : (tap + 1) * shard, :]
                row = piece[TAPS * shard :, :LANES].astype(WIDE)
                spread = row
                for s in range(1, slots):
                    spread = spread + pltpu.roll(row, s * shard, 1)
                for v in range(len(smalls)):
                    smalls[v] = jnp.where(lane + v * slots == where, spread, smalls[v])
        for v, value in enumerate(smalls):
            small_ref[:, v * LANES : (v + 1) * LANES] = value
        line = side * group
        bias = small_ref[0:1, :]
        for low, high_row in ((0, (side + 1) // 2), ((side + 1) // 2, side)):
            tall = high_row - low
            windows = [
                x_ref[tap // 3 + low : tap // 3 + high_row, tap % 3 : tap % 3 + side].reshape(tall * line, width_in)
                for tap in range(TAPS)
            ]
            acc[low * line : high_row * line, :] = dot(jnp.concatenate(windows, axis=1), weights[...], NT)
        for h in range(side):
            value, slope = silu_and_slope(acc[h * line : (h + 1) * line, :] + bias)
            slope_ref[h] = slope.reshape(side, group, full).astype(LOW)
            acc[h * line : (h + 1) * line, :] = value
            copies[h].start()
        cell = lambda h, w: acc[(h * side + w) * group : (h * side + w + 1) * group, :]
        for r in range(6):
            rows = [cell(2 * r, w) + cell(2 * r + 1, w) + cell(2 * r + 2, w) for w in range(side)]
            for c in range(6):
                pooled_ref[6 * r + c] = (rows[2 * c] + rows[2 * c + 1] + rows[2 * c + 2]) * (1.0 / 9.0)
        for copy in copies:
            copy.wait()

    area = side * side * group
    return pl.pallas_call(
        kernel,
        in_specs=[SCALARS] * 2 + [WHOLE] * (1 + count),
        out_specs=[WHOLE, pl.BlockSpec(memory_space=pltpu.HBM), WHOLE],
        out_shape=[
            like((CELLS, group, full), WIDE),
            like((side, side, group, full), LOW),
            like((EXTRA, full), WIDE),
        ],
        scratch_shapes=[
            pltpu.VMEM((full, TAPS * width_in), LOW),
            pltpu.VMEM((area, full), WIDE),
            pltpu.VMEM((side, side, group, full), LOW),
            pltpu.SemaphoreType.DMA((side,)),
        ],
        compiler_params=pltpu.CompilerParams(vmem_limit_bytes=16 << 20),
        cost_estimate=pl.CostEstimate(
            flops=2 * area * TAPS * width_in * full,
            bytes_accessed=2 * images.size + 2 * area * full,
            transcendentals=0,
        ),
    )(core, chip, images, *parts)


def turn(value):
    half = value.shape[0] // 2
    return jnp.concatenate([value[half:], value[:half]], axis=0)


def mix_pieces(pooled, other, small, core, plane, planes):
    cells, group, full = pooled.shape
    width = full // planes
    per = LANES // width

    def kernel(core_ref, plane_ref, a_ref, b_ref, small_ref, *refs):
        outs, held = refs[:planes], refs[planes]
        first = core_ref[0] == 0
        place = lane_place(width)
        one, two = small_ref[1:2, :], small_ref[2:3, :]
        for start in range(0, cells, per):
            mixed = [
                one * a_ref[start + i] + two * turn(b_ref[start + i]) for i in range(per)
            ]
            mixed = [jnp.where(first, value, turn(value)) for value in mixed]
            for p in range(planes):
                column, source = divmod(p * width, LANES)
                out = None
                for i in range(per):
                    moved = shift_slots(
                        mixed[i][:, column * LANES : (column + 1) * LANES], width, source // width, i
                    )
                    out = moved if out is None else jnp.where(place == i, moved, out)
                held[p, :, start * width : (start + per) * width] = out.astype(LOW)
        for k in range(planes):
            outs[k][...] = held[plane_ref[0] ^ k]

    rows = cells * width
    return pl.pallas_call(
        kernel,
        in_specs=[SCALARS] * 2 + [WHOLE] * 3,
        out_specs=[WHOLE] * planes,
        out_shape=[like((group, rows), LOW)] * planes,
        scratch_shapes=[pltpu.VMEM((planes, group, rows), LOW)],
        compiler_params=pltpu.CompilerParams(vmem_limit_bytes=8 << 20),
        cost_estimate=pl.CostEstimate(flops=4 * pooled.size, bytes_accessed=8 * pooled.size, transcendentals=0),
    )(core, plane, pooled, other, small)


def fc_forward(gathered, weights, chip, chips, planes):
    half, group, rows = gathered[0].shape
    units = weights[0].shape[-1]
    count = 2 * chips
    block = chips * group

    def kernel(chip_ref, *refs):
        pieces, (own, cross) = refs[:count], refs[count : count + 2]
        rows_ref, outs = refs[count + 2], refs[count + 3 :]
        for j in range(chips):
            for h in range(2):
                for i in range(half):
                    start = ((h * half + i) * chips + (chip_ref[0] ^ j)) * group
                    rows_ref[pl.ds(pl.multiple_of(start, group), group), :] = pieces[2 * j + h][i]
        for n, weight in enumerate((own, cross)):
            part = dot(rows_ref[...], weight[...], NN)
            for k in range(planes):
                outs[k][:, n * units : (n + 1) * units] = part[k * block : (k + 1) * block].astype(
                    outs[k].dtype
                )

    n_images = planes * block
    return pl.pallas_call(
        kernel,
        in_specs=[SCALARS] + [WHOLE] * (count + 2),
        out_specs=[WHOLE] * (1 + planes),
        out_shape=[like((n_images, rows), LOW)]
        + [like((block, 2 * units), LOW if k else WIDE) for k in range(planes)],
        compiler_params=pltpu.CompilerParams(vmem_limit_bytes=16 << 20),
        cost_estimate=pl.CostEstimate(
            flops=4 * n_images * rows * units, bytes_accessed=4 * rows * units, transcendentals=0
        ),
    )(chip, *gathered, *weights)


def fc_backward(grads, crossed, weights, chip, chips, planes):
    _, block, units = grads[0].shape
    rows = weights[0].shape[0]
    group = block // chips
    half = planes // 2
    n_images = planes * block

    def kernel(chip_ref, *refs):
        pieces, got = refs[:planes], refs[planes]
        own, cross = refs[planes + 1 : planes + 3]
        outs = refs[planes + 3 : planes + 3 + 2 * chips]
        held_own, held_cross, held = refs[planes + 3 + 2 * chips :]
        for k in range(planes):
            held_own[pl.ds(k * block, block), :] = pieces[k][0]
            held_cross[pl.ds(k * block, block), :] = got[k]
        step = rows // 3
        for s in range(3):
            at = pl.ds(s * step, step)
            value = dot(held_own[...], own[at, :], NT) + dot(held_cross[...], cross[at, :], NT)
            held[:, at] = value.astype(LOW)
        for j in range(chips):
            for h in range(2):
                for i in range(half):
                    start = ((h * half + i) * chips + (chip_ref[0] ^ j)) * group
                    outs[2 * j + h][i] = held[pl.ds(pl.multiple_of(start, group), group), :]

    return pl.pallas_call(
        kernel,
        in_specs=[SCALARS] + [WHOLE] * (planes + 3),
        out_specs=[WHOLE] * (2 * chips),
        out_shape=[like((half, group, rows), LOW)] * (2 * chips),
        scratch_shapes=[
            pltpu.VMEM((n_images, units), LOW),
            pltpu.VMEM((n_images, units), LOW),
            pltpu.VMEM((n_images, rows), LOW),
        ],
        compiler_params=pltpu.CompilerParams(vmem_limit_bytes=20 << 20),
        cost_estimate=pl.CostEstimate(
            flops=4 * n_images * rows * units, bytes_accessed=4 * rows * units, transcendentals=0
        ),
    )(chip, *grads, crossed, *weights)


def conv_backward(gate, own, other, pooled, pooled_other, slope, images, small, core, chip, plane):
    planes = len(own)
    cells, group, full = pooled.shape
    high, _, _, width_in = images.shape
    side = high - 2
    width = full // planes
    per = LANES // width
    columns = full // LANES
    shards = lax.axis_size("chan")
    shard = full // shards
    slots = LANES // shard
    area = side * side * group

    def covering(h):
        return [r for r in range(6) if 2 * r <= h <= 2 * r + 2]

    def kernel(core_ref, chip_ref, plane_ref, gate_ref, *refs):
        own_refs, other_ref = refs[:planes], refs[planes]
        a_ref, b_ref, slope_ref, x_ref, small_ref = refs[planes + 1 : planes + 6]
        outs = refs[planes + 6 : planes + 6 + shards]
        grad_ref = refs[planes + 6 + shards]
        flat, pool_grad, turned, taps, smalls = refs[planes + 7 + shards :]
        place = lane_place(width)
        first = core_ref[0] == 0
        for k in range(planes):
            for t, value in enumerate((own_refs[k][...], other_ref[k])):
                value = value.astype(WIDE)
                flat[t, plane_ref[0] ^ k] = jnp.where(first, value, turn(value))
        one, back = small_ref[1:2, :] * (1.0 / 9.0), small_ref[3:4, :] * (1.0 / 9.0)
        sum_one = jnp.zeros((group, full), WIDE)
        sum_two = jnp.zeros((group, full), WIDE)
        for cell in range(cells):
            column, source = divmod(cell * width, LANES)
            both = []
            for t in range(2):
                blocks = []
                for v in range(columns):
                    out = None
                    for i in range(per):
                        piece = flat[t, v * per + i, :, column * LANES : (column + 1) * LANES]
                        moved = shift_slots(piece, width, source // width, i)
                        out = moved if out is None else jnp.where(place == i, moved, out)
                    blocks.append(out)
                both.append(jnp.concatenate(blocks, axis=1))
            sum_one += both[0] * a_ref[cell]
            sum_two += both[0] * turn(b_ref[cell])
            pool_grad[cell] = one * both[0] + back * both[1]
        sum_bias = jnp.zeros((group, full), WIDE)
        for h in range(side):
            line = [sum(pool_grad[6 * r + c] for r in covering(h)) for c in range(6)]
            for w in range(side):
                value = sum(line[c] for c in covering(w))
                value = (value * slope_ref[h, w].astype(WIDE)).astype(LOW)
                grad_ref[h, w] = value
                sum_bias += value.astype(WIDE)
        turned[...] = grad_ref[...].reshape(area, full).T
        for start in range(0, TAPS, 2):
            some = range(start, min(start + 2, TAPS))
            windows = [
                x_ref[tap // 3 : tap // 3 + side, tap % 3 : tap % 3 + side].reshape(area, width_in) for tap in some
            ]
            part = dot(turned[...], jnp.concatenate(windows, axis=1), NN)
            for n, tap in enumerate(some):
                taps[tap] = part[:, n * width_in : (n + 1) * width_in].astype(LOW)
        sums = [jnp.sum(value, axis=0, keepdims=True) for value in (sum_bias, sum_one, sum_two)]
        sums = jnp.concatenate(sums + [jnp.zeros((EXTRA - 3, full), WIDE)], axis=0)
        for v in range(columns):
            smalls[v] = sums[:, v * LANES : (v + 1) * LANES]
        lane = lax.broadcasted_iota(jnp.int32, (EXTRA, LANES), 1)
        for j in range(shards // 2):
            for r in range(2):
                where = (chip_ref[0] ^ j) * 2 + (core_ref[0] ^ r)
                at = pl.ds(pl.multiple_of(where * shard, shard), shard)
                out = outs[2 * j + r]
                for tap in range(TAPS):
                    out[tap * shard : (tap + 1) * shard, :] = taps[tap, at, :]
                row = smalls[where // slots]
                value = jnp.zeros((EXTRA, LANES), WIDE)
                for s in range(slots):
                    moved = row if s == 0 else pltpu.roll(row, LANES - s * shard, 1)
                    value = jnp.where(where % slots == s, moved, value)
                out[TAPS * shard :, :] = jnp.zeros((EXTRA, width_in), LOW)
                out[TAPS * shard :, :LANES] = jnp.where(lane < shard, value, 0.0).astype(LOW)

    return pl.pallas_call(
        kernel,
        in_specs=[SCALARS] * 3 + [pl.BlockSpec(memory_space=pl.ANY)] + [WHOLE] * (planes + 6),
        out_specs=[WHOLE] * (shards + 1),
        out_shape=[like((TAPS * shard + EXTRA, width_in), LOW)] * shards
        + [like((side, side, group, full), LOW)],
        scratch_shapes=[
            pltpu.VMEM((2, planes, group, cells * width), WIDE),
            pltpu.VMEM((cells, group, full), WIDE),
            pltpu.VMEM((full, area), LOW),
            pltpu.VMEM((TAPS, full, width_in), LOW),
            pltpu.VMEM((columns, EXTRA, LANES), WIDE),
        ],
        compiler_params=pltpu.CompilerParams(vmem_limit_bytes=14 << 20),
        cost_estimate=pl.CostEstimate(
            flops=2 * area * TAPS * width_in * full,
            bytes_accessed=2 * images.size + 6 * area * full,
            transcendentals=0,
        ),
    )(core, chip, plane, gate, *own, other, pooled, pooled_other, slope, images, small)


def fc_update(weight, moment, rows, grads, core, which, part, previous, gate):
    _, depth, units = weight.shape
    width = depth // CELLS
    n_images = rows.shape[0]
    planes = len(grads)
    block = n_images // planes
    columns = units // LANES
    steps = 4
    few = width // 2
    tall = depth // 2 // steps
    weight, moment = (pltpu.with_memory_space_constraint(value, pltpu.HBM) for value in (weight, moment))

    def kernel(core_ref, w_ref, m_ref, rows_ref, *refs):
        grad_refs = refs[:planes]
        new_w, new_m, token, joined, product = refs[-5:]
        step = pl.program_id(0)

        @pl.when(step == 0)
        def _():
            token[...] = jnp.zeros_like(token)
            for k in range(planes):
                joined[pl.ds(k * block, block), :] = grad_refs[k][which]
            for v in range(columns):
                grad = dot(rows_ref[...], joined[:, v * LANES : (v + 1) * LANES], TN)
                for cell in range(CELLS):
                    start = cell * width + part * few
                    product[v, pl.ds(cell, few, stride=CELLS), :] = grad[start : start + few]

        at = pl.ds(pl.multiple_of(step * tall, tall), tall)
        for v in range(columns):
            lanes = slice(v * LANES, (v + 1) * LANES)
            fresh = MOMENTUM * m_ref[0, :, lanes] + product[v, at, :]
            new_m[0, :, lanes] = fresh
            new_w[0, :, lanes] = w_ref[0, :, lanes] - LEARN_RATE * fresh

    big = pl.BlockSpec((1, tall, units), lambda s, core: (core[0] ^ which, part * steps + s, 0))
    fixed = lambda shape: pl.BlockSpec(shape, lambda s, core: (0,) * len(shape))
    anywhere = pl.BlockSpec(memory_space=pl.ANY)
    extra = [] if previous is None else list(previous)
    return pl.pallas_call(
        kernel,
        grid_spec=pltpu.PrefetchScalarGridSpec(
            num_scalar_prefetch=1,
            grid=(steps,),
            in_specs=[big, big, fixed(rows.shape)]
            + [fixed(value.shape) for value in grads]
            + [anywhere] * (len(extra) + 1),
            out_specs=[big, big, fixed((8, LANES))],
            scratch_shapes=[
                pltpu.VMEM((n_images, units), LOW),
                pltpu.VMEM((columns, depth // 2, LANES), WIDE),
            ],
        ),
        out_shape=[like(weight.shape, WIDE)] * 2 + [like((8, LANES), WIDE)],
        input_output_aliases={} if previous is None else {4 + planes: 0, 5 + planes: 1},
        compiler_params=pltpu.CompilerParams(vmem_limit_bytes=14 << 20),
        cost_estimate=pl.CostEstimate(
            flops=2 * n_images * depth * units, bytes_accessed=8 * depth * units, transcendentals=0
        ),
    )(core, weight, moment, rows, *grads, *extra, gate)


def order_towers(own, other, core):
    def kernel(core_ref, own_ref, other_ref, out_ref):
        out_ref[core_ref[0]] = own_ref[...]
        out_ref[1 - core_ref[0]] = other_ref[...]

    return pl.pallas_call(
        kernel,
        in_specs=[SCALARS, WHOLE, WHOLE],
        out_specs=WHOLE,
        out_shape=like((2, *own.shape), own.dtype),
        compiler_params=pltpu.CompilerParams(vmem_limit_bytes=8 << 20),
        cost_estimate=pl.CostEstimate(flops=0, bytes_accessed=8 * own.size, transcendentals=0),
    )(core, own, other)


def small_update(gates, pieces, lines, params, moments, core, plane):
    planes = len(pieces)
    height, width_in = pieces[0].shape
    shard = params[1].shape[-1]
    units = params[3].shape[-1]
    count = lines - EXTRA
    rates = (LEARN_RATE, BIAS_RATE, STITCH_RATE, STITCH_RATE)

    def kernel(core_ref, plane_ref, done_ref, ready_ref, *refs):
        piece_refs = refs[:planes]
        p_refs, m_refs = refs[planes : planes + 4], refs[planes + 4 : planes + 8]
        new_p, new_m = refs[planes + 8 : planes + 12], refs[planes + 12 : planes + 16]
        whole = refs[planes + 16]
        for k in range(planes):
            at = pl.ds(pl.multiple_of((plane_ref[0] ^ k) * height, height), height)
            whole[at, :] = piece_refs[k][...].astype(WIDE)

        def advance(which, at, grad):
            fresh = MOMENTUM * m_refs[which][at] + grad
            new_m[which][at] = fresh
            new_p[which][at] = p_refs[which][at] - rates[which] * fresh

        first = core_ref[0] == 0
        for a in range(2):
            advance(0, core_ref[0] ^ a, whole[a * lines : a * lines + count, :])
        rows = [[whole[a * lines + count + i : a * lines + count + i + 1, :shard] for i in range(3)] for a in range(2)]
        rows = [[jnp.where(first, rows[a][i], rows[1 - a][i]) for i in range(3)] for a in range(2)]
        for t in range(2):
            advance(1, (slice(t, t + 1), slice(None)), rows[t][0])
            advance(2, (t, slice(t, t + 1), slice(None)), rows[t][1])
            advance(2, (t, slice(1 - t, 2 - t), slice(None)), rows[t][2])
        base = 2 * lines
        parts, start = [], 0
        while start < units:
            step = min(width_in, units - start)
            parts.append(whole[base : base + 4, :step])
            base, start = base + 4, start + step
        packed = jnp.concatenate(parts, axis=1) if len(parts) > 1 else parts[0]
        for i in range(4):
            row = jnp.where(first, packed[i : i + 1, :], packed[3 - i : 4 - i, :])
            advance(3, (i // 2, slice(i % 2, i % 2 + 1), slice(None)), row)

    out_shape = [like(value.shape, WIDE) for value in (*params, *moments)]
    return pl.pallas_call(
        kernel,
        in_specs=[SCALARS] * 2 + [pl.BlockSpec(memory_space=pl.ANY)] * 2 + [WHOLE] * (planes + 8),
        out_specs=[WHOLE] * 8,
        out_shape=out_shape,
        scratch_shapes=[pltpu.VMEM((planes * height, width_in), WIDE)],
        compiler_params=pltpu.CompilerParams(vmem_limit_bytes=12 << 20),
        cost_estimate=pl.CostEstimate(flops=0, bytes_accessed=24 * 2 * lines * width_in, transcendentals=0),
    )(core, plane, *gates, *pieces, *params, *moments)


def reorder(parts, place):
    bit = 1
    while bit < len(parts):
        flip = (place & bit) != 0
        parts = [
            jax.tree.map(lambda a, b: jnp.where(flip, b, a), parts[j], parts[j ^ bit])
            for j in range(len(parts))
        ]
        bit *= 2
    return parts


def pick(stacked, place, count):
    return [lax.dynamic_index_in_dim(stacked, place ^ j, 0, keepdims=False) for j in range(count)]


def pool(values):
    rows = values[0:11:2] + values[1:12:2] + values[2:13:2]
    return (rows[:, 0:11:2] + rows[:, 1:12:2] + rows[:, 2:13:2]) * (1.0 / 9.0)


def spread(values, axis):
    values = jnp.moveaxis(values, axis, 0)
    zero = jnp.zeros_like(values[:1])
    even = jnp.concatenate([values, zero]) + jnp.concatenate([zero, values])
    inter = jnp.stack([even[:-1], values], axis=1).reshape((12,) + values.shape[1:])
    return jnp.moveaxis(jnp.concatenate([inter, even[-1:]]), 0, axis)


def any_mesh(
    images,
    conv_weight,
    conv_bias,
    stitch_conv,
    fc_weight,
    fc_bias,
    stitch_fc,
    conv_moment,
    bias_moment,
    stitch_conv_moment,
    fc_moment,
    fc_bias_moment,
    stitch_fc_moment,
    cotangent,
    task_mask,
):
    chan_size, planes = lax.axis_size("chan"), lax.axis_size("batch")
    chips = chan_size // 2
    me, plane = lax.axis_index("chan"), lax.axis_index("batch")
    core, chip = me % 2, me // 2
    swap = lambda value: trade(value, "chan", 1)
    mine = lambda a, b: jnp.where(core == 0, a, b)
    per_core, side, width_in = images.shape[0], images.shape[2], images.shape[-1]
    chan_width = conv_weight.shape[-1]
    full_chan = chan_width * chan_size
    units = fc_weight.shape[-1]
    rows = fc_weight.shape[1]
    cells = 36
    plane_chan = rows // cells
    group = 2 * per_core

    kernel_rows = jnp.transpose(conv_weight, (0, 1, 2, 4, 3)).astype(LOW)
    kernel_rows = kernel_rows.reshape(2, 9 * chan_width, width_in)
    cross = stitch_conv[:, ::-1]
    small = jnp.stack(
        [
            conv_bias,
            jnp.stack([stitch_conv[0, 0], stitch_conv[1, 1]]),
            jnp.stack([stitch_conv[0, 1], stitch_conv[1, 0]]),
            jnp.stack([stitch_conv[1, 0], stitch_conv[0, 1]]),
        ],
        axis=1,
    ).astype(LOW)
    small = jnp.pad(small, ((0, 0), (0, 12), (0, width_in - chan_width)))
    kernel_rows = jnp.concatenate([kernel_rows, small], axis=1)
    keep = mine(kernel_rows[0], kernel_rows[1])
    got = swap(mine(kernel_rows[1], kernel_rows[0]))
    halves = mine(keep, got), mine(got, keep)
    kernel_parts = gather_chips(halves[0], halves[1], chips)

    keep = mine(images[:, 0], images[:, 1])
    got = swap(mine(images[:, 1], images[:, 0]))
    tower_images = jnp.concatenate([mine(keep, got), mine(got, keep)], axis=0)
    tower_images = jnp.transpose(tower_images, (1, 2, 0, 3))

    fc_low = fc_weight.astype(LOW).reshape(2, plane_chan, cells, units)
    fc_low = jnp.swapaxes(fc_low, 1, 2).reshape(2, rows, units)
    fc_keep = mine(fc_low[0], fc_low[1])
    fc_got = swap(mine(fc_low[1], fc_low[0]))
    fc_halves = mine(fc_keep, fc_got), mine(fc_got, fc_keep)

    ordered = reorder(kernel_parts, chip)
    kernel = jnp.concatenate(
        [half[: 9 * chan_width].reshape(9, chan_width, width_in) for pair in ordered for half in pair],
        axis=1,
    )
    small_all = jnp.concatenate(
        [half[9 * chan_width :, :chan_width] for pair in ordered for half in pair], axis=1
    ).astype(WIDE)
    bias_all, self_mix, cross_mix, back_mix = (small_all[i] for i in range(4))

    conv_out = lax.conv_general_dilated(
        tower_images,
        kernel.reshape(3, 3, full_chan, width_in),
        (1, 1),
        "SAME",
        dimension_numbers=("HWNC", "HWOI", "HWNC"),
        preferred_element_type=WIDE,
    )
    act, slope = silu_and_slope(conv_out + bias_all)
    pooled = pool(act)
    pooled_other = swap(pooled)
    mixed = (self_mix * pooled + cross_mix * pooled_other).astype(LOW)
    mixed = mixed.reshape(cells, group, planes, plane_chan)
    pieces = jnp.transpose(mixed, (2, 1, 0, 3)).reshape(planes, group, rows)
    got = exchange_planes(pick(pieces, plane, planes))
    half = planes // 2
    gathered = reorder(
        gather_chips(jnp.stack(got[:half]), jnp.stack(got[half:]), chips), chip
    )
    tower_rows = jnp.concatenate(
        [jnp.stack([pair[h] for pair in gathered], axis=1) for h in range(2)], axis=0
    )
    tower_rows = tower_rows.reshape(planes * chips * group, rows)
    other_rows = swap(tower_rows)

    fc_tower = jnp.concatenate(fc_halves, axis=1)
    partial = jnp.dot(tower_rows, fc_tower, preferred_element_type=WIDE).astype(LOW)
    partial = partial.reshape(planes, chips * group, 2 * units)
    fc_sum = total(exchange_planes([partial[k] for k in range(planes)]))
    fc_keep = mine(fc_sum[:, :units], fc_sum[:, units:])
    fc_got = swap(mine(fc_sum[:, units:], fc_sum[:, :units]))
    fc_out = [mine(fc_keep, fc_got) + fc_bias[0], mine(fc_got, fc_keep) + fc_bias[1]]

    acts, slopes = zip(*[silu_and_slope(value) for value in fc_out])
    features_out = jnp.stack(
        [stitch_fc[t, 0] * acts[0] + stitch_fc[t, 1] * acts[1] for t in range(2)], axis=1
    ).astype(LOW)
    out_grad = [
        cotangent[:, t].astype(WIDE) * task_mask[:, t].astype(WIDE)[:, None] for t in range(2)
    ]
    stitch_fc_grad = jnp.stack(
        [jnp.stack([jnp.sum(out_grad[t] * acts[s], axis=0) for s in range(2)]) for t in range(2)]
    )
    grad_low = jnp.stack(
        [
            (slopes[s] * (stitch_fc[0, s] * out_grad[0] + stitch_fc[1, s] * out_grad[1])).astype(LOW)
            for s in range(2)
        ]
    )
    grad_all = exchange_planes([grad_low] * planes)
    grad_all = jnp.stack(grad_all, axis=1).reshape(2, planes * chips * group, units)
    grad_keep = mine(grad_all[0], grad_all[1])
    grad_got = swap(mine(grad_all[1], grad_all[0]))
    grad_tower = jnp.concatenate([mine(grad_keep, grad_got), mine(grad_got, grad_keep)], axis=1)

    flat_grad = lax.dot_general(
        grad_tower, fc_tower, (((1,), (1,)), ((), ())), preferred_element_type=WIDE
    ).astype(LOW)
    flat_grad = flat_grad.reshape(2, half, chips, group, rows)
    by_chip = reorder([(flat_grad[0, :, m], flat_grad[1, :, m]) for m in range(chips)], chip)
    first, second = scatter_chips(by_chip, chips)
    sums = jnp.concatenate([total(first), total(second)]).astype(LOW)
    got = reorder(exchange_planes([sums[k] for k in range(planes)]), plane)
    mixed_grad = jnp.stack(got)
    mixed_grad_other = swap(mixed_grad)

    def unflatten(value):
        value = value.astype(WIDE).reshape(planes, group, cells, plane_chan)
        return jnp.transpose(value, (2, 1, 0, 3)).reshape(6, 6, group, full_chan)

    own_grad, other_grad = unflatten(mixed_grad), unflatten(mixed_grad_other)
    self_stitch = jnp.sum(own_grad * pooled, axis=(0, 1, 2))
    cross_stitch = jnp.sum(own_grad * pooled_other, axis=(0, 1, 2))
    pooled_grad = (self_mix * own_grad + back_mix * other_grad) * (1.0 / 9.0)
    conv_grad = (slope * spread(spread(pooled_grad, 0), 1)).astype(LOW)
    bias_grad = jnp.sum(conv_grad.astype(WIDE), axis=(0, 1, 2))

    padded = jnp.pad(tower_images, ((1, 1), (1, 1), (0, 0), (0, 0)))
    taps = []
    for down in range(3):
        for right in range(3):
            window = padded[down : down + side, right : right + side]
            taps.append(
                lax.dot_general(
                    conv_grad.reshape(-1, full_chan),
                    window.reshape(-1, width_in),
                    (((0,), (0,)), ((), ())),
                    preferred_element_type=WIDE,
                ).astype(LOW)
            )
    kernel_grad = jnp.stack(taps).reshape(9, chips, 2, chan_width, width_in)
    smalls = jnp.stack([bias_grad, self_stitch, cross_stitch]).astype(LOW)
    smalls = jnp.pad(
        smalls.reshape(3, chips, 2, chan_width), ((0, 13), (0, 0), (0, 0), (0, width_in - chan_width))
    )
    blocks = [
        tuple(
            jnp.concatenate([kernel_grad[:, m, c].reshape(9 * chan_width, width_in), smalls[:, m, c]])
            for c in range(2)
        )
        for m in range(chips)
    ]
    first, second = scatter_chips(reorder(blocks, chip), chips)
    sums = [total(first).astype(LOW), total(second).astype(LOW)]
    keep = mine(sums[0], sums[1])
    got = swap(mine(sums[1], sums[0]))
    towers = jnp.stack([mine(keep, got), mine(got, keep)])
    towers = lax.psum(towers, "batch").astype(WIDE)
    stitch_fc_grad = lax.psum(stitch_fc_grad.astype(LOW), "batch").astype(WIDE)

    images_grad = lax.conv_general_dilated(
        conv_grad,
        kernel.reshape(3, 3, full_chan, width_in)[::-1, ::-1],
        (1, 1),
        "SAME",
        dimension_numbers=("HWNC", "HWIO", "HWNC"),
        preferred_element_type=WIDE,
    ).astype(LOW)
    images_grad = jnp.transpose(images_grad, (2, 0, 1, 3))
    keep = mine(images_grad[:per_core], images_grad[per_core:])
    got = swap(mine(images_grad[per_core:], images_grad[:per_core]))
    images_grad = jnp.stack([mine(keep, got), mine(got, keep)], axis=1)

    both_rows = [mine(tower_rows, other_rows), mine(other_rows, tower_rows)]
    fc_weight_grad = jnp.stack(
        [
            lax.dot_general(
                jnp.swapaxes(both_rows[t].reshape(-1, cells, plane_chan), 1, 2).reshape(-1, rows),
                grad_all[t],
                (((0,), (0,)), ((), ())),
                preferred_element_type=WIDE,
            )
            for t in range(2)
        ]
    )
    fc_bias_grad = jnp.sum(grad_all.astype(WIDE), axis=1)

    conv_weight_grad = jnp.swapaxes(
        towers[:, : 9 * chan_width].reshape(2, 3, 3, chan_width, width_in), 3, 4
    )
    conv_bias_grad = towers[:, 9 * chan_width, :chan_width]
    straight = towers[:, 9 * chan_width + 1, :chan_width]
    crossed = towers[:, 9 * chan_width + 2, :chan_width]
    stitch_conv_grad = jnp.stack(
        [jnp.stack([straight[0], crossed[0]]), jnp.stack([crossed[1], straight[1]])]
    )
    grads = (
        conv_weight_grad,
        conv_bias_grad,
        stitch_conv_grad,
        fc_weight_grad,
        fc_bias_grad,
        stitch_fc_grad,
    )
    params = (conv_weight, conv_bias, stitch_conv, fc_weight, fc_bias, stitch_fc)
    moments = (
        conv_moment,
        bias_moment,
        stitch_conv_moment,
        fc_moment,
        fc_bias_moment,
        stitch_fc_moment,
    )
    rates = (LEARN_RATE, BIAS_RATE, STITCH_RATE, LEARN_RATE, BIAS_RATE, STITCH_RATE)
    fresh = [MOMENTUM * moments[place] + grads[place] for place in range(6)]
    updated = [params[place] - rates[place] * fresh[place] for place in range(6)]
    return (features_out, images_grad, *updated, *fresh)


def four_by_four(
    images,
    conv_weight,
    conv_bias,
    stitch_conv,
    fc_weight,
    fc_bias,
    stitch_fc,
    conv_moment,
    bias_moment,
    stitch_conv_moment,
    fc_moment,
    fc_bias_moment,
    stitch_fc_moment,
    cotangent,
    task_mask,
):
    chips, planes = lax.axis_size("chan") // 2, lax.axis_size("batch")
    me, plane = lax.axis_index("chan"), lax.axis_index("batch")
    core, chip = me % 2, me // 2
    as_scalar = lambda value: value.reshape(1).astype(jnp.int32)
    core_at, chip_at, plane_at = as_scalar(core), as_scalar(chip), as_scalar(plane)
    swap = lambda value: trade(value, "chan", 1)
    mine = lambda a, b: jnp.where(core == 0, a, b)
    per_core, side, width_in = images.shape[0], images.shape[2], images.shape[-1]
    shard = conv_weight.shape[-1]
    units = fc_weight.shape[-1]
    half = planes // 2

    as_rows = lambda value: jnp.transpose(value, (0, 1, 2, 4, 3)).reshape(2, TAPS * shard, width_in)
    keep, give = pack_kernels(as_rows(conv_weight), conv_bias, stitch_conv, core_at)
    got = swap(give)
    kernel_parts = [part for pair in gather_chips(keep, got, chips) for part in pair]
    fc_own, fc_give = fc_prepare(fc_weight, core_at, kernel_parts[3])
    fc_cross = swap(fc_give)

    late_core, kernel_parts[3] = tie(core, kernel_parts[3])
    towers = lax.optimization_barrier(jnp.transpose(images, (1, 2, 3, 0, 4)))
    keep, give = (jnp.where(late_core == 0, towers[a], towers[1 - a]) for a in range(2))
    tower_images = jnp.concatenate([keep, swap(give)], axis=2)
    tower_images = jnp.pad(tower_images, ((1, 1), (1, 1), (0, 0), (0, 0)))

    pooled, slope, small_all = conv_forward(tower_images, kernel_parts, core_at, chip_at)
    pooled_other = swap(pooled)
    pieces = mix_pieces(pooled, pooled_other, small_all, core_at, plane_at, planes)
    got = exchange_planes(pieces)
    gathered = gather_chips(jnp.stack(got[:half]), jnp.stack(got[half:]), chips)
    tower_rows, *partial = fc_forward(
        [part for pair in gathered for part in pair], (fc_own, fc_cross), chip_at, chips, planes
    )
    other_rows = swap(tower_rows)

    fc_sum = total(exchange_planes(partial))
    fc_out = [fc_sum[:, :units], swap(fc_sum[:, units:])]
    fc_out = [fc_out[a] + mine(fc_bias[a], fc_bias[1 - a]) for a in range(2)]
    acts, slopes = zip(*[silu_and_slope(value) for value in fc_out])
    mix = [[mine(stitch_fc[a, b], stitch_fc[1 - a, 1 - b]) for b in range(2)] for a in range(2)]
    features = [mix[a][0] * acts[0] + mix[a][1] * acts[1] for a in range(2)]
    features_out = jnp.stack([mine(features[0], features[1]), mine(features[1], features[0])], axis=1)
    masked = [cotangent[:, t].astype(WIDE) * task_mask[:, t].astype(WIDE)[:, None] for t in range(2)]
    out_grad = [mine(masked[a], masked[1 - a]) for a in range(2)]
    grad_low = jnp.stack(
        [(slopes[b] * (mix[0][b] * out_grad[0] + mix[1][b] * out_grad[1])).astype(LOW) for b in range(2)]
    )
    stitch_fc_grad = jnp.stack(
        [jnp.stack([jnp.sum(out_grad[a] * acts[b], axis=0) for b in range(2)]) for a in range(2)]
    )
    grads = exchange_planes([grad_low] * planes)
    grads_cross = swap(jnp.stack([value[1] for value in grads]))

    step = done = None

    def update_own(gate, value):
        nonlocal step, done
        *step, done = fc_update(fc_weight, fc_moment, tower_rows, grads, core_at, 0, 0, None, gate)
        value, done = tie(value, done)
        return gate, value

    blocks = fc_backward(grads, grads_cross, (fc_own, fc_cross), chip_at, chips, planes)
    first, second = scatter_chips(
        [blocks[2 * j : 2 * j + 2] for j in range(chips)], chips, later=update_own
    )
    sums = [total([value[i] for value in part]).astype(LOW) for part in (first, second) for i in range(half)]
    mixed_grad = exchange_planes(sums)
    *step, token = fc_update(fc_weight, fc_moment, tower_rows, grads, core_at, 0, 1, step, sums[-1])
    mixed_grad[1], done, token = tie(mixed_grad[1], done, token)
    done = done + token
    mixed_grad_other = swap(jnp.stack(mixed_grad))

    *blocks, conv_grad = conv_backward(
        done, mixed_grad, mixed_grad_other, pooled, pooled_other, slope, tower_images, small_all, core_at, chip_at, plane_at
    )

    def turned_conv(grad):
        return lax.conv_general_dilated(
            grad,
            kernel[::-1, ::-1],
            (1, 1),
            "SAME",
            dimension_numbers=("HWNC", "HWIO", "HWNC"),
            preferred_element_type=WIDE,
        ).astype(LOW)

    full_chan = conv_grad.shape[-1]
    ordered = reorder([(kernel_parts[2 * j], kernel_parts[2 * j + 1]) for j in range(chips)], chip)
    ordered = [part for a, b in ordered for part in (mine(a, b), mine(b, a))]
    kernel = jnp.concatenate(
        [part[: TAPS * shard].reshape(3, 3, shard, width_in) for part in ordered], axis=2
    )
    images_grad = None

    def after_sums(gate, value):
        nonlocal images_grad
        gate, grad = tie(gate, conv_grad)
        value, images_grad = tie(value, turned_conv(grad))
        return gate, value

    first, second = scatter_chips(
        [blocks[2 * j : 2 * j + 2] for j in range(chips)],
        chips,
        later=after_sums,
    )
    towers = jnp.stack([total(first).astype(LOW), swap(total(second).astype(LOW))])
    lines = towers.shape[1]

    vectors = stitch_fc_grad.reshape(4, units)
    packed = [vectors[:, at : at + width_in] for at in range(0, units, width_in)]
    packed = jnp.concatenate(
        [jnp.pad(value, ((0, 0), (0, width_in - value.shape[1]))) for value in packed]
    ).astype(LOW)
    tail = (-(2 * lines + packed.shape[0])) % (planes * EXTRA)
    flat = jnp.concatenate([towers.reshape(-1, width_in), jnp.pad(packed, ((0, tail), (0, 0)))])
    flat = flat.reshape(planes, -1, width_in)
    quarters = [lax.dynamic_index_in_dim(flat, plane ^ k, 0, keepdims=False) for k in range(planes)]
    quarters = exchange_planes(quarters)
    *step, done = fc_update(fc_weight, fc_moment, other_rows, grads, core_at, 1, 0, step, quarters[0])
    quarters[1], done = tie(quarters[1], done)
    quarter = total(quarters).astype(LOW)
    quarters = exchange_planes([quarter] * planes)
    *step, done = fc_update(fc_weight, fc_moment, other_rows, grads, core_at, 1, 1, step, done)

    images_grad, quarters[0] = tie(images_grad, quarters[0])
    keep, got = images_grad[:, :, :per_core], swap(images_grad[:, :, per_core:])
    images_grad = order_towers(keep, got, core_at)
    images_grad = jnp.transpose(images_grad, (3, 1, 2, 0, 4))

    new_small = small_update(
        (done, images_grad),
        quarters,
        lines,
        (as_rows(conv_weight), conv_bias, stitch_conv, stitch_fc),
        (as_rows(conv_moment), bias_moment, stitch_conv_moment, stitch_fc_moment),
        core_at,
        plane_at,
    )

    fc_bias_grad = sum(jnp.sum(value.astype(WIDE), axis=1) for value in grads)
    fc_bias_grad = mine(fc_bias_grad, fc_bias_grad[::-1])
    new_fc_bias_moment = MOMENTUM * fc_bias_moment + fc_bias_grad
    new_fc_bias = fc_bias - BIAS_RATE * new_fc_bias_moment

    as_given = lambda value: jnp.swapaxes(value.reshape(2, 3, 3, shard, width_in), 3, 4)
    params, fresh = list(new_small[:4]), list(new_small[4:])
    params[0], fresh[0] = as_given(params[0]), as_given(fresh[0])
    params[3:3], fresh[3:3] = (step[0], new_fc_bias), (step[1], new_fc_bias_moment)
    images_grad = jnp.transpose(images_grad, (0, 3, 1, 2, 4))
    return (features_out.astype(LOW), images_grad, *params, *fresh)


def solution(mesh):
    chan_last = P(None, None, None, None, "chan")
    fc_spec = P(None, "batch", "chan")
    params = (chan_last, P(None, "chan"), P(None, None, "chan"), fc_spec, P(None, "chan"), P(None, None, "chan"))
    image_spec = P(("batch", "chan"), None, None, None, None)
    feature_spec = P("batch", None, "chan")
    in_specs = (image_spec, *params, *params, feature_spec, P("batch", None))
    out_specs = (feature_spec, image_spec, *params, *params)
    body = four_by_four if dict(mesh.shape) == {"chan": 8, "batch": 4} else any_mesh
    return jax.shard_map(body, mesh=mesh, in_specs=in_specs, out_specs=out_specs, check_vma=False)
```

```python
import functools

import jax
import jax.numpy as jnp
from jax import lax
from jax.experimental import pallas as pl
from jax.experimental.pallas import tpu as pltpu
from jax.sharding import PartitionSpec as P

MOMENTUM = 0.9
LEARN_RATE = 0.002
BIAS_RATE = 0.02
STITCH_RATE = 0.02
LOW = jnp.bfloat16
WIDE = jnp.float32
TAPS = 9
CELLS = 36
EXTRA = 16
PORTION = 160
LANES = 128
WHOLE = pl.BlockSpec(memory_space=pltpu.VMEM)
SCALARS = pl.BlockSpec(memory_space=pltpu.SMEM)
BRIEF = pl.CostEstimate(flops=0, bytes_accessed=0, transcendentals=0)
NN = (((1,), (0,)), ((), ()))
NT = (((1,), (1,)), ((), ()))
TN = (((0,), (0,)), ((), ()))


def like(shape, dtype):
    return jax.ShapeDtypeStruct(shape, dtype)


def dot(a, b, dims):
    return lax.dot_general(a, b, dims, preferred_element_type=WIDE)


def trade(value, axis, bit):
    size = lax.axis_size(axis)
    return lax.ppermute(value, axis, [(i, i ^ bit) for i in range(size)])


def tie(*values):
    return lax.optimization_barrier(values)


def gather_chips(first, second, chips):
    if chips == 4:
        first_y = trade(first, "chan", 4)
        second_x = trade(second, "chan", 2)
        first_x = trade(first, "chan", 2)
        second_y = trade(second, "chan", 4)
        first_d = trade(first_y, "chan", 2)
        second_d = trade(second_x, "chan", 4)
        return [(first, second), (first_x, second_x), (first_y, second_y), (first_d, second_d)]
    return [(first, second)] + [
        (trade(first, "chan", 2 * j), trade(second, "chan", 2 * j)) for j in range(1, chips)
    ]


def add_low(a, b):
    return (a.astype(WIDE) + b.astype(WIDE)).astype(LOW)


def scatter_chips(parts, chips, later=lambda gate, value: (gate, value)):
    if chips == 4:
        from_x = trade(parts[3][0], "chan", 2)
        from_y = trade(parts[3][1], "chan", 4)
        first_x = trade(parts[1][0], "chan", 2)
        second_y = trade(parts[2][1], "chan", 4)
        to_y = add_low(parts[2][0], from_x)
        first_y = trade(to_y, "chan", 4)
        to_x = add_low(parts[1][1], from_y)
        to_x, first_y = later(to_x, first_y)
        second_x = trade(to_x, "chan", 2)
        return (parts[0][0], first_x, first_y), (parts[0][1], second_x, second_y)
    got = [(trade(parts[j][0], "chan", 2 * j), trade(parts[j][1], "chan", 2 * j)) for j in range(1, chips)]
    return (
        (parts[0][0],) + tuple(pair[0] for pair in got),
        (parts[0][1],) + tuple(pair[1] for pair in got),
    )


def total(values):
    out = values[0].astype(WIDE)
    for value in values[1:]:
        out = out + value.astype(WIDE)
    return out


def exchange_planes(parts):
    got = {k: trade(parts[k], "batch", k) for k in range(len(parts) - 1, 0, -1)}
    return [parts[0]] + [got[k] for k in range(1, len(parts))]


def gate_of(value):
    return 1.0 / (1.0 + jnp.exp(-value))


def silu_and_slope(value):
    gate = gate_of(value)
    act = value * gate
    return act, gate + act * (1.0 - gate)


def lane_place(width):
    return lax.broadcasted_iota(jnp.int32, (1, LANES), 1) // width


def shift_slots(value, width, source, target):
    if source == target:
        return value
    return pltpu.roll(value, ((target - source) * width) % LANES, 1)


def pack_kernels(conv_weight, conv_bias, stitch_conv, core):
    _, lines, width_in = conv_weight.shape
    shard = conv_bias.shape[-1]

    def kernel(core_ref, w_hbm, bias_hbm, mix_hbm, keep_ref, give_ref, w_ref, bias_ref, mix_ref, sems):
        pairs = ((bias_hbm, bias_ref), (mix_hbm, mix_ref), (w_hbm, w_ref))
        copies = [pltpu.make_async_copy(source, held, sems.at[i]) for i, (source, held) in enumerate(pairs)]
        for copy in copies:
            copy.start()
        first = core_ref[0] == 0
        for copy in copies:
            copy.wait()
        for a, out in enumerate((keep_ref, give_ref)):
            out[:lines, :] = w_ref[core_ref[0] ^ a].astype(LOW)
            choose = lambda p, q: jnp.where(first, *((q, p) if a else (p, q)))
            rows = [
                choose(bias_ref[0:1, :], bias_ref[1:2, :]),
                choose(mix_ref[0, 0:1, :], mix_ref[1, 1:2, :]),
                choose(mix_ref[0, 1:2, :], mix_ref[1, 0:1, :]),
                choose(mix_ref[1, 0:1, :], mix_ref[0, 1:2, :]),
                jnp.zeros((EXTRA - 4, shard), WIDE),
            ]
            out[lines:, :] = jnp.zeros((EXTRA, width_in), LOW)
            out[lines:, :shard] = jnp.concatenate(rows, axis=0).astype(LOW)

    sources = (conv_weight, conv_bias, stitch_conv)
    return pl.pallas_call(
        kernel,
        in_specs=[SCALARS] + [pl.BlockSpec(memory_space=pltpu.HBM)] * 3,
        out_specs=[WHOLE] * 2,
        out_shape=[like((lines + EXTRA, width_in), LOW)] * 2,
        scratch_shapes=[pltpu.VMEM(value.shape, WIDE) for value in sources] + [pltpu.SemaphoreType.DMA((3,))],
        compiler_params=pltpu.CompilerParams(vmem_limit_bytes=8 << 20),
        cost_estimate=BRIEF,
    )(core, *(pltpu.with_memory_space_constraint(value, pltpu.HBM) for value in sources))


def fc_prepare(fc_weight, core, gate):
    _, rows, units = fc_weight.shape
    width = rows // CELLS
    fc_weight = pltpu.with_memory_space_constraint(fc_weight, pltpu.HBM)

    def kernel(core_ref, own_ref, other_ref, _, keep_ref, give_ref):
        for source, out in ((own_ref, keep_ref), (other_ref, give_ref)):
            for cell in range(CELLS):
                out[pl.ds(cell * width, width), :] = source[
                    0, pl.ds(cell, width, stride=CELLS), :
                ].astype(LOW)

    return pl.pallas_call(
        kernel,
        grid_spec=pltpu.PrefetchScalarGridSpec(
            num_scalar_prefetch=1,
            grid=(units // LANES,),
            in_specs=[
                pl.BlockSpec((1, rows, LANES), lambda j, core: (core[0], 0, j)),
                pl.BlockSpec((1, rows, LANES), lambda j, core: (core[0] ^ 1, 0, j)),
                pl.BlockSpec(memory_space=pl.ANY),
            ],
            out_specs=[pl.BlockSpec((rows, LANES), lambda j, core: (0, j))] * 2,
        ),
        out_shape=[like((rows, units), LOW)] * 2,
        compiler_params=pltpu.CompilerParams(vmem_limit_bytes=12 << 20),
        cost_estimate=BRIEF,
    )(core, fc_weight, fc_weight, gate)


def conv_forward(images, parts, core, chip):
    high, wide, group, width_in = images.shape
    side = high - 2
    count = len(parts)
    shard = (parts[0].shape[0] - EXTRA) // TAPS
    full = shard * count
    slots = LANES // shard

    def kernel(core_ref, chip_ref, x_ref, *refs):
        pieces = refs[:count]
        pooled_ref, slope_out, small_ref, weights_out = refs[count : count + 4]
        weights, acc, slope_ref, sems = refs[count + 4 :]
        copies = [pltpu.make_async_copy(slope_ref.at[h], slope_out.at[h], sems.at[h]) for h in range(side)]
        copies += [
            pltpu.make_async_copy(
                weights.at[:, pl.ds(tap * width_in, width_in)], weights_out.at[tap], sems.at[side + tap]
            )
            for tap in range(TAPS)
        ]
        lane = lax.broadcasted_iota(jnp.int32, (EXTRA, LANES), 1) // shard
        smalls = [jnp.zeros((EXTRA, LANES), WIDE) for _ in range(full // LANES)]
        for j in range(count // 2):
            for r in range(2):
                piece = pieces[2 * j + r]
                where = (chip_ref[0] ^ j) * 2 + (core_ref[0] ^ r)
                at = pl.ds(pl.multiple_of(where * shard, shard), shard)
                for tap in range(TAPS):
                    weights[at, tap * width_in : (tap + 1) * width_in] = piece[tap * shard : (tap + 1) * shard, :]
                row = piece[TAPS * shard :, :LANES].astype(WIDE)
                spread = row
                for s in range(1, slots):
                    spread = spread + pltpu.roll(row, s * shard, 1)
                for v in range(len(smalls)):
                    smalls[v] = jnp.where(lane + v * slots == where, spread, smalls[v])
        for v, value in enumerate(smalls):
            small_ref[:, v * LANES : (v + 1) * LANES] = value
        for copy in copies[side:]:
            copy.start()
        line = side * group
        bias = small_ref[0:1, :]
        for low, high_row in ((0, (side + 1) // 2), ((side + 1) // 2, side)):
            tall = high_row - low
            windows = [
                x_ref[tap // 3 + low : tap // 3 + high_row, tap % 3 : tap % 3 + side].reshape(tall * line, width_in)
                for tap in range(TAPS)
            ]
            acc[low * line : high_row * line, :] = dot(jnp.concatenate(windows, axis=1), weights[...], NT)
        for h in range(side):
            value, slope = silu_and_slope(acc[h * line : (h + 1) * line, :] + bias)
            slope_ref[h] = slope.reshape(side, group, full).astype(LOW)
            acc[h * line : (h + 1) * line, :] = value
            copies[h].start()
        cell = lambda h, w: acc[(h * side + w) * group : (h * side + w + 1) * group, :]
        for r in range(6):
            rows = [cell(2 * r, w) + cell(2 * r + 1, w) + cell(2 * r + 2, w) for w in range(side)]
            for c in range(6):
                pooled_ref[6 * r + c] = (rows[2 * c] + rows[2 * c + 1] + rows[2 * c + 2]) * (1.0 / 9.0)
        for copy in copies:
            copy.wait()

    area = side * side * group
    return pl.pallas_call(
        kernel,
        in_specs=[SCALARS] * 2 + [WHOLE] * (1 + count),
        out_specs=[WHOLE, pl.BlockSpec(memory_space=pltpu.HBM), WHOLE, pl.BlockSpec(memory_space=pltpu.HBM)],
        out_shape=[
            like((CELLS, group, full), WIDE),
            pltpu.HBM((side, side, group, full), LOW),
            like((EXTRA, full), WIDE),
            pltpu.HBM((TAPS, full, width_in), LOW),
        ],
        scratch_shapes=[
            pltpu.VMEM((full, TAPS * width_in), LOW),
            pltpu.VMEM((area, full), WIDE),
            pltpu.VMEM((side, side, group, full), LOW),
            pltpu.SemaphoreType.DMA((side + TAPS,)),
        ],
        compiler_params=pltpu.CompilerParams(vmem_limit_bytes=16 << 20),
        cost_estimate=BRIEF,
    )(core, chip, images, *parts)


def turn(value):
    half = value.shape[0] // 2
    return jnp.concatenate([value[half:], value[:half]], axis=0)


def mix_pieces(pooled, other, small, core, plane, planes):
    cells, group, full = pooled.shape
    width = full // planes
    per = LANES // width

    def kernel(core_ref, plane_ref, a_ref, b_ref, small_ref, *refs):
        outs, held = refs[:planes], refs[planes]
        first = core_ref[0] == 0
        place = lane_place(width)
        one, two = small_ref[1:2, :], small_ref[2:3, :]
        for start in range(0, cells, per):
            mixed = [
                one * a_ref[start + i] + two * turn(b_ref[start + i]) for i in range(per)
            ]
            mixed = [jnp.where(first, value, turn(value)) for value in mixed]
            for p in range(planes):
                column, source = divmod(p * width, LANES)
                out = None
                for i in range(per):
                    moved = shift_slots(
                        mixed[i][:, column * LANES : (column + 1) * LANES], width, source // width, i
                    )
                    out = moved if out is None else jnp.where(place == i, moved, out)
                held[p, :, start * width : (start + per) * width] = out.astype(LOW)
        for k in range(planes):
            outs[k][...] = held[plane_ref[0] ^ k]

    rows = cells * width
    return pl.pallas_call(
        kernel,
        in_specs=[SCALARS] * 2 + [WHOLE] * 3,
        out_specs=[WHOLE] * planes,
        out_shape=[like((group, rows), LOW)] * planes,
        scratch_shapes=[pltpu.VMEM((planes, group, rows), LOW)],
        compiler_params=pltpu.CompilerParams(vmem_limit_bytes=8 << 20),
        cost_estimate=BRIEF,
    )(core, plane, pooled, other, small)


def fc_forward(gathered, weights, chip, chips, planes):
    half, group, rows = gathered[0].shape
    units = weights[0].shape[-1]
    count = 2 * chips
    block = chips * group

    def kernel(chip_ref, *refs):
        pieces, (own, cross) = refs[:count], refs[count : count + 2]
        rows_ref, outs = refs[count + 2], refs[count + 3 :]
        for j in range(chips):
            for h in range(2):
                for i in range(half):
                    start = ((h * half + i) * chips + (chip_ref[0] ^ j)) * group
                    rows_ref[pl.ds(pl.multiple_of(start, group), group), :] = pieces[2 * j + h][i]
        for n, weight in enumerate((own, cross)):
            part = dot(rows_ref[...], weight[...], NN)
            for k in range(planes):
                outs[k][:, n * units : (n + 1) * units] = part[k * block : (k + 1) * block].astype(
                    outs[k].dtype
                )

    n_images = planes * block
    return pl.pallas_call(
        kernel,
        in_specs=[SCALARS] + [WHOLE] * (count + 2),
        out_specs=[WHOLE] * (1 + planes),
        out_shape=[like((n_images, rows), LOW)]
        + [like((block, 2 * units), LOW if k else WIDE) for k in range(planes)],
        compiler_params=pltpu.CompilerParams(vmem_limit_bytes=16 << 20),
        cost_estimate=BRIEF,
    )(chip, *gathered, *weights)


def fc_backward(grads, crossed, weights, chip, chips, planes):
    _, block, units = grads[0].shape
    rows = weights[0].shape[0]
    group = block // chips
    half = planes // 2
    n_images = planes * block

    def kernel(chip_ref, *refs):
        pieces, got = refs[:planes], refs[planes]
        own, cross = refs[planes + 1 : planes + 3]
        outs = refs[planes + 3 : planes + 3 + 2 * chips]
        held_own, held_cross, held = refs[planes + 3 + 2 * chips :]
        for k in range(planes):
            held_own[pl.ds(k * block, block), :] = pieces[k][0]
            held_cross[pl.ds(k * block, block), :] = got[k]
        step = rows // 3
        for s in range(3):
            at = pl.ds(s * step, step)
            value = dot(held_own[...], own[at, :], NT) + dot(held_cross[...], cross[at, :], NT)
            held[:, at] = value.astype(LOW)
        for j in range(chips):
            for h in range(2):
                for i in range(half):
                    start = ((h * half + i) * chips + (chip_ref[0] ^ j)) * group
                    outs[2 * j + h][i] = held[pl.ds(pl.multiple_of(start, group), group), :]

    return pl.pallas_call(
        kernel,
        in_specs=[SCALARS] + [WHOLE] * (planes + 3),
        out_specs=[WHOLE] * (2 * chips),
        out_shape=[like((half, group, rows), LOW)] * (2 * chips),
        scratch_shapes=[
            pltpu.VMEM((n_images, units), LOW),
            pltpu.VMEM((n_images, units), LOW),
            pltpu.VMEM((n_images, rows), LOW),
        ],
        compiler_params=pltpu.CompilerParams(vmem_limit_bytes=20 << 20),
        cost_estimate=BRIEF,
    )(chip, *grads, crossed, *weights)


def conv_backward(gate, own, other, pooled, pooled_other, slope, images, small, core, chip, plane):
    planes = len(own)
    cells, group, full = pooled.shape
    high, _, _, width_in = images.shape
    side = high - 2
    width = full // planes
    per = LANES // width
    columns = full // LANES
    shards = lax.axis_size("chan")
    shard = full // shards
    slots = LANES // shard
    area = side * side * group

    def covering(h):
        return [r for r in range(6) if 2 * r <= h <= 2 * r + 2]

    def kernel(core_ref, chip_ref, plane_ref, gate_ref, *refs):
        own_refs, other_ref = refs[:planes], refs[planes]
        a_ref, b_ref, slope_ref, x_ref, small_ref = refs[planes + 1 : planes + 6]
        outs = refs[planes + 6 : planes + 6 + shards]
        grad_out = refs[planes + 6 + shards]
        flat, pool_grad, turned, taps, smalls, grad_ref, sem = refs[planes + 7 + shards :]
        copy = pltpu.make_async_copy(grad_ref, grad_out, sem)
        place = lane_place(width)
        first = core_ref[0] == 0
        for k in range(planes):
            for t, value in enumerate((own_refs[k][...], other_ref[k])):
                value = value.astype(WIDE)
                flat[t, plane_ref[0] ^ k] = jnp.where(first, value, turn(value))
        one, back = small_ref[1:2, :] * (1.0 / 9.0), small_ref[3:4, :] * (1.0 / 9.0)
        sum_one = jnp.zeros((group, full), WIDE)
        sum_two = jnp.zeros((group, full), WIDE)
        for cell in range(cells):
            column, source = divmod(cell * width, LANES)
            both = []
            for t in range(2):
                blocks = []
                for v in range(columns):
                    out = None
                    for i in range(per):
                        piece = flat[t, v * per + i, :, column * LANES : (column + 1) * LANES]
                        moved = shift_slots(piece, width, source // width, i)
                        out = moved if out is None else jnp.where(place == i, moved, out)
                    blocks.append(out)
                both.append(jnp.concatenate(blocks, axis=1))
            sum_one += both[0] * a_ref[cell]
            sum_two += both[0] * turn(b_ref[cell])
            pool_grad[cell] = one * both[0] + back * both[1]
        sum_bias = jnp.zeros((group, full), WIDE)
        for h in range(side):
            line = [sum(pool_grad[6 * r + c] for r in covering(h)) for c in range(6)]
            for w in range(side):
                value = sum(line[c] for c in covering(w))
                value = (value * slope_ref[h, w].astype(WIDE)).astype(LOW)
                grad_ref[h, w] = value
                sum_bias += value.astype(WIDE)
        copy.start()
        turned[...] = grad_ref[...].reshape(area, full).T
        for start in range(0, TAPS, 2):
            some = range(start, min(start + 2, TAPS))
            windows = [
                x_ref[tap // 3 : tap // 3 + side, tap % 3 : tap % 3 + side].reshape(area, width_in) for tap in some
            ]
            part = dot(turned[...], jnp.concatenate(windows, axis=1), NN)
            for n, tap in enumerate(some):
                taps[tap] = part[:, n * width_in : (n + 1) * width_in].astype(LOW)
        sums = [jnp.sum(value, axis=0, keepdims=True) for value in (sum_bias, sum_one, sum_two)]
        sums = jnp.concatenate(sums + [jnp.zeros((EXTRA - 3, full), WIDE)], axis=0)
        for v in range(columns):
            smalls[v] = sums[:, v * LANES : (v + 1) * LANES]
        lane = lax.broadcasted_iota(jnp.int32, (EXTRA, LANES), 1)
        for j in range(shards // 2):
            for r in range(2):
                where = (chip_ref[0] ^ j) * 2 + (core_ref[0] ^ r)
                at = pl.ds(pl.multiple_of(where * shard, shard), shard)
                out = outs[2 * j + r]
                for tap in range(TAPS):
                    out[tap * shard : (tap + 1) * shard, :] = taps[tap, at, :]
                row = smalls[where // slots]
                value = jnp.zeros((EXTRA, LANES), WIDE)
                for s in range(slots):
                    moved = row if s == 0 else pltpu.roll(row, LANES - s * shard, 1)
                    value = jnp.where(where % slots == s, moved, value)
                out[TAPS * shard :, :] = jnp.zeros((EXTRA, width_in), LOW)
                out[TAPS * shard :, :LANES] = jnp.where(lane < shard, value, 0.0).astype(LOW)
        copy.wait()

    return pl.pallas_call(
        kernel,
        in_specs=[SCALARS] * 3 + [pl.BlockSpec(memory_space=pl.ANY)] + [WHOLE] * (planes + 6),
        out_specs=[WHOLE] * shards + [pl.BlockSpec(memory_space=pltpu.HBM)],
        out_shape=[like((TAPS * shard + EXTRA, width_in), LOW)] * shards
        + [pltpu.HBM((side, side, group, full), LOW)],
        scratch_shapes=[
            pltpu.VMEM((2, planes, group, cells * width), WIDE),
            pltpu.VMEM((cells, group, full), WIDE),
            pltpu.VMEM((full, area), LOW),
            pltpu.VMEM((TAPS, full, width_in), LOW),
            pltpu.VMEM((columns, EXTRA, LANES), WIDE),
            pltpu.VMEM((side, side, group, full), LOW),
            pltpu.SemaphoreType.DMA(()),
        ],
        compiler_params=pltpu.CompilerParams(vmem_limit_bytes=14 << 20),
        cost_estimate=BRIEF,
    )(core, chip, plane, gate, *own, other, pooled, pooled_other, slope, images, small)


def fc_update(weight, moment, rows, grads, core, which, part, previous, gate):
    _, depth, units = weight.shape
    width = depth // CELLS
    n_images = rows.shape[0]
    planes = len(grads)
    block = n_images // planes
    columns = units // LANES
    steps = 4
    few = width // 2
    tall = depth // 2 // steps
    hbm = pl.BlockSpec(memory_space=pltpu.HBM)
    weight, moment = (pltpu.with_memory_space_constraint(value, pltpu.HBM) for value in (weight, moment))

    def kernel(core_ref, w_hbm, m_hbm, rows_ref, *refs):
        grad_refs = refs[:planes]
        new_w, new_m, token, joined, product, held_w, held_m, sems = refs[-8:]
        tower = core_ref[0] ^ which

        def copies(pairs, s, first):
            at = pl.ds((part * steps + s) * tall, tall)
            return [
                pltpu.make_async_copy(held.at[s], hbm_ref.at[tower, at, :], sems.at[s, first + i])
                if first
                else pltpu.make_async_copy(hbm_ref.at[tower, at, :], held.at[s], sems.at[s, i])
                for i, (hbm_ref, held) in enumerate(pairs)
            ]

        loads = [copies(((w_hbm, held_w), (m_hbm, held_m)), s, 0) for s in range(steps)]
        stores = [copies(((new_w, held_w), (new_m, held_m)), s, 2) for s in range(steps)]
        for pair in loads:
            for copy in pair:
                copy.start()
        token[...] = jnp.zeros_like(token)
        for k in range(planes):
            joined[pl.ds(k * block, block), :] = grad_refs[k][which]
        for v in range(columns):
            grad = dot(rows_ref[...], joined[:, v * LANES : (v + 1) * LANES], TN)
            for cell in range(CELLS):
                start = cell * width + part * few
                product[v, pl.ds(cell, few, stride=CELLS), :] = grad[start : start + few]
        for s in range(steps):
            for copy in loads[s]:
                copy.wait()
            for v in range(columns):
                at = (s, slice(None), slice(v * LANES, (v + 1) * LANES))
                fresh = MOMENTUM * held_m[at] + product[v, s * tall : (s + 1) * tall, :]
                held_m[at] = fresh
                held_w[at] = held_w[at] - LEARN_RATE * fresh
            for copy in stores[s]:
                copy.start()
        for pair in stores:
            for copy in pair:
                copy.wait()

    anywhere = pl.BlockSpec(memory_space=pl.ANY)
    extra = [] if previous is None else list(previous)
    return pl.pallas_call(
        kernel,
        in_specs=[SCALARS, hbm, hbm] + [WHOLE] * (1 + planes) + [hbm] * len(extra) + [anywhere],
        out_specs=[hbm, hbm, WHOLE],
        out_shape=[pltpu.HBM(weight.shape, WIDE)] * 2 + [like((8, LANES), WIDE)],
        scratch_shapes=[
            pltpu.VMEM((n_images, units), LOW),
            pltpu.VMEM((columns, depth // 2, LANES), WIDE),
            pltpu.VMEM((steps, tall, units), WIDE),
            pltpu.VMEM((steps, tall, units), WIDE),
            pltpu.SemaphoreType.DMA((steps, 4)),
        ],
        input_output_aliases={} if previous is None else {4 + planes: 0, 5 + planes: 1},
        compiler_params=pltpu.CompilerParams(vmem_limit_bytes=12 << 20),
        cost_estimate=BRIEF,
    )(core, weight, moment, rows, *grads, *extra, gate)


def order_towers(own, other, core):
    def kernel(core_ref, own_ref, other_ref, out_ref):
        out_ref[core_ref[0]] = own_ref[...]
        out_ref[1 - core_ref[0]] = other_ref[...]

    return pl.pallas_call(
        kernel,
        in_specs=[SCALARS, WHOLE, WHOLE],
        out_specs=WHOLE,
        out_shape=like((2, *own.shape), own.dtype),
        compiler_params=pltpu.CompilerParams(vmem_limit_bytes=8 << 20),
        cost_estimate=BRIEF,
    )(core, own, other)


def small_update(gate, ready, pieces, lines, params, moments, core, plane):
    planes = len(pieces)
    height, width_in = pieces[0].shape
    shard = params[1].shape[-1]
    units = params[3].shape[-1]
    count = lines - EXTRA
    rates = (LEARN_RATE, BIAS_RATE, STITCH_RATE, STITCH_RATE)

    def kernel(core_ref, plane_ref, gate_ref, ready_ref, *refs):
        piece_refs = refs[:planes]
        p_refs, m_refs = refs[planes : planes + 4], refs[planes + 4 : planes + 8]
        new_p, new_m = refs[planes + 8 : planes + 12], refs[planes + 12 : planes + 16]
        whole = refs[planes + 17]
        for k in range(planes):
            at = pl.ds(pl.multiple_of((plane_ref[0] ^ k) * height, height), height)
            whole[at, :] = piece_refs[k][...].astype(WIDE)

        def advance(which, at, grad):
            fresh = MOMENTUM * m_refs[which][at] + grad
            new_m[which][at] = fresh
            new_p[which][at] = p_refs[which][at] - rates[which] * fresh

        first = core_ref[0] == 0
        for a in range(2):
            advance(0, core_ref[0] ^ a, whole[a * lines : a * lines + count, :])
        rows = [[whole[a * lines + count + i : a * lines + count + i + 1, :shard] for i in range(3)] for a in range(2)]
        rows = [[jnp.where(first, rows[a][i], rows[1 - a][i]) for i in range(3)] for a in range(2)]
        for t in range(2):
            advance(1, (slice(t, t + 1), slice(None)), rows[t][0])
            advance(2, (t, slice(t, t + 1), slice(None)), rows[t][1])
            advance(2, (t, slice(1 - t, 2 - t), slice(None)), rows[t][2])
        base = 2 * lines
        parts, start = [], 0
        while start < units:
            step = min(width_in, units - start)
            parts.append(whole[base : base + 4, :step])
            base, start = base + 4, start + step
        packed = jnp.concatenate(parts, axis=1) if len(parts) > 1 else parts[0]
        for i in range(4):
            row = jnp.where(first, packed[i : i + 1, :], packed[3 - i : 4 - i, :])
            advance(3, (i // 2, slice(i % 2, i % 2 + 1), slice(None)), row)

    out_shape = [like(value.shape, WIDE) for value in (*params, *moments)]
    return pl.pallas_call(
        kernel,
        in_specs=[SCALARS] * 2
        + [pl.BlockSpec(memory_space=pl.ANY), pl.BlockSpec(memory_space=pltpu.HBM)]
        + [WHOLE] * (planes + 8),
        out_specs=[WHOLE] * 8 + [pl.BlockSpec(memory_space=pltpu.HBM)],
        out_shape=out_shape + [pltpu.HBM(ready.shape, ready.dtype)],
        input_output_aliases={3: 8},
        scratch_shapes=[pltpu.VMEM((planes * height, width_in), WIDE)],
        compiler_params=pltpu.CompilerParams(vmem_limit_bytes=12 << 20),
        cost_estimate=BRIEF,
    )(core, plane, gate, ready, *pieces, *params, *moments)


def reorder(parts, place):
    bit = 1
    while bit < len(parts):
        flip = (place & bit) != 0
        parts = [
            jax.tree.map(lambda a, b: jnp.where(flip, b, a), parts[j], parts[j ^ bit])
            for j in range(len(parts))
        ]
        bit *= 2
    return parts


def pick(stacked, place, count):
    return [lax.dynamic_index_in_dim(stacked, place ^ j, 0, keepdims=False) for j in range(count)]


def pool(values):
    rows = values[0:11:2] + values[1:12:2] + values[2:13:2]
    return (rows[:, 0:11:2] + rows[:, 1:12:2] + rows[:, 2:13:2]) * (1.0 / 9.0)


def spread(values, axis):
    values = jnp.moveaxis(values, axis, 0)
    zero = jnp.zeros_like(values[:1])
    even = jnp.concatenate([values, zero]) + jnp.concatenate([zero, values])
    inter = jnp.stack([even[:-1], values], axis=1).reshape((12,) + values.shape[1:])
    return jnp.moveaxis(jnp.concatenate([inter, even[-1:]]), 0, axis)


def any_mesh(
    images,
    conv_weight,
    conv_bias,
    stitch_conv,
    fc_weight,
    fc_bias,
    stitch_fc,
    conv_moment,
    bias_moment,
    stitch_conv_moment,
    fc_moment,
    fc_bias_moment,
    stitch_fc_moment,
    cotangent,
    task_mask,
):
    chan_size, planes = lax.axis_size("chan"), lax.axis_size("batch")
    chips = chan_size // 2
    me, plane = lax.axis_index("chan"), lax.axis_index("batch")
    core, chip = me % 2, me // 2
    swap = lambda value: trade(value, "chan", 1)
    mine = lambda a, b: jnp.where(core == 0, a, b)
    per_core, side, width_in = images.shape[0], images.shape[2], images.shape[-1]
    chan_width = conv_weight.shape[-1]
    full_chan = chan_width * chan_size
    units = fc_weight.shape[-1]
    rows = fc_weight.shape[1]
    cells = 36
    plane_chan = rows // cells
    group = 2 * per_core

    kernel_rows = jnp.transpose(conv_weight, (0, 1, 2, 4, 3)).astype(LOW)
    kernel_rows = kernel_rows.reshape(2, 9 * chan_width, width_in)
    cross = stitch_conv[:, ::-1]
    small = jnp.stack(
        [
            conv_bias,
            jnp.stack([stitch_conv[0, 0], stitch_conv[1, 1]]),
            jnp.stack([stitch_conv[0, 1], stitch_conv[1, 0]]),
            jnp.stack([stitch_conv[1, 0], stitch_conv[0, 1]]),
        ],
        axis=1,
    ).astype(LOW)
    small = jnp.pad(small, ((0, 0), (0, 12), (0, width_in - chan_width)))
    kernel_rows = jnp.concatenate([kernel_rows, small], axis=1)
    keep = mine(kernel_rows[0], kernel_rows[1])
    got = swap(mine(kernel_rows[1], kernel_rows[0]))
    halves = mine(keep, got), mine(got, keep)
    kernel_parts = gather_chips(halves[0], halves[1], chips)

    keep = mine(images[:, 0], images[:, 1])
    got = swap(mine(images[:, 1], images[:, 0]))
    tower_images = jnp.concatenate([mine(keep, got), mine(got, keep)], axis=0)
    tower_images = jnp.transpose(tower_images, (1, 2, 0, 3))

    fc_low = fc_weight.astype(LOW).reshape(2, plane_chan, cells, units)
    fc_low = jnp.swapaxes(fc_low, 1, 2).reshape(2, rows, units)
    fc_keep = mine(fc_low[0], fc_low[1])
    fc_got = swap(mine(fc_low[1], fc_low[0]))
    fc_halves = mine(fc_keep, fc_got), mine(fc_got, fc_keep)

    ordered = reorder(kernel_parts, chip)
    kernel = jnp.concatenate(
        [half[: 9 * chan_width].reshape(9, chan_width, width_in) for pair in ordered for half in pair],
        axis=1,
    )
    small_all = jnp.concatenate(
        [half[9 * chan_width :, :chan_width] for pair in ordered for half in pair], axis=1
    ).astype(WIDE)
    bias_all, self_mix, cross_mix, back_mix = (small_all[i] for i in range(4))

    conv_out = lax.conv_general_dilated(
        tower_images,
        kernel.reshape(3, 3, full_chan, width_in),
        (1, 1),
        "SAME",
        dimension_numbers=("HWNC", "HWOI", "HWNC"),
        preferred_element_type=WIDE,
    )
    act, slope = silu_and_slope(conv_out + bias_all)
    pooled = pool(act)
    pooled_other = swap(pooled)
    mixed = (self_mix * pooled + cross_mix * pooled_other).astype(LOW)
    mixed = mixed.reshape(cells, group, planes, plane_chan)
    pieces = jnp.transpose(mixed, (2, 1, 0, 3)).reshape(planes, group, rows)
    got = exchange_planes(pick(pieces, plane, planes))
    half = planes // 2
    gathered = reorder(
        gather_chips(jnp.stack(got[:half]), jnp.stack(got[half:]), chips), chip
    )
    tower_rows = jnp.concatenate(
        [jnp.stack([pair[h] for pair in gathered], axis=1) for h in range(2)], axis=0
    )
    tower_rows = tower_rows.reshape(planes * chips * group, rows)
    other_rows = swap(tower_rows)

    fc_tower = jnp.concatenate(fc_halves, axis=1)
    partial = jnp.dot(tower_rows, fc_tower, preferred_element_type=WIDE).astype(LOW)
    partial = partial.reshape(planes, chips * group, 2 * units)
    fc_sum = total(exchange_planes([partial[k] for k in range(planes)]))
    fc_keep = mine(fc_sum[:, :units], fc_sum[:, units:])
    fc_got = swap(mine(fc_sum[:, units:], fc_sum[:, :units]))
    fc_out = [mine(fc_keep, fc_got) + fc_bias[0], mine(fc_got, fc_keep) + fc_bias[1]]

    acts, slopes = zip(*[silu_and_slope(value) for value in fc_out])
    features_out = jnp.stack(
        [stitch_fc[t, 0] * acts[0] + stitch_fc[t, 1] * acts[1] for t in range(2)], axis=1
    ).astype(LOW)
    out_grad = [
        cotangent[:, t].astype(WIDE) * task_mask[:, t].astype(WIDE)[:, None] for t in range(2)
    ]
    stitch_fc_grad = jnp.stack(
        [jnp.stack([jnp.sum(out_grad[t] * acts[s], axis=0) for s in range(2)]) for t in range(2)]
    )
    grad_low = jnp.stack(
        [
            (slopes[s] * (stitch_fc[0, s] * out_grad[0] + stitch_fc[1, s] * out_grad[1])).astype(LOW)
            for s in range(2)
        ]
    )
    grad_all = exchange_planes([grad_low] * planes)
    grad_all = jnp.stack(grad_all, axis=1).reshape(2, planes * chips * group, units)
    grad_keep = mine(grad_all[0], grad_all[1])
    grad_got = swap(mine(grad_all[1], grad_all[0]))
    grad_tower = jnp.concatenate([mine(grad_keep, grad_got), mine(grad_got, grad_keep)], axis=1)

    flat_grad = lax.dot_general(
        grad_tower, fc_tower, (((1,), (1,)), ((), ())), preferred_element_type=WIDE
    ).astype(LOW)
    flat_grad = flat_grad.reshape(2, half, chips, group, rows)
    by_chip = reorder([(flat_grad[0, :, m], flat_grad[1, :, m]) for m in range(chips)], chip)
    first, second = scatter_chips(by_chip, chips)
    sums = jnp.concatenate([total(first), total(second)]).astype(LOW)
    got = reorder(exchange_planes([sums[k] for k in range(planes)]), plane)
    mixed_grad = jnp.stack(got)
    mixed_grad_other = swap(mixed_grad)

    def unflatten(value):
        value = value.astype(WIDE).reshape(planes, group, cells, plane_chan)
        return jnp.transpose(value, (2, 1, 0, 3)).reshape(6, 6, group, full_chan)

    own_grad, other_grad = unflatten(mixed_grad), unflatten(mixed_grad_other)
    self_stitch = jnp.sum(own_grad * pooled, axis=(0, 1, 2))
    cross_stitch = jnp.sum(own_grad * pooled_other, axis=(0, 1, 2))
    pooled_grad = (self_mix * own_grad + back_mix * other_grad) * (1.0 / 9.0)
    conv_grad = (slope * spread(spread(pooled_grad, 0), 1)).astype(LOW)
    bias_grad = jnp.sum(conv_grad.astype(WIDE), axis=(0, 1, 2))

    padded = jnp.pad(tower_images, ((1, 1), (1, 1), (0, 0), (0, 0)))
    taps = []
    for down in range(3):
        for right in range(3):
            window = padded[down : down + side, right : right + side]
            taps.append(
                lax.dot_general(
                    conv_grad.reshape(-1, full_chan),
                    window.reshape(-1, width_in),
                    (((0,), (0,)), ((), ())),
                    preferred_element_type=WIDE,
                ).astype(LOW)
            )
    kernel_grad = jnp.stack(taps).reshape(9, chips, 2, chan_width, width_in)
    smalls = jnp.stack([bias_grad, self_stitch, cross_stitch]).astype(LOW)
    smalls = jnp.pad(
        smalls.reshape(3, chips, 2, chan_width), ((0, 13), (0, 0), (0, 0), (0, width_in - chan_width))
    )
    blocks = [
        tuple(
            jnp.concatenate([kernel_grad[:, m, c].reshape(9 * chan_width, width_in), smalls[:, m, c]])
            for c in range(2)
        )
        for m in range(chips)
    ]
    first, second = scatter_chips(reorder(blocks, chip), chips)
    sums = [total(first).astype(LOW), total(second).astype(LOW)]
    keep = mine(sums[0], sums[1])
    got = swap(mine(sums[1], sums[0]))
    towers = jnp.stack([mine(keep, got), mine(got, keep)])
    towers = lax.psum(towers, "batch").astype(WIDE)
    stitch_fc_grad = lax.psum(stitch_fc_grad.astype(LOW), "batch").astype(WIDE)

    images_grad = lax.conv_general_dilated(
        conv_grad,
        kernel.reshape(3, 3, full_chan, width_in)[::-1, ::-1],
        (1, 1),
        "SAME",
        dimension_numbers=("HWNC", "HWIO", "HWNC"),
        preferred_element_type=WIDE,
    ).astype(LOW)
    images_grad = jnp.transpose(images_grad, (2, 0, 1, 3))
    keep = mine(images_grad[:per_core], images_grad[per_core:])
    got = swap(mine(images_grad[per_core:], images_grad[:per_core]))
    images_grad = jnp.stack([mine(keep, got), mine(got, keep)], axis=1)

    both_rows = [mine(tower_rows, other_rows), mine(other_rows, tower_rows)]
    fc_weight_grad = jnp.stack(
        [
            lax.dot_general(
                jnp.swapaxes(both_rows[t].reshape(-1, cells, plane_chan), 1, 2).reshape(-1, rows),
                grad_all[t],
                (((0,), (0,)), ((), ())),
                preferred_element_type=WIDE,
            )
            for t in range(2)
        ]
    )
    fc_bias_grad = jnp.sum(grad_all.astype(WIDE), axis=1)

    conv_weight_grad = jnp.swapaxes(
        towers[:, : 9 * chan_width].reshape(2, 3, 3, chan_width, width_in), 3, 4
    )
    conv_bias_grad = towers[:, 9 * chan_width, :chan_width]
    straight = towers[:, 9 * chan_width + 1, :chan_width]
    crossed = towers[:, 9 * chan_width + 2, :chan_width]
    stitch_conv_grad = jnp.stack(
        [jnp.stack([straight[0], crossed[0]]), jnp.stack([crossed[1], straight[1]])]
    )
    grads = (
        conv_weight_grad,
        conv_bias_grad,
        stitch_conv_grad,
        fc_weight_grad,
        fc_bias_grad,
        stitch_fc_grad,
    )
    params = (conv_weight, conv_bias, stitch_conv, fc_weight, fc_bias, stitch_fc)
    moments = (
        conv_moment,
        bias_moment,
        stitch_conv_moment,
        fc_moment,
        fc_bias_moment,
        stitch_fc_moment,
    )
    rates = (LEARN_RATE, BIAS_RATE, STITCH_RATE, LEARN_RATE, BIAS_RATE, STITCH_RATE)
    fresh = [MOMENTUM * moments[place] + grads[place] for place in range(6)]
    updated = [params[place] - rates[place] * fresh[place] for place in range(6)]
    return (features_out, images_grad, *updated, *fresh)


def four_by_four(
    images,
    conv_weight,
    conv_bias,
    stitch_conv,
    fc_weight,
    fc_bias,
    stitch_fc,
    conv_moment,
    bias_moment,
    stitch_conv_moment,
    fc_moment,
    fc_bias_moment,
    stitch_fc_moment,
    cotangent,
    task_mask,
):
    chips, planes = lax.axis_size("chan") // 2, lax.axis_size("batch")
    me, plane = lax.axis_index("chan"), lax.axis_index("batch")
    core, chip = me % 2, me // 2
    as_scalar = lambda value: value.reshape(1).astype(jnp.int32)
    core_at, chip_at, plane_at = as_scalar(core), as_scalar(chip), as_scalar(plane)
    swap = lambda value: trade(value, "chan", 1)
    per_core, side, width_in = images.shape[0], images.shape[2], images.shape[-1]
    shard = conv_weight.shape[-1]
    units = fc_weight.shape[-1]
    half = planes // 2

    as_rows = lambda value: jnp.transpose(value, (0, 1, 2, 4, 3)).reshape(2, TAPS * shard, width_in)
    keep, give = pack_kernels(as_rows(conv_weight), conv_bias, stitch_conv, core_at)
    starts = [(plane ^ k).astype(jnp.uint32) * jnp.uint32(PORTION) for k in range(planes)]
    keep, give, core_at, chip_at, plane_at, first_core, starts = tie(
        keep, give, core_at, chip_at, plane_at, core == 0, starts
    )
    mine = lambda a, b: jnp.where(first_core, a, b)
    keep_y, give_x = trade(keep, "chan", 4), trade(give, "chan", 3)
    keep_x, give_y = trade(keep, "chan", 2), trade(give, "chan", 5)
    keep_d, give_d = trade(keep_y, "chan", 2), trade(give_x, "chan", 4)
    kernel_parts = [keep, swap(give), keep_x, give_x, keep_y, give_y, keep_d, give_d]
    fc_own, fc_give = fc_prepare(fc_weight, core_at, kernel_parts[3])
    fc_cross = swap(fc_give)

    late_core, kernel_parts[3] = tie(first_core, kernel_parts[3])
    towers = lax.optimization_barrier(jnp.transpose(images, (1, 2, 3, 0, 4)))
    keep, give = (jnp.where(late_core, towers[a], towers[1 - a]) for a in range(2))
    tower_images = jnp.concatenate([keep, swap(give)], axis=2)
    tower_images = jnp.pad(tower_images, ((1, 1), (1, 1), (0, 0), (0, 0)))

    pooled, slope, small_all, joined = conv_forward(tower_images, kernel_parts, core_at, chip_at)
    pooled_other = swap(pooled)
    pieces = mix_pieces(pooled, pooled_other, small_all, core_at, plane_at, planes)
    got = exchange_planes(pieces)
    gathered = gather_chips(jnp.stack(got[:half]), jnp.stack(got[half:]), chips)
    tower_rows, *partial = fc_forward(
        [part for pair in gathered for part in pair], (fc_own, fc_cross), chip_at, chips, planes
    )
    other_rows = swap(tower_rows)

    fc_sum = total(exchange_planes(partial))
    fc_out = [fc_sum[:, :units], swap(fc_sum[:, units:])]
    fc_out = [fc_out[a] + mine(fc_bias[a], fc_bias[1 - a]) for a in range(2)]
    acts, slopes = zip(*[silu_and_slope(value) for value in fc_out])
    mix = [[mine(stitch_fc[a, b], stitch_fc[1 - a, 1 - b]) for b in range(2)] for a in range(2)]
    features = [mix[a][0] * acts[0] + mix[a][1] * acts[1] for a in range(2)]
    features_out = jnp.stack([mine(features[0], features[1]), mine(features[1], features[0])], axis=1)
    masked = [cotangent[:, t].astype(WIDE) * task_mask[:, t].astype(WIDE)[:, None] for t in range(2)]
    out_grad = [mine(masked[a], masked[1 - a]) for a in range(2)]
    grad_low = jnp.stack(
        [(slopes[b] * (mix[0][b] * out_grad[0] + mix[1][b] * out_grad[1])).astype(LOW) for b in range(2)]
    )
    stitch_fc_grad = jnp.concatenate(
        [jnp.sum(out_grad[a] * acts[b], axis=0, keepdims=True) for a in range(2) for b in range(2)]
    )
    packed = jnp.concatenate(
        [
            jnp.pad(stitch_fc_grad[:, at : at + width_in], ((0, 0), (0, max(0, at + width_in - units))))
            for at in range(0, units, width_in)
        ]
    ).astype(LOW)
    grads = exchange_planes([grad_low] * planes)
    grads[1], packed = tie(grads[1], packed)
    grads_cross = swap(jnp.stack([value[1] for value in grads]))

    step = done = None

    def update_own(gate, value):
        nonlocal step, done
        *step, done = fc_update(fc_weight, fc_moment, tower_rows, grads, core_at, 0, 0, None, gate)
        value, done = tie(value, done)
        return gate, value

    blocks = fc_backward(grads, grads_cross, (fc_own, fc_cross), chip_at, chips, planes)
    first, second = scatter_chips(
        [blocks[2 * j : 2 * j + 2] for j in range(chips)], chips, later=update_own
    )
    sums = [total([value[i] for value in part]).astype(LOW) for part in (first, second) for i in range(half)]
    mixed_grad = exchange_planes(sums)
    *step, token = fc_update(fc_weight, fc_moment, tower_rows, grads, core_at, 0, 1, step, sums[-1])
    mixed_grad[1], done, token = tie(mixed_grad[1], done, token)
    done = done + token
    mixed_grad_other = swap(jnp.stack(mixed_grad))

    *blocks, conv_grad = conv_backward(
        done, mixed_grad, mixed_grad_other, pooled, pooled_other, slope, tower_images, small_all, core_at, chip_at, plane_at
    )

    def turned_conv(grad):
        return lax.conv_general_dilated(
            grad,
            kernel[::-1, ::-1],
            (1, 1),
            "SAME",
            dimension_numbers=("HWNC", "HWIO", "HWNC"),
            preferred_element_type=WIDE,
        ).astype(LOW)

    kernel = joined.reshape(3, 3, -1, width_in)
    images_grad = None

    def after_sums(gate, value):
        nonlocal images_grad
        gate, grad = tie(gate, conv_grad)
        value, images_grad = tie(value, turned_conv(grad))
        return gate, value

    first, second = scatter_chips(
        [blocks[2 * j : 2 * j + 2] for j in range(chips)],
        chips,
        later=after_sums,
    )
    towers = jnp.stack([total(first).astype(LOW), swap(total(second).astype(LOW))])
    lines = towers.shape[1]

    flat = jnp.concatenate([towers.reshape(-1, width_in), packed])
    assert flat.shape[0] <= planes * PORTION
    flat = jnp.pad(flat, ((0, planes * PORTION - flat.shape[0]), (0, 0)))
    nothing = jnp.uint32(0)
    quarters = [lax.dynamic_slice(flat, (start, nothing), (PORTION, width_in)) for start in starts]
    quarters = exchange_planes(quarters)
    *step, done = fc_update(fc_weight, fc_moment, other_rows, grads, core_at, 1, 0, step, quarters[0])
    quarters[1], done = tie(quarters[1], done)
    quarter = total(quarters).astype(LOW)
    quarters = exchange_planes([quarter] * planes)
    *step, done = fc_update(fc_weight, fc_moment, other_rows, grads, core_at, 1, 1, step, done)

    images_grad, quarters[0] = tie(images_grad, quarters[0])
    keep, got = images_grad[:, :, :per_core], swap(images_grad[:, :, per_core:])
    images_grad = order_towers(keep, got, core_at)
    images_grad = jnp.transpose(images_grad, (3, 1, 2, 0, 4))

    *new_small, images_grad = small_update(
        done,
        images_grad,
        quarters,
        lines,
        (as_rows(conv_weight), conv_bias, stitch_conv, stitch_fc),
        (as_rows(conv_moment), bias_moment, stitch_conv_moment, stitch_fc_moment),
        core_at,
        plane_at,
    )

    fc_bias_grad = sum(jnp.sum(value.astype(WIDE), axis=1) for value in grads)
    fc_bias_grad = jnp.stack([mine(fc_bias_grad[a], fc_bias_grad[1 - a]) for a in range(2)])
    new_fc_bias_moment = MOMENTUM * fc_bias_moment + fc_bias_grad
    new_fc_bias = fc_bias - BIAS_RATE * new_fc_bias_moment

    as_given = lambda value: jnp.swapaxes(value.reshape(2, 3, 3, shard, width_in), 3, 4)
    params, fresh = new_small[:4], new_small[4:]
    params[0], fresh[0] = as_given(params[0]), as_given(fresh[0])
    params[3:3], fresh[3:3] = (step[0], new_fc_bias), (step[1], new_fc_bias_moment)
    images_grad = jnp.transpose(images_grad, (0, 3, 1, 2, 4))
    return (features_out.astype(LOW), images_grad, *params, *fresh)


def solution(mesh):
    chan_last = P(None, None, None, None, "chan")
    fc_spec = P(None, "batch", "chan")
    params = (chan_last, P(None, "chan"), P(None, None, "chan"), fc_spec, P(None, "chan"), P(None, None, "chan"))
    image_spec = P(("batch", "chan"), None, None, None, None)
    feature_spec = P("batch", None, "chan")
    in_specs = (image_spec, *params, *params, feature_spec, P("batch", None))
    out_specs = (feature_spec, image_spec, *params, *params)
    body = four_by_four if dict(mesh.shape) == {"chan": 8, "batch": 4} else any_mesh
    return jax.shard_map(body, mesh=mesh, in_specs=in_specs, out_specs=out_specs, check_vma=False)
```

```python
import functools

import jax
import jax.numpy as jnp
from jax import lax
from jax.experimental import pallas as pl
from jax.experimental.pallas import tpu as pltpu
from jax.sharding import PartitionSpec as P

MOMENTUM = 0.9
LEARN_RATE = 0.002
BIAS_RATE = 0.02
STITCH_RATE = 0.02
LOW = jnp.bfloat16
WIDE = jnp.float32
TAPS = 9
CELLS = 36
EXTRA = 16
PORTION = 80
LANES = 128
WHOLE = pl.BlockSpec(memory_space=pltpu.VMEM)
SCALARS = pl.BlockSpec(memory_space=pltpu.SMEM)
BRIEF = pl.CostEstimate(flops=0, bytes_accessed=0, transcendentals=0)
NN = (((1,), (0,)), ((), ()))
NT = (((1,), (1,)), ((), ()))
TN = (((0,), (0,)), ((), ()))


def like(shape, dtype):
    return jax.ShapeDtypeStruct(shape, dtype)


def dot(a, b, dims):
    return lax.dot_general(a, b, dims, preferred_element_type=WIDE)


def trade(value, axis, bit):
    size = lax.axis_size(axis)
    return lax.ppermute(value, axis, [(i, i ^ bit) for i in range(size)])


def tie(*values):
    return lax.optimization_barrier(values)


def gather_chips(first, second, chips):
    if chips == 4:
        first_y = trade(first, "chan", 4)
        second_x = trade(second, "chan", 2)
        first_x = trade(first, "chan", 2)
        second_y = trade(second, "chan", 4)
        first_d = trade(first_y, "chan", 2)
        second_d = trade(second_x, "chan", 4)
        return [(first, second), (first_x, second_x), (first_y, second_y), (first_d, second_d)]
    return [(first, second)] + [
        (trade(first, "chan", 2 * j), trade(second, "chan", 2 * j)) for j in range(1, chips)
    ]


def add_low(a, b):
    return (a.astype(WIDE) + b.astype(WIDE)).astype(LOW)


def scatter_chips(parts, chips, early=lambda *pair: pair, later=lambda gate, value: (gate, value)):
    if chips == 4:
        from_x = trade(parts[3][0], "chan", 2)
        from_y = trade(parts[3][1], "chan", 4)
        first_x = trade(parts[1][0], "chan", 2)
        second_y = trade(parts[2][1], "chan", 4)
        from_x, from_y = early(from_x, from_y)
        to_y = add_low(parts[2][0], from_x)
        first_y = trade(to_y, "chan", 4)
        to_x = add_low(parts[1][1], from_y)
        to_x, first_y = later(to_x, first_y)
        second_x = trade(to_x, "chan", 2)
        return (parts[0][0], first_x, first_y), (parts[0][1], second_x, second_y)
    got = [(trade(parts[j][0], "chan", 2 * j), trade(parts[j][1], "chan", 2 * j)) for j in range(1, chips)]
    return (
        (parts[0][0],) + tuple(pair[0] for pair in got),
        (parts[0][1],) + tuple(pair[1] for pair in got),
    )


def total(values):
    out = values[0].astype(WIDE)
    for value in values[1:]:
        out = out + value.astype(WIDE)
    return out


def exchange_planes(parts):
    got = {k: trade(parts[k], "batch", k) for k in range(len(parts) - 1, 0, -1)}
    return [parts[0]] + [got[k] for k in range(1, len(parts))]


def reduce_planes(first, second):
    passed = [trade(parts[3], "batch", 1) for parts in (first, second)]
    near = [trade(parts[1], "batch", 1) for parts in (first, second)]
    sent = [add_low(parts[2], term) for parts, term in zip((first, second), passed)]
    far = [trade(value, "batch", 2) for value in sent]
    return [[parts[0], a, b] for parts, a, b in zip((first, second), near, far)]


def spread_planes(first, second):
    far = [trade(value, "batch", 2) for value in (first, second)]
    near = [trade(value, "batch", 1) for value in (first, second)]
    passed = [trade(value, "batch", 1) for value in far]
    return [list(values) for values in zip((first, second), near, far, passed)]


def gate_of(value):
    return 1.0 / (1.0 + jnp.exp(-value))


def silu_and_slope(value):
    gate = gate_of(value)
    act = value * gate
    return act, gate + act * (1.0 - gate)


def lane_place(width):
    return lax.broadcasted_iota(jnp.int32, (1, LANES), 1) // width


def shift_slots(value, width, source, target):
    if source == target:
        return value
    return pltpu.roll(value, ((target - source) * width) % LANES, 1)


def pack_kernels(conv_weight, conv_bias, stitch_conv, core):
    _, lines, width_in = conv_weight.shape
    shard = conv_bias.shape[-1]

    def kernel(core_ref, w_hbm, bias_hbm, mix_hbm, keep_ref, give_ref, w_ref, bias_ref, mix_ref, sems):
        pairs = ((bias_hbm, bias_ref), (mix_hbm, mix_ref), (w_hbm, w_ref))
        copies = [pltpu.make_async_copy(source, held, sems.at[i]) for i, (source, held) in enumerate(pairs)]
        for copy in copies:
            copy.start()
        first = core_ref[0] == 0
        for copy in copies:
            copy.wait()
        for a, out in enumerate((keep_ref, give_ref)):
            out[:lines, :] = w_ref[core_ref[0] ^ a].astype(LOW)
            choose = lambda p, q: jnp.where(first, *((q, p) if a else (p, q)))
            rows = [
                choose(bias_ref[0:1, :], bias_ref[1:2, :]),
                choose(mix_ref[0, 0:1, :], mix_ref[1, 1:2, :]),
                choose(mix_ref[0, 1:2, :], mix_ref[1, 0:1, :]),
                choose(mix_ref[1, 0:1, :], mix_ref[0, 1:2, :]),
                jnp.zeros((EXTRA - 4, shard), WIDE),
            ]
            out[lines:, :] = jnp.zeros((EXTRA, width_in), LOW)
            out[lines:, :shard] = jnp.concatenate(rows, axis=0).astype(LOW)

    sources = (conv_weight, conv_bias, stitch_conv)
    return pl.pallas_call(
        kernel,
        in_specs=[SCALARS] + [pl.BlockSpec(memory_space=pltpu.HBM)] * 3,
        out_specs=[WHOLE] * 2,
        out_shape=[like((lines + EXTRA, width_in), LOW)] * 2,
        scratch_shapes=[pltpu.VMEM(value.shape, WIDE) for value in sources] + [pltpu.SemaphoreType.DMA((3,))],
        compiler_params=pltpu.CompilerParams(vmem_limit_bytes=8 << 20),
        cost_estimate=BRIEF,
    )(core, *(pltpu.with_memory_space_constraint(value, pltpu.HBM) for value in sources))


def fc_prepare(fc_weight, core, gate):
    _, rows, units = fc_weight.shape
    width = rows // CELLS
    fc_weight = pltpu.with_memory_space_constraint(fc_weight, pltpu.HBM)

    def kernel(core_ref, own_ref, other_ref, _, keep_ref, give_ref):
        for source, out in ((own_ref, keep_ref), (other_ref, give_ref)):
            for cell in range(CELLS):
                out[pl.ds(cell * width, width), :] = source[
                    0, pl.ds(cell, width, stride=CELLS), :
                ].astype(LOW)

    return pl.pallas_call(
        kernel,
        grid_spec=pltpu.PrefetchScalarGridSpec(
            num_scalar_prefetch=1,
            grid=(units // LANES,),
            in_specs=[
                pl.BlockSpec((1, rows, LANES), lambda j, core: (core[0], 0, j)),
                pl.BlockSpec((1, rows, LANES), lambda j, core: (core[0] ^ 1, 0, j)),
                pl.BlockSpec(memory_space=pl.ANY),
            ],
            out_specs=[pl.BlockSpec((rows, LANES), lambda j, core: (0, j))] * 2,
        ),
        out_shape=[like((rows, units), LOW)] * 2,
        compiler_params=pltpu.CompilerParams(vmem_limit_bytes=12 << 20),
        cost_estimate=pl.CostEstimate(flops=0, bytes_accessed=6 * fc_weight.size, transcendentals=0),
    )(core, fc_weight, fc_weight, gate)


def conv_forward(images, parts, core, chip):
    high, wide, group, width_in = images.shape
    side = high - 2
    count = len(parts)
    shard = (parts[0].shape[0] - EXTRA) // TAPS
    full = shard * count
    slots = LANES // shard

    def kernel(core_ref, chip_ref, x_ref, *refs):
        pieces = refs[:count]
        pooled_ref, slope_out, small_ref, weights_out = refs[count : count + 4]
        weights, acc, slope_ref, sems = refs[count + 4 :]
        copies = [pltpu.make_async_copy(slope_ref.at[h], slope_out.at[h], sems.at[h]) for h in range(side)]
        copies += [
            pltpu.make_async_copy(
                weights.at[:, pl.ds(tap * width_in, width_in)], weights_out.at[tap], sems.at[side + tap]
            )
            for tap in range(TAPS)
        ]
        lane = lax.broadcasted_iota(jnp.int32, (EXTRA, LANES), 1) // shard
        smalls = [jnp.zeros((EXTRA, LANES), WIDE) for _ in range(full // LANES)]
        for j in range(count // 2):
            for r in range(2):
                piece = pieces[2 * j + r]
                where = (chip_ref[0] ^ j) * 2 + (core_ref[0] ^ r)
                at = pl.ds(pl.multiple_of(where * shard, shard), shard)
                for tap in range(TAPS):
                    weights[at, tap * width_in : (tap + 1) * width_in] = piece[tap * shard : (tap + 1) * shard, :]
                row = piece[TAPS * shard :, :LANES].astype(WIDE)
                spread = row
                for s in range(1, slots):
                    spread = spread + pltpu.roll(row, s * shard, 1)
                for v in range(len(smalls)):
                    smalls[v] = jnp.where(lane + v * slots == where, spread, smalls[v])
        for v, value in enumerate(smalls):
            small_ref[:, v * LANES : (v + 1) * LANES] = value
        for copy in copies[side:]:
            copy.start()
        line = side * group
        bias = small_ref[0:1, :]
        for low, high_row in ((0, (side + 1) // 2), ((side + 1) // 2, side)):
            tall = high_row - low
            windows = [
                x_ref[tap // 3 + low : tap // 3 + high_row, tap % 3 : tap % 3 + side].reshape(tall * line, width_in)
                for tap in range(TAPS)
            ]
            acc[low * line : high_row * line, :] = dot(jnp.concatenate(windows, axis=1), weights[...], NT)
        for h in range(side):
            value, slope = silu_and_slope(acc[h * line : (h + 1) * line, :] + bias)
            slope_ref[h] = slope.reshape(side, group, full).astype(LOW)
            acc[h * line : (h + 1) * line, :] = value
            copies[h].start()
        cell = lambda h, w: acc[(h * side + w) * group : (h * side + w + 1) * group, :]
        for r in range(6):
            rows = [cell(2 * r, w) + cell(2 * r + 1, w) + cell(2 * r + 2, w) for w in range(side)]
            for c in range(6):
                pooled_ref[6 * r + c] = (rows[2 * c] + rows[2 * c + 1] + rows[2 * c + 2]) * (1.0 / 9.0)
        for copy in copies:
            copy.wait()

    area = side * side * group
    return pl.pallas_call(
        kernel,
        in_specs=[SCALARS] * 2 + [WHOLE] * (1 + count),
        out_specs=[WHOLE, pl.BlockSpec(memory_space=pltpu.HBM), WHOLE, pl.BlockSpec(memory_space=pltpu.HBM)],
        out_shape=[
            like((CELLS, group, full), WIDE),
            pltpu.HBM((side, side, group, full), LOW),
            like((EXTRA, full), WIDE),
            pltpu.HBM((TAPS, full, width_in), LOW),
        ],
        scratch_shapes=[
            pltpu.VMEM((full, TAPS * width_in), LOW),
            pltpu.VMEM((area, full), WIDE),
            pltpu.VMEM((side, side, group, full), LOW),
            pltpu.SemaphoreType.DMA((side + TAPS,)),
        ],
        compiler_params=pltpu.CompilerParams(vmem_limit_bytes=16 << 20),
        cost_estimate=BRIEF,
    )(core, chip, images, *parts)


def turn(value):
    half = value.shape[0] // 2
    return jnp.concatenate([value[half:], value[:half]], axis=0)


def mix_pieces(pooled, other, small, core, plane, planes):
    cells, group, full = pooled.shape
    width = full // planes
    per = LANES // width

    def kernel(core_ref, plane_ref, a_ref, b_ref, small_ref, *refs):
        outs, held = refs[:planes], refs[planes]
        first = core_ref[0] == 0
        place = lane_place(width)
        one, two = small_ref[1:2, :], small_ref[2:3, :]
        for start in range(0, cells, per):
            mixed = [
                one * a_ref[start + i] + two * turn(b_ref[start + i]) for i in range(per)
            ]
            mixed = [jnp.where(first, value, turn(value)) for value in mixed]
            for p in range(planes):
                column, source = divmod(p * width, LANES)
                out = None
                for i in range(per):
                    moved = shift_slots(
                        mixed[i][:, column * LANES : (column + 1) * LANES], width, source // width, i
                    )
                    out = moved if out is None else jnp.where(place == i, moved, out)
                held[p, :, start * width : (start + per) * width] = out.astype(LOW)
        for k in range(planes):
            outs[k][...] = held[plane_ref[0] ^ k]

    rows = cells * width
    return pl.pallas_call(
        kernel,
        in_specs=[SCALARS] * 2 + [WHOLE] * 3,
        out_specs=[WHOLE] * planes,
        out_shape=[like((group, rows), LOW)] * planes,
        scratch_shapes=[pltpu.VMEM((planes, group, rows), LOW)],
        compiler_params=pltpu.CompilerParams(vmem_limit_bytes=8 << 20),
        cost_estimate=BRIEF,
    )(core, plane, pooled, other, small)


def fc_forward(gathered, weights, chip, chips, planes):
    half, group, rows = gathered[0].shape
    units = weights[0].shape[-1]
    count = 2 * chips
    block = chips * group

    def kernel(chip_ref, *refs):
        pieces, (own, cross) = refs[:count], refs[count : count + 2]
        rows_ref, outs = refs[count + 2], refs[count + 3 :]
        for j in range(chips):
            for h in range(2):
                for i in range(half):
                    start = ((h * half + i) * chips + (chip_ref[0] ^ j)) * group
                    rows_ref[pl.ds(pl.multiple_of(start, group), group), :] = pieces[2 * j + h][i]
        for n, weight in enumerate((own, cross)):
            part = dot(rows_ref[...], weight[...], NN)
            for k in range(planes):
                out = outs[n * planes + k]
                out[...] = part[k * block : (k + 1) * block].astype(out.dtype)

    n_images = planes * block
    return pl.pallas_call(
        kernel,
        in_specs=[SCALARS] + [WHOLE] * (count + 2),
        out_specs=[WHOLE] * (1 + 2 * planes),
        out_shape=[like((n_images, rows), LOW)]
        + [like((block, units), LOW if k else WIDE) for k in range(planes)] * 2,
        compiler_params=pltpu.CompilerParams(vmem_limit_bytes=16 << 20),
        cost_estimate=BRIEF,
    )(chip, *gathered, *weights)


def fc_backward(grads, crossed, weights, chip, chips, planes):
    block, units = grads[0].shape
    rows = weights[0].shape[0]
    group = block // chips
    half = planes // 2
    n_images = planes * block

    def kernel(chip_ref, *refs):
        pieces, got = refs[:planes], refs[planes]
        own, cross = refs[planes + 1 : planes + 3]
        outs = refs[planes + 3 : planes + 3 + 2 * chips]
        held_own, held_cross, held = refs[planes + 3 + 2 * chips :]
        for k in range(planes):
            held_own[pl.ds(k * block, block), :] = pieces[k][...]
            held_cross[pl.ds(k * block, block), :] = got[k]
        step = rows // 3
        for s in range(3):
            at = pl.ds(s * step, step)
            value = dot(held_own[...], own[at, :], NT) + dot(held_cross[...], cross[at, :], NT)
            held[:, at] = value.astype(LOW)
        for j in range(chips):
            for h in range(2):
                for i in range(half):
                    start = ((h * half + i) * chips + (chip_ref[0] ^ j)) * group
                    outs[2 * j + h][i] = held[pl.ds(pl.multiple_of(start, group), group), :]

    return pl.pallas_call(
        kernel,
        in_specs=[SCALARS] + [WHOLE] * (planes + 3),
        out_specs=[WHOLE] * (2 * chips),
        out_shape=[like((half, group, rows), LOW)] * (2 * chips),
        scratch_shapes=[
            pltpu.VMEM((n_images, units), LOW),
            pltpu.VMEM((n_images, units), LOW),
            pltpu.VMEM((n_images, rows), LOW),
        ],
        compiler_params=pltpu.CompilerParams(vmem_limit_bytes=20 << 20),
        cost_estimate=BRIEF,
    )(chip, *grads, crossed, *weights)


def conv_backward(gate, own, other, pooled, pooled_other, slope, images, small, core, chip, plane):
    planes = len(own)
    cells, group, full = pooled.shape
    high, _, _, width_in = images.shape
    side = high - 2
    width = full // planes
    per = LANES // width
    columns = full // LANES
    shards = lax.axis_size("chan")
    shard = full // shards
    slots = LANES // shard
    area = side * side * group

    def covering(h):
        return [r for r in range(6) if 2 * r <= h <= 2 * r + 2]

    def kernel(core_ref, chip_ref, plane_ref, gate_ref, *refs):
        own_refs, other_ref = refs[:planes], refs[planes]
        a_ref, b_ref, slope_ref, x_ref, small_ref = refs[planes + 1 : planes + 6]
        outs = refs[planes + 6 : planes + 6 + shards]
        grad_out = refs[planes + 6 + shards]
        flat, pool_grad, turned, taps, smalls, grad_ref, sem = refs[planes + 7 + shards :]
        copy = pltpu.make_async_copy(grad_ref, grad_out, sem)
        place = lane_place(width)
        first = core_ref[0] == 0
        for k in range(planes):
            for t, value in enumerate((own_refs[k][...], other_ref[k])):
                value = value.astype(WIDE)
                flat[t, plane_ref[0] ^ k] = jnp.where(first, value, turn(value))
        one, back = small_ref[1:2, :] * (1.0 / 9.0), small_ref[3:4, :] * (1.0 / 9.0)
        sum_one = jnp.zeros((group, full), WIDE)
        sum_two = jnp.zeros((group, full), WIDE)
        for cell in range(cells):
            column, source = divmod(cell * width, LANES)
            both = []
            for t in range(2):
                blocks = []
                for v in range(columns):
                    out = None
                    for i in range(per):
                        piece = flat[t, v * per + i, :, column * LANES : (column + 1) * LANES]
                        moved = shift_slots(piece, width, source // width, i)
                        out = moved if out is None else jnp.where(place == i, moved, out)
                    blocks.append(out)
                both.append(jnp.concatenate(blocks, axis=1))
            sum_one += both[0] * a_ref[cell]
            sum_two += both[0] * turn(b_ref[cell])
            pool_grad[cell] = one * both[0] + back * both[1]
        sum_bias = jnp.zeros((group, full), WIDE)
        for h in range(side):
            line = [sum(pool_grad[6 * r + c] for r in covering(h)) for c in range(6)]
            for w in range(side):
                value = sum(line[c] for c in covering(w))
                value = (value * slope_ref[h, w].astype(WIDE)).astype(LOW)
                grad_ref[h, w] = value
                sum_bias += value.astype(WIDE)
        copy.start()
        turned[...] = grad_ref[...].reshape(area, full).T
        for start in range(0, TAPS, 2):
            some = range(start, min(start + 2, TAPS))
            windows = [
                x_ref[tap // 3 : tap // 3 + side, tap % 3 : tap % 3 + side].reshape(area, width_in) for tap in some
            ]
            part = dot(turned[...], jnp.concatenate(windows, axis=1), NN)
            for n, tap in enumerate(some):
                taps[tap] = part[:, n * width_in : (n + 1) * width_in].astype(LOW)
        sums = [jnp.sum(value, axis=0, keepdims=True) for value in (sum_bias, sum_one, sum_two)]
        sums = jnp.concatenate(sums + [jnp.zeros((EXTRA - 3, full), WIDE)], axis=0)
        for v in range(columns):
            smalls[v] = sums[:, v * LANES : (v + 1) * LANES]
        lane = lax.broadcasted_iota(jnp.int32, (EXTRA, LANES), 1)
        for j in range(shards // 2):
            for r in range(2):
                where = (chip_ref[0] ^ j) * 2 + (core_ref[0] ^ r)
                at = pl.ds(pl.multiple_of(where * shard, shard), shard)
                out = outs[2 * j + r]
                for tap in range(TAPS):
                    out[tap * shard : (tap + 1) * shard, :] = taps[tap, at, :]
                row = smalls[where // slots]
                value = jnp.zeros((EXTRA, LANES), WIDE)
                for s in range(slots):
                    moved = row if s == 0 else pltpu.roll(row, LANES - s * shard, 1)
                    value = jnp.where(where % slots == s, moved, value)
                out[TAPS * shard :, :] = jnp.zeros((EXTRA, width_in), LOW)
                out[TAPS * shard :, :LANES] = jnp.where(lane < shard, value, 0.0).astype(LOW)
        copy.wait()

    return pl.pallas_call(
        kernel,
        in_specs=[SCALARS] * 3 + [pl.BlockSpec(memory_space=pl.ANY)] + [WHOLE] * (planes + 6),
        out_specs=[WHOLE] * shards + [pl.BlockSpec(memory_space=pltpu.HBM)],
        out_shape=[like((TAPS * shard + EXTRA, width_in), LOW)] * shards
        + [pltpu.HBM((side, side, group, full), LOW)],
        scratch_shapes=[
            pltpu.VMEM((2, planes, group, cells * width), WIDE),
            pltpu.VMEM((cells, group, full), WIDE),
            pltpu.VMEM((full, area), LOW),
            pltpu.VMEM((TAPS, full, width_in), LOW),
            pltpu.VMEM((columns, EXTRA, LANES), WIDE),
            pltpu.VMEM((side, side, group, full), LOW),
            pltpu.SemaphoreType.DMA(()),
        ],
        compiler_params=pltpu.CompilerParams(vmem_limit_bytes=14 << 20),
        cost_estimate=BRIEF,
    )(core, chip, plane, gate, *own, other, pooled, pooled_other, slope, images, small)


def fc_update(weight, moment, rows, grads, core, which, part, previous, gate):
    _, depth, units = weight.shape
    width = depth // CELLS
    n_images = rows.shape[0]
    planes = len(grads)
    block = n_images // planes
    columns = units // LANES
    steps = 4
    few = width // 2
    tall = depth // 2 // steps
    hbm = pl.BlockSpec(memory_space=pltpu.HBM)

    def kernel(core_ref, w_ref, m_ref, rows_ref, *refs):
        grad_refs = refs[:planes]
        new_w, new_m, token, joined, product, held_w, held_m, sems = refs[-8:]
        tower = core_ref[0] ^ which
        token[...] = jnp.zeros_like(token)
        for k in range(planes):
            joined[pl.ds(k * block, block), :] = grad_refs[k][...]
        for v in range(columns):
            grad = dot(rows_ref[...], joined[:, v * LANES : (v + 1) * LANES], TN)
            for cell in range(CELLS):
                start = cell * width + part * few
                product[v, pl.ds(cell, few, stride=CELLS), :] = grad[start : start + few]
        stores = []
        for s in range(steps):
            at = pl.ds((part * steps + s) * tall, tall)
            for v in range(columns):
                lanes = slice(v * LANES, (v + 1) * LANES)
                fresh = MOMENTUM * m_ref[tower, at, lanes] + product[v, s * tall : (s + 1) * tall, :]
                held_m[s, :, lanes] = fresh
                held_w[s, :, lanes] = w_ref[tower, at, lanes] - LEARN_RATE * fresh
            for i, (held, out) in enumerate(((held_w, new_w), (held_m, new_m))):
                stores.append(pltpu.make_async_copy(held.at[s], out.at[tower, at, :], sems.at[s, i]))
                stores[-1].start()
        for copy in stores:
            copy.wait()

    anywhere = pl.BlockSpec(memory_space=pl.ANY)
    extra = [] if previous is None else list(previous)
    return pl.pallas_call(
        kernel,
        in_specs=[SCALARS] + [WHOLE] * (3 + planes) + [hbm] * len(extra) + [anywhere],
        out_specs=[hbm, hbm, WHOLE],
        out_shape=[pltpu.HBM(weight.shape, WIDE)] * 2 + [like((8, LANES), WIDE)],
        scratch_shapes=[
            pltpu.VMEM((n_images, units), LOW),
            pltpu.VMEM((columns, depth // 2, LANES), WIDE),
            pltpu.VMEM((steps, tall, units), WIDE),
            pltpu.VMEM((steps, tall, units), WIDE),
            pltpu.SemaphoreType.DMA((steps, 2)),
        ],
        input_output_aliases={} if previous is None else {4 + planes: 0, 5 + planes: 1},
        compiler_params=pltpu.CompilerParams(vmem_limit_bytes=12 << 20),
        cost_estimate=pl.CostEstimate(flops=0, bytes_accessed=8 * depth * units, transcendentals=0),
    )(core, weight, moment, rows, *grads, *extra, gate)


def order_towers(own, other, core):
    def kernel(core_ref, own_ref, other_ref, out_ref):
        out_ref[core_ref[0]] = own_ref[...]
        out_ref[1 - core_ref[0]] = other_ref[...]

    return pl.pallas_call(
        kernel,
        in_specs=[SCALARS, WHOLE, WHOLE],
        out_specs=WHOLE,
        out_shape=like((2, *own.shape), own.dtype),
        compiler_params=pltpu.CompilerParams(vmem_limit_bytes=8 << 20),
        cost_estimate=BRIEF,
    )(core, own, other)


def small_update(gate, ready, pieces, lines, params, moments, core, plane):
    planes = len(pieces)
    height, width_in = pieces[0].shape
    height = height // 2
    shard = params[1].shape[-1]
    units = params[3].shape[-1]
    count = lines - EXTRA
    rates = (LEARN_RATE, BIAS_RATE, STITCH_RATE, STITCH_RATE)

    def kernel(core_ref, plane_ref, gate_ref, ready_ref, *refs):
        piece_refs, refs = refs[:planes], refs[planes:]
        p_refs, m_refs, new_p, new_m, whole = refs[:4], refs[4:8], refs[8:12], refs[12:16], refs[17]
        for a in range(2):
            for k in range(planes):
                at = pl.ds(pl.multiple_of((plane_ref[0] ^ k) * height, height), height)
                whole[a, at, :] = piece_refs[k][a * height : (a + 1) * height, :].astype(WIDE)

        def advance(which, at, grad):
            fresh = MOMENTUM * m_refs[which][at] + grad
            new_m[which][at] = fresh
            new_p[which][at] = p_refs[which][at] - rates[which] * fresh

        first = core_ref[0] == 0
        for a in range(2):
            advance(0, core_ref[0] ^ a, whole[a, :count, :])
        rows = [[whole[a, count + i : count + i + 1, :shard] for i in range(3)] for a in range(2)]
        rows = [[jnp.where(first, rows[a][i], rows[1 - a][i]) for i in range(3)] for a in range(2)]
        for t in range(2):
            advance(1, (slice(t, t + 1), slice(None)), rows[t][0])
            advance(2, (t, slice(t, t + 1), slice(None)), rows[t][1])
            advance(2, (t, slice(1 - t, 2 - t), slice(None)), rows[t][2])
        base = lines
        parts, start = [], 0
        while start < units:
            step = min(width_in, units - start)
            parts.append(whole[0, base : base + 4, :step])
            base, start = base + 4, start + step
        packed = jnp.concatenate(parts, axis=1) if len(parts) > 1 else parts[0]
        for i in range(4):
            row = jnp.where(first, packed[i : i + 1, :], packed[3 - i : 4 - i, :])
            advance(3, (i // 2, slice(i % 2, i % 2 + 1), slice(None)), row)

    out_shape = [like(value.shape, WIDE) for value in (*params, *moments)]
    return pl.pallas_call(
        kernel,
        in_specs=[SCALARS] * 2
        + [pl.BlockSpec(memory_space=pl.ANY), pl.BlockSpec(memory_space=pltpu.HBM)]
        + [WHOLE] * (planes + 8),
        out_specs=[WHOLE] * 8 + [pl.BlockSpec(memory_space=pltpu.HBM)],
        out_shape=out_shape + [pltpu.HBM(ready.shape, ready.dtype)],
        input_output_aliases={3: 8},
        scratch_shapes=[pltpu.VMEM((2, planes * height, width_in), WIDE)],
        compiler_params=pltpu.CompilerParams(vmem_limit_bytes=12 << 20),
        cost_estimate=BRIEF,
    )(core, plane, gate, ready, *pieces, *params, *moments)


def reorder(parts, place):
    bit = 1
    while bit < len(parts):
        flip = (place & bit) != 0
        parts = [
            jax.tree.map(lambda a, b: jnp.where(flip, b, a), parts[j], parts[j ^ bit])
            for j in range(len(parts))
        ]
        bit *= 2
    return parts


def pick(stacked, place, count):
    return [lax.dynamic_index_in_dim(stacked, place ^ j, 0, keepdims=False) for j in range(count)]


def pool(values):
    rows = values[0:11:2] + values[1:12:2] + values[2:13:2]
    return (rows[:, 0:11:2] + rows[:, 1:12:2] + rows[:, 2:13:2]) * (1.0 / 9.0)


def spread(values, axis):
    values = jnp.moveaxis(values, axis, 0)
    zero = jnp.zeros_like(values[:1])
    even = jnp.concatenate([values, zero]) + jnp.concatenate([zero, values])
    inter = jnp.stack([even[:-1], values], axis=1).reshape((12,) + values.shape[1:])
    return jnp.moveaxis(jnp.concatenate([inter, even[-1:]]), 0, axis)


def any_mesh(
    images,
    conv_weight,
    conv_bias,
    stitch_conv,
    fc_weight,
    fc_bias,
    stitch_fc,
    conv_moment,
    bias_moment,
    stitch_conv_moment,
    fc_moment,
    fc_bias_moment,
    stitch_fc_moment,
    cotangent,
    task_mask,
):
    chan_size, planes = lax.axis_size("chan"), lax.axis_size("batch")
    chips = chan_size // 2
    me, plane = lax.axis_index("chan"), lax.axis_index("batch")
    core, chip = me % 2, me // 2
    swap = lambda value: trade(value, "chan", 1)
    mine = lambda a, b: jnp.where(core == 0, a, b)
    per_core, side, width_in = images.shape[0], images.shape[2], images.shape[-1]
    chan_width = conv_weight.shape[-1]
    full_chan = chan_width * chan_size
    units = fc_weight.shape[-1]
    rows = fc_weight.shape[1]
    cells = 36
    plane_chan = rows // cells
    group = 2 * per_core

    kernel_rows = jnp.transpose(conv_weight, (0, 1, 2, 4, 3)).astype(LOW)
    kernel_rows = kernel_rows.reshape(2, 9 * chan_width, width_in)
    cross = stitch_conv[:, ::-1]
    small = jnp.stack(
        [
            conv_bias,
            jnp.stack([stitch_conv[0, 0], stitch_conv[1, 1]]),
            jnp.stack([stitch_conv[0, 1], stitch_conv[1, 0]]),
            jnp.stack([stitch_conv[1, 0], stitch_conv[0, 1]]),
        ],
        axis=1,
    ).astype(LOW)
    small = jnp.pad(small, ((0, 0), (0, 12), (0, width_in - chan_width)))
    kernel_rows = jnp.concatenate([kernel_rows, small], axis=1)
    keep = mine(kernel_rows[0], kernel_rows[1])
    got = swap(mine(kernel_rows[1], kernel_rows[0]))
    halves = mine(keep, got), mine(got, keep)
    kernel_parts = gather_chips(halves[0], halves[1], chips)

    keep = mine(images[:, 0], images[:, 1])
    got = swap(mine(images[:, 1], images[:, 0]))
    tower_images = jnp.concatenate([mine(keep, got), mine(got, keep)], axis=0)
    tower_images = jnp.transpose(tower_images, (1, 2, 0, 3))

    fc_low = fc_weight.astype(LOW).reshape(2, plane_chan, cells, units)
    fc_low = jnp.swapaxes(fc_low, 1, 2).reshape(2, rows, units)
    fc_keep = mine(fc_low[0], fc_low[1])
    fc_got = swap(mine(fc_low[1], fc_low[0]))
    fc_halves = mine(fc_keep, fc_got), mine(fc_got, fc_keep)

    ordered = reorder(kernel_parts, chip)
    kernel = jnp.concatenate(
        [half[: 9 * chan_width].reshape(9, chan_width, width_in) for pair in ordered for half in pair],
        axis=1,
    )
    small_all = jnp.concatenate(
        [half[9 * chan_width :, :chan_width] for pair in ordered for half in pair], axis=1
    ).astype(WIDE)
    bias_all, self_mix, cross_mix, back_mix = (small_all[i] for i in range(4))

    conv_out = lax.conv_general_dilated(
        tower_images,
        kernel.reshape(3, 3, full_chan, width_in),
        (1, 1),
        "SAME",
        dimension_numbers=("HWNC", "HWOI", "HWNC"),
        preferred_element_type=WIDE,
    )
    act, slope = silu_and_slope(conv_out + bias_all)
    pooled = pool(act)
    pooled_other = swap(pooled)
    mixed = (self_mix * pooled + cross_mix * pooled_other).astype(LOW)
    mixed = mixed.reshape(cells, group, planes, plane_chan)
    pieces = jnp.transpose(mixed, (2, 1, 0, 3)).reshape(planes, group, rows)
    got = exchange_planes(pick(pieces, plane, planes))
    half = planes // 2
    gathered = reorder(
        gather_chips(jnp.stack(got[:half]), jnp.stack(got[half:]), chips), chip
    )
    tower_rows = jnp.concatenate(
        [jnp.stack([pair[h] for pair in gathered], axis=1) for h in range(2)], axis=0
    )
    tower_rows = tower_rows.reshape(planes * chips * group, rows)
    other_rows = swap(tower_rows)

    fc_tower = jnp.concatenate(fc_halves, axis=1)
    partial = jnp.dot(tower_rows, fc_tower, preferred_element_type=WIDE).astype(LOW)
    partial = partial.reshape(planes, chips * group, 2 * units)
    fc_sum = total(exchange_planes([partial[k] for k in range(planes)]))
    fc_keep = mine(fc_sum[:, :units], fc_sum[:, units:])
    fc_got = swap(mine(fc_sum[:, units:], fc_sum[:, :units]))
    fc_out = [mine(fc_keep, fc_got) + fc_bias[0], mine(fc_got, fc_keep) + fc_bias[1]]

    acts, slopes = zip(*[silu_and_slope(value) for value in fc_out])
    features_out = jnp.stack(
        [stitch_fc[t, 0] * acts[0] + stitch_fc[t, 1] * acts[1] for t in range(2)], axis=1
    ).astype(LOW)
    out_grad = [
        cotangent[:, t].astype(WIDE) * task_mask[:, t].astype(WIDE)[:, None] for t in range(2)
    ]
    stitch_fc_grad = jnp.stack(
        [jnp.stack([jnp.sum(out_grad[t] * acts[s], axis=0) for s in range(2)]) for t in range(2)]
    )
    grad_low = jnp.stack(
        [
            (slopes[s] * (stitch_fc[0, s] * out_grad[0] + stitch_fc[1, s] * out_grad[1])).astype(LOW)
            for s in range(2)
        ]
    )
    grad_all = exchange_planes([grad_low] * planes)
    grad_all = jnp.stack(grad_all, axis=1).reshape(2, planes * chips * group, units)
    grad_keep = mine(grad_all[0], grad_all[1])
    grad_got = swap(mine(grad_all[1], grad_all[0]))
    grad_tower = jnp.concatenate([mine(grad_keep, grad_got), mine(grad_got, grad_keep)], axis=1)

    flat_grad = lax.dot_general(
        grad_tower, fc_tower, (((1,), (1,)), ((), ())), preferred_element_type=WIDE
    ).astype(LOW)
    flat_grad = flat_grad.reshape(2, half, chips, group, rows)
    by_chip = reorder([(flat_grad[0, :, m], flat_grad[1, :, m]) for m in range(chips)], chip)
    first, second = scatter_chips(by_chip, chips)
    sums = jnp.concatenate([total(first), total(second)]).astype(LOW)
    got = reorder(exchange_planes([sums[k] for k in range(planes)]), plane)
    mixed_grad = jnp.stack(got)
    mixed_grad_other = swap(mixed_grad)

    def unflatten(value):
        value = value.astype(WIDE).reshape(planes, group, cells, plane_chan)
        return jnp.transpose(value, (2, 1, 0, 3)).reshape(6, 6, group, full_chan)

    own_grad, other_grad = unflatten(mixed_grad), unflatten(mixed_grad_other)
    self_stitch = jnp.sum(own_grad * pooled, axis=(0, 1, 2))
    cross_stitch = jnp.sum(own_grad * pooled_other, axis=(0, 1, 2))
    pooled_grad = (self_mix * own_grad + back_mix * other_grad) * (1.0 / 9.0)
    conv_grad = (slope * spread(spread(pooled_grad, 0), 1)).astype(LOW)
    bias_grad = jnp.sum(conv_grad.astype(WIDE), axis=(0, 1, 2))

    padded = jnp.pad(tower_images, ((1, 1), (1, 1), (0, 0), (0, 0)))
    taps = []
    for down in range(3):
        for right in range(3):
            window = padded[down : down + side, right : right + side]
            taps.append(
                lax.dot_general(
                    conv_grad.reshape(-1, full_chan),
                    window.reshape(-1, width_in),
                    (((0,), (0,)), ((), ())),
                    preferred_element_type=WIDE,
                ).astype(LOW)
            )
    kernel_grad = jnp.stack(taps).reshape(9, chips, 2, chan_width, width_in)
    smalls = jnp.stack([bias_grad, self_stitch, cross_stitch]).astype(LOW)
    smalls = jnp.pad(
        smalls.reshape(3, chips, 2, chan_width), ((0, 13), (0, 0), (0, 0), (0, width_in - chan_width))
    )
    blocks = [
        tuple(
            jnp.concatenate([kernel_grad[:, m, c].reshape(9 * chan_width, width_in), smalls[:, m, c]])
            for c in range(2)
        )
        for m in range(chips)
    ]
    first, second = scatter_chips(reorder(blocks, chip), chips)
    sums = [total(first).astype(LOW), total(second).astype(LOW)]
    keep = mine(sums[0], sums[1])
    got = swap(mine(sums[1], sums[0]))
    towers = jnp.stack([mine(keep, got), mine(got, keep)])
    towers = lax.psum(towers, "batch").astype(WIDE)
    stitch_fc_grad = lax.psum(stitch_fc_grad.astype(LOW), "batch").astype(WIDE)

    images_grad = lax.conv_general_dilated(
        conv_grad,
        kernel.reshape(3, 3, full_chan, width_in)[::-1, ::-1],
        (1, 1),
        "SAME",
        dimension_numbers=("HWNC", "HWIO", "HWNC"),
        preferred_element_type=WIDE,
    ).astype(LOW)
    images_grad = jnp.transpose(images_grad, (2, 0, 1, 3))
    keep = mine(images_grad[:per_core], images_grad[per_core:])
    got = swap(mine(images_grad[per_core:], images_grad[:per_core]))
    images_grad = jnp.stack([mine(keep, got), mine(got, keep)], axis=1)

    both_rows = [mine(tower_rows, other_rows), mine(other_rows, tower_rows)]
    fc_weight_grad = jnp.stack(
        [
            lax.dot_general(
                jnp.swapaxes(both_rows[t].reshape(-1, cells, plane_chan), 1, 2).reshape(-1, rows),
                grad_all[t],
                (((0,), (0,)), ((), ())),
                preferred_element_type=WIDE,
            )
            for t in range(2)
        ]
    )
    fc_bias_grad = jnp.sum(grad_all.astype(WIDE), axis=1)

    conv_weight_grad = jnp.swapaxes(
        towers[:, : 9 * chan_width].reshape(2, 3, 3, chan_width, width_in), 3, 4
    )
    conv_bias_grad = towers[:, 9 * chan_width, :chan_width]
    straight = towers[:, 9 * chan_width + 1, :chan_width]
    crossed = towers[:, 9 * chan_width + 2, :chan_width]
    stitch_conv_grad = jnp.stack(
        [jnp.stack([straight[0], crossed[0]]), jnp.stack([crossed[1], straight[1]])]
    )
    grads = (
        conv_weight_grad,
        conv_bias_grad,
        stitch_conv_grad,
        fc_weight_grad,
        fc_bias_grad,
        stitch_fc_grad,
    )
    params = (conv_weight, conv_bias, stitch_conv, fc_weight, fc_bias, stitch_fc)
    moments = (
        conv_moment,
        bias_moment,
        stitch_conv_moment,
        fc_moment,
        fc_bias_moment,
        stitch_fc_moment,
    )
    rates = (LEARN_RATE, BIAS_RATE, STITCH_RATE, LEARN_RATE, BIAS_RATE, STITCH_RATE)
    fresh = [MOMENTUM * moments[place] + grads[place] for place in range(6)]
    updated = [params[place] - rates[place] * fresh[place] for place in range(6)]
    return (features_out, images_grad, *updated, *fresh)


def four_by_four(
    images,
    conv_weight,
    conv_bias,
    stitch_conv,
    fc_weight,
    fc_bias,
    stitch_fc,
    conv_moment,
    bias_moment,
    stitch_conv_moment,
    fc_moment,
    fc_bias_moment,
    stitch_fc_moment,
    cotangent,
    task_mask,
):
    chips, planes = lax.axis_size("chan") // 2, lax.axis_size("batch")
    me, plane = lax.axis_index("chan"), lax.axis_index("batch")
    core, chip = me % 2, me // 2
    as_scalar = lambda value: value.reshape(1).astype(jnp.int32)
    core_at, chip_at, plane_at = as_scalar(core), as_scalar(chip), as_scalar(plane)
    swap = lambda value: trade(value, "chan", 1)
    per_core, side, width_in = images.shape[0], images.shape[2], images.shape[-1]
    shard = conv_weight.shape[-1]
    units = fc_weight.shape[-1]
    half = planes // 2

    as_rows = lambda value: jnp.transpose(value, (0, 1, 2, 4, 3)).reshape(2, TAPS * shard, width_in)
    keep, give = pack_kernels(as_rows(conv_weight), conv_bias, stitch_conv, core_at)
    starts = [(plane ^ k).astype(jnp.uint32) * jnp.uint32(PORTION) for k in range(planes)]
    keep, give, core_at, chip_at, plane_at, first_core, starts = tie(
        keep, give, core_at, chip_at, plane_at, core == 0, starts
    )
    mine = lambda a, b: jnp.where(first_core, a, b)
    keep_y, give_x = trade(keep, "chan", 4), trade(give, "chan", 3)
    keep_x, give_y = tie(trade(keep, "chan", 2), trade(give, "chan", 5))
    keep_d, give_d = trade(keep_y, "chan", 2), trade(give_x, "chan", 4)
    kernel_parts = [keep, swap(give), keep_x, give_x, keep_y, give_y, keep_d, give_d]

    towers = lax.optimization_barrier(jnp.transpose(images, (1, 2, 3, 0, 4)))
    keep, give = (jnp.where(first_core, towers[a], towers[1 - a]) for a in range(2))
    tower_images = jnp.concatenate([keep, swap(give)], axis=2)
    tower_images = jnp.pad(tower_images, ((1, 1), (1, 1), (0, 0), (0, 0)))

    fc_own, fc_give = fc_prepare(fc_weight, core_at, keep_x)
    fc_cross = swap(fc_give)

    pooled, slope, small_all, joined = conv_forward(tower_images, kernel_parts, core_at, chip_at)
    pooled_other = swap(pooled)
    pieces = mix_pieces(pooled, pooled_other, small_all, core_at, plane_at, planes)
    got = exchange_planes(pieces)
    gathered = gather_chips(jnp.stack(got[:half]), jnp.stack(got[half:]), chips)
    tower_rows, *partial = fc_forward(
        [part for pair in gathered for part in pair], (fc_own, fc_cross), chip_at, chips, planes
    )
    other_rows = swap(tower_rows)

    crossed, own = reduce_planes(partial[planes:], partial[:planes])
    fc_out = [total(own), swap(total(crossed))]
    fc_out = [fc_out[a] + mine(fc_bias[a], fc_bias[1 - a]) for a in range(2)]
    acts, slopes = zip(*[silu_and_slope(value) for value in fc_out])
    mix = [[mine(stitch_fc[a, b], stitch_fc[1 - a, 1 - b]) for b in range(2)] for a in range(2)]
    features = [mix[a][0] * acts[0] + mix[a][1] * acts[1] for a in range(2)]
    features_out = jnp.stack([mine(features[0], features[1]), mine(features[1], features[0])], axis=1)
    masked = [cotangent[:, t].astype(WIDE) * task_mask[:, t].astype(WIDE)[:, None] for t in range(2)]
    out_grad = [mine(masked[a], masked[1 - a]) for a in range(2)]
    grad_low = [(slopes[b] * (mix[0][b] * out_grad[0] + mix[1][b] * out_grad[1])).astype(LOW) for b in range(2)]
    stitch_fc_grad = jnp.concatenate(
        [jnp.sum(out_grad[a] * acts[b], axis=0, keepdims=True) for a in range(2) for b in range(2)]
    )
    packed = jnp.concatenate(
        [
            jnp.pad(stitch_fc_grad[:, at : at + width_in], ((0, 0), (0, max(0, at + width_in - units))))
            for at in range(0, units, width_in)
        ]
    ).astype(LOW)
    grads_other, grads_own = spread_planes(grad_low[1], grad_low[0])
    grads_own[1], packed = tie(grads_own[1], packed)
    grads_cross = swap(jnp.stack(grads_other))

    step = done = None

    def update_own(gate, value):
        nonlocal step, done
        *step, done = fc_update(fc_weight, fc_moment, tower_rows, grads_own, core_at, 0, 0, None, gate)
        value, done = tie(value, done)
        return gate, value

    blocks = fc_backward(grads_own, grads_cross, (fc_own, fc_cross), chip_at, chips, planes)
    first, second = scatter_chips(
        [blocks[2 * j : 2 * j + 2] for j in range(chips)], chips, later=update_own
    )
    sums = [total([value[i] for value in part]).astype(LOW) for part in (first, second) for i in range(half)]
    mixed_grad = exchange_planes(sums)
    *step, token = fc_update(fc_weight, fc_moment, tower_rows, grads_own, core_at, 0, 1, step, sums[-1])
    mixed_grad[1], done, token = tie(mixed_grad[1], done, token)
    done = done + token
    mixed_grad_other = swap(jnp.stack(mixed_grad))

    *blocks, conv_grad = conv_backward(
        done, mixed_grad, mixed_grad_other, pooled, pooled_other, slope, tower_images, small_all, core_at, chip_at, plane_at
    )

    def turned_conv(grad):
        return lax.conv_general_dilated(
            grad,
            kernel[::-1, ::-1],
            (1, 1),
            "SAME",
            dimension_numbers=("HWNC", "HWIO", "HWNC"),
            preferred_element_type=WIDE,
        ).astype(LOW)

    kernel = joined.reshape(3, 3, -1, width_in)
    def update_early(*pair):
        nonlocal step, done
        *step, done = fc_update(fc_weight, fc_moment, other_rows, grads_other, core_at, 1, 0, step, blocks[0])
        *pair, done = tie(*pair, done)
        return pair

    def update_late(gate, value):
        nonlocal step, done
        *step, token = fc_update(fc_weight, fc_moment, other_rows, grads_other, core_at, 1, 1, step, gate)
        value, done, token = tie(value, done, token)
        done = done + token
        return gate, value

    first, second = scatter_chips(
        [blocks[2 * j : 2 * j + 2] for j in range(chips)], chips, update_early, update_late
    )
    lines = TAPS * shard + EXTRA

    fill = lambda count: jnp.zeros((count, width_in), LOW)
    spare = planes * PORTION - lines
    flats = (
        jnp.concatenate([total(first).astype(LOW), packed, fill(spare - packed.shape[0])]),
        jnp.concatenate([swap(total(second).astype(LOW)), fill(spare)]),
    )
    nothing = jnp.uint32(0)
    quarters = [
        [lax.dynamic_slice(flat, (start, nothing), (PORTION, width_in)) for start in starts] for flat in flats
    ]
    quarters = exchange_planes([jnp.concatenate(pair) for pair in zip(*quarters)])
    quarters[0], conv_grad = tie(quarters[0], conv_grad)
    quarters[1], images_grad = tie(quarters[1], turned_conv(conv_grad))
    quarter = total(quarters).astype(LOW)
    quarters = exchange_planes([quarter] * planes)

    images_grad, quarters[0] = tie(images_grad, quarters[0])
    keep, got = images_grad[:, :, :per_core], swap(images_grad[:, :, per_core:])
    images_grad = order_towers(keep, got, core_at)
    images_grad = jnp.transpose(images_grad, (3, 1, 2, 0, 4))

    *new_small, images_grad = small_update(
        done,
        images_grad,
        quarters,
        lines,
        (as_rows(conv_weight), conv_bias, stitch_conv, stitch_fc),
        (as_rows(conv_moment), bias_moment, stitch_conv_moment, stitch_fc_moment),
        core_at,
        plane_at,
    )

    fc_bias_grad = [sum(jnp.sum(value.astype(WIDE), axis=0) for value in grads) for grads in (grads_own, grads_other)]
    fc_bias_grad = jnp.stack([mine(fc_bias_grad[a], fc_bias_grad[1 - a]) for a in range(2)])
    new_fc_bias_moment = MOMENTUM * fc_bias_moment + fc_bias_grad
    new_fc_bias = fc_bias - BIAS_RATE * new_fc_bias_moment

    as_given = lambda value: jnp.swapaxes(value.reshape(2, 3, 3, shard, width_in), 3, 4)
    params, fresh = new_small[:4], new_small[4:]
    params[0], fresh[0] = as_given(params[0]), as_given(fresh[0])
    params[3:3], fresh[3:3] = (step[0], new_fc_bias), (step[1], new_fc_bias_moment)
    images_grad = jnp.transpose(images_grad, (0, 3, 1, 2, 4))
    return (features_out.astype(LOW), images_grad, *params, *fresh)


def solution(mesh):
    chan_last = P(None, None, None, None, "chan")
    fc_spec = P(None, "batch", "chan")
    params = (chan_last, P(None, "chan"), P(None, None, "chan"), fc_spec, P(None, "chan"), P(None, None, "chan"))
    image_spec = P(("batch", "chan"), None, None, None, None)
    feature_spec = P("batch", None, "chan")
    in_specs = (image_spec, *params, *params, feature_spec, P("batch", None))
    out_specs = (feature_spec, image_spec, *params, *params)
    body = four_by_four if dict(mesh.shape) == {"chan": 8, "batch": 4} else any_mesh
    return jax.shard_map(body, mesh=mesh, in_specs=in_specs, out_specs=out_specs, check_vma=False)
```

```python
import functools

import jax
import jax.numpy as jnp
from jax import lax
from jax.experimental.layout import Layout, with_layout_constraint
from jax.experimental import pallas as pl
from jax.experimental.pallas import tpu as pltpu
from jax.sharding import PartitionSpec as P

MOMENTUM = 0.9
LEARN_RATE = 0.002
BIAS_RATE = 0.02
STITCH_RATE = 0.02
LOW = jnp.bfloat16
WIDE = jnp.float32
TAPS = 9
CELLS = 36
EXTRA = 16
PORTION = 80
LANES = 128
WHOLE = pl.BlockSpec(memory_space=pltpu.VMEM)
SCALARS = pl.BlockSpec(memory_space=pltpu.SMEM)
BRIEF = pl.CostEstimate(flops=0, bytes_accessed=0, transcendentals=0)
NN = (((1,), (0,)), ((), ()))
NT = (((1,), (1,)), ((), ()))
TN = (((0,), (0,)), ((), ()))


def like(shape, dtype):
    return jax.ShapeDtypeStruct(shape, dtype)


def dot(a, b, dims):
    return lax.dot_general(a, b, dims, preferred_element_type=WIDE)


def trade(value, axis, bit):
    size = lax.axis_size(axis)
    return lax.ppermute(value, axis, [(i, i ^ bit) for i in range(size)])


def tie(*values):
    return lax.optimization_barrier(values)


def gather_chips(first, second, chips):
    if chips == 4:
        first_y = trade(first, "chan", 4)
        second_x = trade(second, "chan", 2)
        first_x = trade(first, "chan", 2)
        second_y = trade(second, "chan", 4)
        first_d = trade(first_y, "chan", 2)
        second_d = trade(second_x, "chan", 4)
        return [(first, second), (first_x, second_x), (first_y, second_y), (first_d, second_d)]
    return [(first, second)] + [
        (trade(first, "chan", 2 * j), trade(second, "chan", 2 * j)) for j in range(1, chips)
    ]


def add_low(a, b):
    return (a.astype(WIDE) + b.astype(WIDE)).astype(LOW)


def scatter_chips(parts, chips, early=lambda *values: values, later=lambda gate, *values: values):
    if chips == 4:
        from_x = trade(parts[3][0], "chan", 2)
        from_y = trade(parts[3][1], "chan", 4)
        first_x, second_y = trade(parts[1][0], "chan", 2), trade(parts[2][1], "chan", 4)
        from_x, from_y = early(from_x, from_y)
        to_y = add_low(parts[2][0], from_x)
        first_y = trade(to_y, "chan", 4)
        to_x = add_low(parts[1][1], from_y)
        second_x = trade(to_x, "chan", 2)
        first_x, second_y, first_y = later(to_x, first_x, second_y, first_y)
        return (parts[0][0], first_x, first_y), (parts[0][1], second_x, second_y)
    got = [(trade(parts[j][0], "chan", 2 * j), trade(parts[j][1], "chan", 2 * j)) for j in range(1, chips)]
    return (
        (parts[0][0],) + tuple(pair[0] for pair in got),
        (parts[0][1],) + tuple(pair[1] for pair in got),
    )


def total(values):
    out = values[0].astype(WIDE)
    for value in values[1:]:
        out = out + value.astype(WIDE)
    return out


def exchange_planes(parts):
    got = {k: trade(parts[k], "batch", k) for k in range(len(parts) - 1, 0, -1)}
    return [parts[0]] + [got[k] for k in range(1, len(parts))]


def reduce_planes(*lists):
    passed = [trade(parts[3], "batch", 1) for parts in lists]
    near = [trade(parts[1], "batch", 1) for parts in lists]
    far = [trade(add_low(parts[2], term), "batch", 2) for parts, term in zip(lists, passed)]
    return [[parts[0], a, b] for parts, a, b in zip(lists, near, far)]


def spread_planes(first, second):
    far = [trade(value, "batch", 2) for value in (first, second)]
    near = [trade(value, "batch", 1) for value in (first, second)]
    passed = [trade(value, "batch", 1) for value in far]
    return [list(values) for values in zip((first, second), near, far, passed)]


def gate_of(value):
    return 1.0 / (1.0 + jnp.exp(-value))


def silu_and_slope(value):
    gate = gate_of(value)
    act = value * gate
    return act, gate + act * (1.0 - gate)


def lane_place(width):
    return lax.broadcasted_iota(jnp.int32, (1, LANES), 1) // width


def shift_slots(value, width, source, target):
    if source == target:
        return value
    return pltpu.roll(value, ((target - source) * width) % LANES, 1)


def pack_kernels(conv_weight, conv_bias, stitch_conv, core):
    _, lines, width_in = conv_weight.shape
    shard = conv_bias.shape[-1]

    def kernel(core_ref, w_hbm, bias_hbm, mix_hbm, keep_ref, give_ref, w_ref, bias_ref, mix_ref, sems):
        pairs = ((bias_hbm, bias_ref), (mix_hbm, mix_ref), (w_hbm, w_ref))
        copies = [pltpu.make_async_copy(source, held, sems.at[i]) for i, (source, held) in enumerate(pairs)]
        for copy in copies:
            copy.start()
        first = core_ref[0] == 0
        for copy in copies:
            copy.wait()
        for a, out in enumerate((keep_ref, give_ref)):
            out[:lines, :] = w_ref[core_ref[0] ^ a].astype(LOW)
            choose = lambda p, q: jnp.where(first, *((q, p) if a else (p, q)))
            rows = [
                choose(bias_ref[0:1, :], bias_ref[1:2, :]),
                choose(mix_ref[0, 0:1, :], mix_ref[1, 1:2, :]),
                choose(mix_ref[0, 1:2, :], mix_ref[1, 0:1, :]),
                choose(mix_ref[1, 0:1, :], mix_ref[0, 1:2, :]),
                jnp.zeros((EXTRA - 4, shard), WIDE),
            ]
            out[lines:, :] = jnp.zeros((EXTRA, width_in), LOW)
            out[lines:, :shard] = jnp.concatenate(rows, axis=0).astype(LOW)

    sources = (conv_weight, conv_bias, stitch_conv)
    return pl.pallas_call(
        kernel,
        in_specs=[SCALARS] + [pl.BlockSpec(memory_space=pltpu.HBM)] * 3,
        out_specs=[WHOLE] * 2,
        out_shape=[like((lines + EXTRA, width_in), LOW)] * 2,
        scratch_shapes=[pltpu.VMEM(value.shape, WIDE) for value in sources] + [pltpu.SemaphoreType.DMA((3,))],
        compiler_params=pltpu.CompilerParams(vmem_limit_bytes=8 << 20),
        cost_estimate=BRIEF,
    )(core, *(pltpu.with_memory_space_constraint(value, pltpu.HBM) for value in sources))


def fc_prepare(fc_weight, core, which, gate):
    _, rows, units = fc_weight.shape
    width = rows // CELLS
    fc_weight = pltpu.with_memory_space_constraint(fc_weight, pltpu.HBM)

    def kernel(core_ref, source, _, out):
        for cell in range(CELLS):
            out[pl.ds(cell * width, width), :] = source[0, pl.ds(cell, width, stride=CELLS), :].astype(LOW)

    return pl.pallas_call(
        kernel,
        grid_spec=pltpu.PrefetchScalarGridSpec(
            num_scalar_prefetch=1,
            grid=(units // LANES,),
            in_specs=[
                pl.BlockSpec((1, rows, LANES), lambda j, core: (core[0] ^ which, 0, j)),
                pl.BlockSpec(memory_space=pl.ANY),
            ],
            out_specs=pl.BlockSpec((rows, LANES), lambda j, core: (0, j)),
        ),
        out_shape=like((rows, units), LOW),
        compiler_params=pltpu.CompilerParams(vmem_limit_bytes=6 << 20),
        cost_estimate=pl.CostEstimate(flops=0, bytes_accessed=6 * rows * units, transcendentals=0),
    )(core, fc_weight, gate)


def conv_forward(images, parts, core, chip):
    high, wide, group, width_in = images.shape
    side = high - 2
    count = len(parts)
    shard = (parts[0].shape[0] - EXTRA) // TAPS
    full = shard * count
    slots = LANES // shard

    def kernel(core_ref, chip_ref, x_ref, *refs):
        pieces = refs[:count]
        pooled_ref, low_ref, slope_out, small_ref, weights_out = refs[count : count + 5]
        weights, acc, slope_ref, sems = refs[count + 5 :]
        copies = [pltpu.make_async_copy(slope_ref.at[h], slope_out.at[h], sems.at[h]) for h in range(side)]
        copies += [
            pltpu.make_async_copy(
                weights.at[:, pl.ds(tap * width_in, width_in)], weights_out.at[tap], sems.at[side + tap]
            )
            for tap in range(TAPS)
        ]
        lane = lax.broadcasted_iota(jnp.int32, (EXTRA, LANES), 1) // shard
        smalls = [jnp.zeros((EXTRA, LANES), WIDE) for _ in range(full // LANES)]
        for j in range(count // 2):
            for r in range(2):
                piece = pieces[2 * j + r]
                where = (chip_ref[0] ^ j) * 2 + (core_ref[0] ^ r)
                at = pl.ds(pl.multiple_of(where * shard, shard), shard)
                for tap in range(TAPS):
                    weights[at, tap * width_in : (tap + 1) * width_in] = piece[tap * shard : (tap + 1) * shard, :]
                row = piece[TAPS * shard :, :LANES].astype(WIDE)
                spread = row
                for s in range(1, slots):
                    spread = spread + pltpu.roll(row, s * shard, 1)
                for v in range(len(smalls)):
                    smalls[v] = jnp.where(lane + v * slots == where, spread, smalls[v])
        for v, value in enumerate(smalls):
            small_ref[:, v * LANES : (v + 1) * LANES] = value
        for copy in copies[side:]:
            copy.start()
        line = side * group
        bias = small_ref[0:1, :]
        def products(low, high_row):
            tall = high_row - low
            windows = [
                x_ref[tap // 3 + low : tap // 3 + high_row, tap % 3 : tap % 3 + side].reshape(tall * line, width_in)
                for tap in range(TAPS)
            ]
            acc[low * line : high_row * line, :] = dot(jnp.concatenate(windows, axis=1), weights[...], NT)

        def activate(low, high_row):
            for h in range(low, high_row):
                value, slope = silu_and_slope(acc[h * line : (h + 1) * line, :] + bias)
                slope_ref[h] = slope.reshape(side, group, full).astype(LOW)
                acc[h * line : (h + 1) * line, :] = value
                copies[h].start()

        blocks = [(low, min(low + 2, side)) for low in range(0, side, 2)]
        for n, block in enumerate(blocks):
            products(*block)
            if n:
                activate(*blocks[n - 1])
        activate(*blocks[-1])
        cell = lambda h, w: acc[(h * side + w) * group : (h * side + w + 1) * group, :]
        for r in range(6):
            rows = [cell(2 * r, w) + cell(2 * r + 1, w) + cell(2 * r + 2, w) for w in range(side)]
            for c in range(6):
                value = (rows[2 * c] + rows[2 * c + 1] + rows[2 * c + 2]) * (1.0 / 9.0)
                pooled_ref[6 * r + c] = value
                low_ref[6 * r + c] = value.astype(LOW)
        for copy in copies:
            copy.wait()

    area = side * side * group
    return pl.pallas_call(
        kernel,
        in_specs=[SCALARS] * 2 + [WHOLE] * (1 + count),
        out_specs=[WHOLE, WHOLE, pl.BlockSpec(memory_space=pltpu.HBM), WHOLE, pl.BlockSpec(memory_space=pltpu.HBM)],
        out_shape=[
            like((CELLS, group, full), WIDE),
            like((CELLS, group, full), LOW),
            pltpu.HBM((side, side, group, full), LOW),
            like((EXTRA, full), WIDE),
            pltpu.HBM((TAPS, full, width_in), LOW),
        ],
        scratch_shapes=[
            pltpu.VMEM((full, TAPS * width_in), LOW),
            pltpu.VMEM((area, full), WIDE),
            pltpu.VMEM((side, side, group, full), LOW),
            pltpu.SemaphoreType.DMA((side + TAPS,)),
        ],
        compiler_params=pltpu.CompilerParams(vmem_limit_bytes=16 << 20),
        cost_estimate=BRIEF,
    )(core, chip, images, *parts)


def turn(value):
    half = value.shape[0] // 2
    return jnp.concatenate([value[half:], value[:half]], axis=0)


def mix_pieces(pooled, other, small, core, plane, planes):
    cells, group, full = pooled.shape
    width = full // planes
    per = LANES // width

    def kernel(core_ref, plane_ref, a_ref, b_ref, small_ref, *refs):
        outs, held = refs[:planes], refs[planes]
        first = core_ref[0] == 0
        place = lane_place(width)
        one, two = small_ref[1:2, :], small_ref[2:3, :]
        for start in range(0, cells, per):
            mixed = [
                one * a_ref[start + i] + two * turn(b_ref[start + i].astype(WIDE)) for i in range(per)
            ]
            mixed = [jnp.where(first, value, turn(value)) for value in mixed]
            for p in range(planes):
                column, source = divmod(p * width, LANES)
                out = None
                for i in range(per):
                    moved = shift_slots(
                        mixed[i][:, column * LANES : (column + 1) * LANES], width, source // width, i
                    )
                    out = moved if out is None else jnp.where(place == i, moved, out)
                held[p, :, start * width : (start + per) * width] = out.astype(LOW)
        for k in range(planes):
            outs[k][...] = held[plane_ref[0] ^ k]

    rows = cells * width
    return pl.pallas_call(
        kernel,
        in_specs=[SCALARS] * 2 + [WHOLE] * 3,
        out_specs=[WHOLE] * planes,
        out_shape=[like((group, rows), LOW)] * planes,
        scratch_shapes=[pltpu.VMEM((planes, group, rows), LOW)],
        compiler_params=pltpu.CompilerParams(vmem_limit_bytes=8 << 20),
        cost_estimate=BRIEF,
    )(core, plane, pooled, other, small)


def fc_forward(gathered, weights, chip, chips, planes):
    half, group, rows = gathered[0].shape
    units = weights[0].shape[-1]
    count = 2 * chips
    block = chips * group

    def kernel(chip_ref, *refs):
        pieces, (own, cross) = refs[:count], refs[count : count + 2]
        rows_ref, outs = refs[count + 2], refs[count + 3 :]
        for j in range(chips):
            for h in range(2):
                for i in range(half):
                    start = ((h * half + i) * chips + (chip_ref[0] ^ j)) * group
                    rows_ref[pl.ds(pl.multiple_of(start, group), group), :] = pieces[2 * j + h][i]
        for n, weight in enumerate((own, cross)):
            part = dot(rows_ref[...], weight[...], NN)
            for k in range(planes):
                out = outs[n * planes + k]
                out[...] = part[k * block : (k + 1) * block].astype(out.dtype)

    n_images = planes * block
    return pl.pallas_call(
        kernel,
        in_specs=[SCALARS] + [WHOLE] * (count + 2),
        out_specs=[WHOLE] * (1 + 2 * planes),
        out_shape=[like((n_images, rows), LOW)]
        + [like((block, units), LOW if k else WIDE) for k in range(planes)] * 2,
        compiler_params=pltpu.CompilerParams(vmem_limit_bytes=16 << 20),
        cost_estimate=BRIEF,
    )(chip, *gathered, *weights)


def fc_backward(ready, grads, crossed, weights, chip, chips, planes):
    block, units = grads[0].shape
    rows = weights[0].shape[0]
    group = block // chips
    half = planes // 2
    n_images = planes * block

    def kernel(chip_ref, _, *refs):
        pieces, got = refs[:planes], refs[planes]
        own, cross = refs[planes + 1 : planes + 3]
        outs = refs[planes + 3 : planes + 3 + 2 * chips]
        held_own, held_cross, held = refs[planes + 4 + 2 * chips :]
        for k in range(planes):
            held_own[pl.ds(k * block, block), :] = pieces[k][...]
            held_cross[pl.ds(k * block, block), :] = got[k]
        step = rows // 3
        for s in range(3):
            at = pl.ds(s * step, step)
            value = dot(held_own[...], own[at, :], NT) + dot(held_cross[...], cross[at, :], NT)
            held[:, at] = value.astype(LOW)
        for j in range(chips):
            for h in range(2):
                for i in range(half):
                    start = ((h * half + i) * chips + (chip_ref[0] ^ j)) * group
                    outs[2 * j + h][i] = held[pl.ds(pl.multiple_of(start, group), group), :]

    return pl.pallas_call(
        kernel,
        in_specs=[SCALARS, pl.BlockSpec(memory_space=pltpu.HBM)] + [WHOLE] * (planes + 3),
        out_specs=[WHOLE] * (2 * chips) + [pl.BlockSpec(memory_space=pltpu.HBM)],
        out_shape=[like((half, group, rows), LOW)] * (2 * chips) + [pltpu.HBM(ready.shape, ready.dtype)],
        input_output_aliases={1: 2 * chips},
        scratch_shapes=[
            pltpu.VMEM((n_images, units), LOW),
            pltpu.VMEM((n_images, units), LOW),
            pltpu.VMEM((n_images, rows), LOW),
        ],
        compiler_params=pltpu.CompilerParams(vmem_limit_bytes=20 << 20),
        cost_estimate=BRIEF,
    )(chip, ready, *grads, crossed, *weights)


def conv_backward(gate, own, other, pooled, pooled_other, slope, images, small, core, chip, plane):
    planes = len(own)
    cells, group, full = pooled.shape
    high, _, _, width_in = images.shape
    side = high - 2
    width = full // planes
    per = LANES // width
    columns = full // LANES
    shards = lax.axis_size("chan")
    shard = full // shards
    slots = LANES // shard
    area = side * side * group

    def covering(h):
        return [r for r in range(6) if 2 * r <= h <= 2 * r + 2]

    def kernel(core_ref, chip_ref, plane_ref, gate_ref, *refs):
        own_refs, other_ref = refs[:planes], refs[planes]
        a_ref, b_ref, slope_ref, x_ref, small_ref = refs[planes + 1 : planes + 6]
        outs = refs[planes + 6 : planes + 6 + shards]
        grad_out = refs[planes + 6 + shards]
        flat, pool_grad, turned, taps, smalls, grad_ref, sem = refs[planes + 7 + shards :]
        copy = pltpu.make_async_copy(grad_ref, grad_out, sem)
        place = lane_place(width)
        first = core_ref[0] == 0
        for k in range(planes):
            for t, value in enumerate((own_refs[k][...], other_ref[k])):
                value = value.astype(WIDE)
                flat[t, plane_ref[0] ^ k] = jnp.where(first, value, turn(value))
        one, back = small_ref[1:2, :] * (1.0 / 9.0), small_ref[3:4, :] * (1.0 / 9.0)
        sum_one = jnp.zeros((group, full), WIDE)
        sum_two = jnp.zeros((group, full), WIDE)
        for cell in range(cells):
            column, source = divmod(cell * width, LANES)
            both = []
            for t in range(2):
                blocks = []
                for v in range(columns):
                    out = None
                    for i in range(per):
                        piece = flat[t, v * per + i, :, column * LANES : (column + 1) * LANES]
                        moved = shift_slots(piece, width, source // width, i)
                        out = moved if out is None else jnp.where(place == i, moved, out)
                    blocks.append(out)
                both.append(jnp.concatenate(blocks, axis=1))
            sum_one += both[0] * a_ref[cell]
            sum_two += both[0] * turn(b_ref[cell].astype(WIDE))
            pool_grad[cell] = one * both[0] + back * both[1]
        sum_bias = jnp.zeros((group, full), WIDE)
        for h in range(side):
            line = [sum(pool_grad[6 * r + c] for r in covering(h)) for c in range(6)]
            for w in range(side):
                value = sum(line[c] for c in covering(w))
                value = (value * slope_ref[h, w].astype(WIDE)).astype(LOW)
                grad_ref[h, w] = value
                sum_bias += value.astype(WIDE)
        copy.start()
        turned[...] = grad_ref[...].reshape(area, full).T
        for start in range(0, TAPS, 2):
            some = range(start, min(start + 2, TAPS))
            windows = [
                x_ref[tap // 3 : tap // 3 + side, tap % 3 : tap % 3 + side].reshape(area, width_in) for tap in some
            ]
            part = dot(turned[...], jnp.concatenate(windows, axis=1), NN)
            for n, tap in enumerate(some):
                taps[tap] = part[:, n * width_in : (n + 1) * width_in].astype(LOW)
        sums = [jnp.sum(value, axis=0, keepdims=True) for value in (sum_bias, sum_one, sum_two)]
        sums = jnp.concatenate(sums + [jnp.zeros((EXTRA - 3, full), WIDE)], axis=0)
        for v in range(columns):
            smalls[v] = sums[:, v * LANES : (v + 1) * LANES]
        lane = lax.broadcasted_iota(jnp.int32, (EXTRA, LANES), 1)
        for j in range(shards // 2):
            for r in range(2):
                where = (chip_ref[0] ^ j) * 2 + (core_ref[0] ^ r)
                at = pl.ds(pl.multiple_of(where * shard, shard), shard)
                out = outs[2 * j + r]
                for tap in range(TAPS):
                    out[tap * shard : (tap + 1) * shard, :] = taps[tap, at, :]
                row = smalls[where // slots]
                value = jnp.zeros((EXTRA, LANES), WIDE)
                for s in range(slots):
                    moved = row if s == 0 else pltpu.roll(row, LANES - s * shard, 1)
                    value = jnp.where(where % slots == s, moved, value)
                out[TAPS * shard :, :] = jnp.zeros((EXTRA, width_in), LOW)
                out[TAPS * shard :, :LANES] = jnp.where(lane < shard, value, 0.0).astype(LOW)
        copy.wait()

    return pl.pallas_call(
        kernel,
        in_specs=[SCALARS] * 3 + [pl.BlockSpec(memory_space=pl.ANY)] + [WHOLE] * (planes + 6),
        out_specs=[WHOLE] * shards + [pl.BlockSpec(memory_space=pltpu.HBM)],
        out_shape=[like((TAPS * shard + EXTRA, width_in), LOW)] * shards
        + [pltpu.HBM((side, side, group, full), LOW)],
        scratch_shapes=[
            pltpu.VMEM((2, planes, group, cells * width), WIDE),
            pltpu.VMEM((cells, group, full), WIDE),
            pltpu.VMEM((full, area), LOW),
            pltpu.VMEM((TAPS, full, width_in), LOW),
            pltpu.VMEM((columns, EXTRA, LANES), WIDE),
            pltpu.VMEM((side, side, group, full), LOW),
            pltpu.SemaphoreType.DMA(()),
        ],
        compiler_params=pltpu.CompilerParams(vmem_limit_bytes=14 << 20),
        cost_estimate=BRIEF,
    )(core, chip, plane, gate, *own, other, pooled, pooled_other, slope, images, small)


def fc_update(weight, moment, rows, grads, core, which, part, previous, gate):
    _, depth, units = weight.shape
    width = depth // CELLS
    n_images = rows.shape[0]
    planes = len(grads)
    block = n_images // planes
    columns = units // LANES
    steps = 4
    few = width // 2
    tall = depth // 2 // steps
    hbm = pl.BlockSpec(memory_space=pltpu.HBM)

    def kernel(core_ref, w_ref, m_ref, rows_ref, *refs):
        grad_refs = refs[:planes]
        new_w, new_m, token, joined, product, held_w, held_m, sems = refs[-8:]
        tower = core_ref[0] ^ which
        token[...] = jnp.zeros_like(token)
        for k in range(planes):
            joined[pl.ds(k * block, block), :] = grad_refs[k][...]
        for v in range(columns):
            grad = dot(rows_ref[...], joined[:, v * LANES : (v + 1) * LANES], TN)
            for cell in range(CELLS):
                start = cell * width + part * few
                product[v, pl.ds(cell, few, stride=CELLS), :] = grad[start : start + few]
        stores = []
        for s in range(steps):
            at = pl.ds((part * steps + s) * tall, tall)
            for v in range(columns):
                lanes = slice(v * LANES, (v + 1) * LANES)
                fresh = MOMENTUM * m_ref[tower, at, lanes] + product[v, s * tall : (s + 1) * tall, :]
                held_m[s, :, lanes] = fresh
                held_w[s, :, lanes] = w_ref[tower, at, lanes] - LEARN_RATE * fresh
            for i, (held, out) in enumerate(((held_w, new_w), (held_m, new_m))):
                stores.append(pltpu.make_async_copy(held.at[s], out.at[tower, at, :], sems.at[s, i]))
                stores[-1].start()
        for copy in stores:
            copy.wait()

    anywhere = pl.BlockSpec(memory_space=pl.ANY)
    extra = [] if previous is None else list(previous)
    return pl.pallas_call(
        kernel,
        in_specs=[SCALARS] + [WHOLE] * (3 + planes) + [hbm] * len(extra) + [anywhere],
        out_specs=[hbm, hbm, WHOLE],
        out_shape=[pltpu.HBM(weight.shape, WIDE)] * 2 + [like((8, LANES), WIDE)],
        scratch_shapes=[
            pltpu.VMEM((n_images, units), LOW),
            pltpu.VMEM((columns, depth // 2, LANES), WIDE),
            pltpu.VMEM((steps, tall, units), WIDE),
            pltpu.VMEM((steps, tall, units), WIDE),
            pltpu.SemaphoreType.DMA((steps, 2)),
        ],
        input_output_aliases={} if previous is None else {4 + planes: 0, 5 + planes: 1},
        compiler_params=pltpu.CompilerParams(vmem_limit_bytes=12 << 20),
        cost_estimate=pl.CostEstimate(flops=0, bytes_accessed=8 * depth * units, transcendentals=0),
    )(core, weight, moment, rows, *grads, *extra, gate)


def order_towers(own, other, core):
    def kernel(core_ref, own_ref, other_ref, out_ref):
        out_ref[core_ref[0]] = own_ref[...]
        out_ref[1 - core_ref[0]] = other_ref[...]

    return pl.pallas_call(
        kernel,
        in_specs=[SCALARS, WHOLE, WHOLE],
        out_specs=WHOLE,
        out_shape=like((2, *own.shape), own.dtype),
        compiler_params=pltpu.CompilerParams(vmem_limit_bytes=8 << 20),
        cost_estimate=BRIEF,
    )(core, own, other)


def small_update(gate, ready, pieces, lines, params, moments, core, plane):
    planes = len(pieces)
    height, width_in = pieces[0].shape
    height = height // 2
    shard = params[1].shape[-1]
    units = params[3].shape[-1]
    count = lines - EXTRA
    rates = (LEARN_RATE, BIAS_RATE, STITCH_RATE, STITCH_RATE)

    def kernel(core_ref, plane_ref, gate_ref, ready_ref, *refs):
        piece_refs, refs = refs[:planes], refs[planes:]
        p_refs, m_refs, new_p, new_m, whole = refs[:4], refs[4:8], refs[8:12], refs[12:16], refs[17]
        for a in range(2):
            for k in range(planes):
                at = pl.ds(pl.multiple_of((plane_ref[0] ^ k) * height, height), height)
                whole[a, at, :] = piece_refs[k][a * height : (a + 1) * height, :].astype(WIDE)

        def advance(which, at, grad):
            fresh = MOMENTUM * m_refs[which][at] + grad
            new_m[which][at] = fresh
            new_p[which][at] = p_refs[which][at] - rates[which] * fresh

        first = core_ref[0] == 0
        for a in range(2):
            advance(0, core_ref[0] ^ a, whole[a, :count, :])
        rows = [[whole[a, count + i : count + i + 1, :shard] for i in range(3)] for a in range(2)]
        rows = [[jnp.where(first, rows[a][i], rows[1 - a][i]) for i in range(3)] for a in range(2)]
        for t in range(2):
            advance(1, (slice(t, t + 1), slice(None)), rows[t][0])
            advance(2, (t, slice(t, t + 1), slice(None)), rows[t][1])
            advance(2, (t, slice(1 - t, 2 - t), slice(None)), rows[t][2])
        base = lines
        parts, start = [], 0
        while start < units:
            step = min(width_in, units - start)
            parts.append(whole[0, base : base + 4, :step])
            base, start = base + 4, start + step
        packed = jnp.concatenate(parts, axis=1) if len(parts) > 1 else parts[0]
        for i in range(4):
            row = jnp.where(first, packed[i : i + 1, :], packed[3 - i : 4 - i, :])
            advance(3, (i // 2, slice(i % 2, i % 2 + 1), slice(None)), row)

    out_shape = [like(value.shape, WIDE) for value in (*params, *moments)]
    return pl.pallas_call(
        kernel,
        in_specs=[SCALARS] * 2
        + [pl.BlockSpec(memory_space=pl.ANY), pl.BlockSpec(memory_space=pltpu.HBM)]
        + [WHOLE] * (planes + 8),
        out_specs=[WHOLE] * 8 + [pl.BlockSpec(memory_space=pltpu.HBM)],
        out_shape=out_shape + [pltpu.HBM(ready.shape, ready.dtype)],
        input_output_aliases={3: 8},
        scratch_shapes=[pltpu.VMEM((2, planes * height, width_in), WIDE)],
        compiler_params=pltpu.CompilerParams(vmem_limit_bytes=12 << 20),
        cost_estimate=BRIEF,
    )(core, plane, gate, ready, *pieces, *params, *moments)


def reorder(parts, place):
    bit = 1
    while bit < len(parts):
        flip = (place & bit) != 0
        parts = [
            jax.tree.map(lambda a, b: jnp.where(flip, b, a), parts[j], parts[j ^ bit])
            for j in range(len(parts))
        ]
        bit *= 2
    return parts


def pick(stacked, place, count):
    return [lax.dynamic_index_in_dim(stacked, place ^ j, 0, keepdims=False) for j in range(count)]


def pool(values):
    rows = values[0:11:2] + values[1:12:2] + values[2:13:2]
    return (rows[:, 0:11:2] + rows[:, 1:12:2] + rows[:, 2:13:2]) * (1.0 / 9.0)


def spread(values, axis):
    values = jnp.moveaxis(values, axis, 0)
    zero = jnp.zeros_like(values[:1])
    even = jnp.concatenate([values, zero]) + jnp.concatenate([zero, values])
    inter = jnp.stack([even[:-1], values], axis=1).reshape((12,) + values.shape[1:])
    return jnp.moveaxis(jnp.concatenate([inter, even[-1:]]), 0, axis)


def any_mesh(
    images,
    conv_weight,
    conv_bias,
    stitch_conv,
    fc_weight,
    fc_bias,
    stitch_fc,
    conv_moment,
    bias_moment,
    stitch_conv_moment,
    fc_moment,
    fc_bias_moment,
    stitch_fc_moment,
    cotangent,
    task_mask,
):
    chan_size, planes = lax.axis_size("chan"), lax.axis_size("batch")
    chips = chan_size // 2
    me, plane = lax.axis_index("chan"), lax.axis_index("batch")
    core, chip = me % 2, me // 2
    swap = lambda value: trade(value, "chan", 1)
    mine = lambda a, b: jnp.where(core == 0, a, b)
    per_core, side, width_in = images.shape[0], images.shape[2], images.shape[-1]
    chan_width = conv_weight.shape[-1]
    full_chan = chan_width * chan_size
    units = fc_weight.shape[-1]
    rows = fc_weight.shape[1]
    cells = 36
    plane_chan = rows // cells
    group = 2 * per_core

    kernel_rows = jnp.transpose(conv_weight, (0, 1, 2, 4, 3)).astype(LOW)
    kernel_rows = kernel_rows.reshape(2, 9 * chan_width, width_in)
    cross = stitch_conv[:, ::-1]
    small = jnp.stack(
        [
            conv_bias,
            jnp.stack([stitch_conv[0, 0], stitch_conv[1, 1]]),
            jnp.stack([stitch_conv[0, 1], stitch_conv[1, 0]]),
            jnp.stack([stitch_conv[1, 0], stitch_conv[0, 1]]),
        ],
        axis=1,
    ).astype(LOW)
    small = jnp.pad(small, ((0, 0), (0, 12), (0, width_in - chan_width)))
    kernel_rows = jnp.concatenate([kernel_rows, small], axis=1)
    keep = mine(kernel_rows[0], kernel_rows[1])
    got = swap(mine(kernel_rows[1], kernel_rows[0]))
    halves = mine(keep, got), mine(got, keep)
    kernel_parts = gather_chips(halves[0], halves[1], chips)

    keep = mine(images[:, 0], images[:, 1])
    got = swap(mine(images[:, 1], images[:, 0]))
    tower_images = jnp.concatenate([mine(keep, got), mine(got, keep)], axis=0)
    tower_images = jnp.transpose(tower_images, (1, 2, 0, 3))

    fc_low = fc_weight.astype(LOW).reshape(2, plane_chan, cells, units)
    fc_low = jnp.swapaxes(fc_low, 1, 2).reshape(2, rows, units)
    fc_keep = mine(fc_low[0], fc_low[1])
    fc_got = swap(mine(fc_low[1], fc_low[0]))
    fc_halves = mine(fc_keep, fc_got), mine(fc_got, fc_keep)

    ordered = reorder(kernel_parts, chip)
    kernel = jnp.concatenate(
        [half[: 9 * chan_width].reshape(9, chan_width, width_in) for pair in ordered for half in pair],
        axis=1,
    )
    small_all = jnp.concatenate(
        [half[9 * chan_width :, :chan_width] for pair in ordered for half in pair], axis=1
    ).astype(WIDE)
    bias_all, self_mix, cross_mix, back_mix = (small_all[i] for i in range(4))

    conv_out = lax.conv_general_dilated(
        tower_images,
        kernel.reshape(3, 3, full_chan, width_in),
        (1, 1),
        "SAME",
        dimension_numbers=("HWNC", "HWOI", "HWNC"),
        preferred_element_type=WIDE,
    )
    act, slope = silu_and_slope(conv_out + bias_all)
    pooled = pool(act)
    pooled_other = swap(pooled)
    mixed = (self_mix * pooled + cross_mix * pooled_other).astype(LOW)
    mixed = mixed.reshape(cells, group, planes, plane_chan)
    pieces = jnp.transpose(mixed, (2, 1, 0, 3)).reshape(planes, group, rows)
    got = exchange_planes(pick(pieces, plane, planes))
    half = planes // 2
    gathered = reorder(
        gather_chips(jnp.stack(got[:half]), jnp.stack(got[half:]), chips), chip
    )
    tower_rows = jnp.concatenate(
        [jnp.stack([pair[h] for pair in gathered], axis=1) for h in range(2)], axis=0
    )
    tower_rows = tower_rows.reshape(planes * chips * group, rows)
    other_rows = swap(tower_rows)

    fc_tower = jnp.concatenate(fc_halves, axis=1)
    partial = jnp.dot(tower_rows, fc_tower, preferred_element_type=WIDE).astype(LOW)
    partial = partial.reshape(planes, chips * group, 2 * units)
    fc_sum = total(exchange_planes([partial[k] for k in range(planes)]))
    fc_keep = mine(fc_sum[:, :units], fc_sum[:, units:])
    fc_got = swap(mine(fc_sum[:, units:], fc_sum[:, :units]))
    fc_out = [mine(fc_keep, fc_got) + fc_bias[0], mine(fc_got, fc_keep) + fc_bias[1]]

    acts, slopes = zip(*[silu_and_slope(value) for value in fc_out])
    features_out = jnp.stack(
        [stitch_fc[t, 0] * acts[0] + stitch_fc[t, 1] * acts[1] for t in range(2)], axis=1
    ).astype(LOW)
    out_grad = [
        cotangent[:, t].astype(WIDE) * task_mask[:, t].astype(WIDE)[:, None] for t in range(2)
    ]
    stitch_fc_grad = jnp.stack(
        [jnp.stack([jnp.sum(out_grad[t] * acts[s], axis=0) for s in range(2)]) for t in range(2)]
    )
    grad_low = jnp.stack(
        [
            (slopes[s] * (stitch_fc[0, s] * out_grad[0] + stitch_fc[1, s] * out_grad[1])).astype(LOW)
            for s in range(2)
        ]
    )
    grad_all = exchange_planes([grad_low] * planes)
    grad_all = jnp.stack(grad_all, axis=1).reshape(2, planes * chips * group, units)
    grad_keep = mine(grad_all[0], grad_all[1])
    grad_got = swap(mine(grad_all[1], grad_all[0]))
    grad_tower = jnp.concatenate([mine(grad_keep, grad_got), mine(grad_got, grad_keep)], axis=1)

    flat_grad = lax.dot_general(
        grad_tower, fc_tower, (((1,), (1,)), ((), ())), preferred_element_type=WIDE
    ).astype(LOW)
    flat_grad = flat_grad.reshape(2, half, chips, group, rows)
    by_chip = reorder([(flat_grad[0, :, m], flat_grad[1, :, m]) for m in range(chips)], chip)
    first, second = scatter_chips(by_chip, chips)
    sums = jnp.concatenate([total(first), total(second)]).astype(LOW)
    got = reorder(exchange_planes([sums[k] for k in range(planes)]), plane)
    mixed_grad = jnp.stack(got)
    mixed_grad_other = swap(mixed_grad)

    def unflatten(value):
        value = value.astype(WIDE).reshape(planes, group, cells, plane_chan)
        return jnp.transpose(value, (2, 1, 0, 3)).reshape(6, 6, group, full_chan)

    own_grad, other_grad = unflatten(mixed_grad), unflatten(mixed_grad_other)
    self_stitch = jnp.sum(own_grad * pooled, axis=(0, 1, 2))
    cross_stitch = jnp.sum(own_grad * pooled_other, axis=(0, 1, 2))
    pooled_grad = (self_mix * own_grad + back_mix * other_grad) * (1.0 / 9.0)
    conv_grad = (slope * spread(spread(pooled_grad, 0), 1)).astype(LOW)
    bias_grad = jnp.sum(conv_grad.astype(WIDE), axis=(0, 1, 2))

    padded = jnp.pad(tower_images, ((1, 1), (1, 1), (0, 0), (0, 0)))
    taps = []
    for down in range(3):
        for right in range(3):
            window = padded[down : down + side, right : right + side]
            taps.append(
                lax.dot_general(
                    conv_grad.reshape(-1, full_chan),
                    window.reshape(-1, width_in),
                    (((0,), (0,)), ((), ())),
                    preferred_element_type=WIDE,
                ).astype(LOW)
            )
    kernel_grad = jnp.stack(taps).reshape(9, chips, 2, chan_width, width_in)
    smalls = jnp.stack([bias_grad, self_stitch, cross_stitch]).astype(LOW)
    smalls = jnp.pad(
        smalls.reshape(3, chips, 2, chan_width), ((0, 13), (0, 0), (0, 0), (0, width_in - chan_width))
    )
    blocks = [
        tuple(
            jnp.concatenate([kernel_grad[:, m, c].reshape(9 * chan_width, width_in), smalls[:, m, c]])
            for c in range(2)
        )
        for m in range(chips)
    ]
    first, second = scatter_chips(reorder(blocks, chip), chips)
    sums = [total(first).astype(LOW), total(second).astype(LOW)]
    keep = mine(sums[0], sums[1])
    got = swap(mine(sums[1], sums[0]))
    towers = jnp.stack([mine(keep, got), mine(got, keep)])
    towers = lax.psum(towers, "batch").astype(WIDE)
    stitch_fc_grad = lax.psum(stitch_fc_grad.astype(LOW), "batch").astype(WIDE)

    images_grad = lax.conv_general_dilated(
        conv_grad,
        kernel.reshape(3, 3, full_chan, width_in)[::-1, ::-1],
        (1, 1),
        "SAME",
        dimension_numbers=("HWNC", "HWIO", "HWNC"),
        preferred_element_type=WIDE,
    ).astype(LOW)
    images_grad = jnp.transpose(images_grad, (2, 0, 1, 3))
    keep = mine(images_grad[:per_core], images_grad[per_core:])
    got = swap(mine(images_grad[per_core:], images_grad[:per_core]))
    images_grad = jnp.stack([mine(keep, got), mine(got, keep)], axis=1)

    both_rows = [mine(tower_rows, other_rows), mine(other_rows, tower_rows)]
    fc_weight_grad = jnp.stack(
        [
            lax.dot_general(
                jnp.swapaxes(both_rows[t].reshape(-1, cells, plane_chan), 1, 2).reshape(-1, rows),
                grad_all[t],
                (((0,), (0,)), ((), ())),
                preferred_element_type=WIDE,
            )
            for t in range(2)
        ]
    )
    fc_bias_grad = jnp.sum(grad_all.astype(WIDE), axis=1)

    conv_weight_grad = jnp.swapaxes(
        towers[:, : 9 * chan_width].reshape(2, 3, 3, chan_width, width_in), 3, 4
    )
    conv_bias_grad = towers[:, 9 * chan_width, :chan_width]
    straight = towers[:, 9 * chan_width + 1, :chan_width]
    crossed = towers[:, 9 * chan_width + 2, :chan_width]
    stitch_conv_grad = jnp.stack(
        [jnp.stack([straight[0], crossed[0]]), jnp.stack([crossed[1], straight[1]])]
    )
    grads = (
        conv_weight_grad,
        conv_bias_grad,
        stitch_conv_grad,
        fc_weight_grad,
        fc_bias_grad,
        stitch_fc_grad,
    )
    params = (conv_weight, conv_bias, stitch_conv, fc_weight, fc_bias, stitch_fc)
    moments = (
        conv_moment,
        bias_moment,
        stitch_conv_moment,
        fc_moment,
        fc_bias_moment,
        stitch_fc_moment,
    )
    rates = (LEARN_RATE, BIAS_RATE, STITCH_RATE, LEARN_RATE, BIAS_RATE, STITCH_RATE)
    fresh = [MOMENTUM * moments[place] + grads[place] for place in range(6)]
    updated = [params[place] - rates[place] * fresh[place] for place in range(6)]
    return (features_out, images_grad, *updated, *fresh)


def four_by_four(
    images,
    conv_weight,
    conv_bias,
    stitch_conv,
    fc_weight,
    fc_bias,
    stitch_fc,
    conv_moment,
    bias_moment,
    stitch_conv_moment,
    fc_moment,
    fc_bias_moment,
    stitch_fc_moment,
    cotangent,
    task_mask,
):
    chips, planes = lax.axis_size("chan") // 2, lax.axis_size("batch")
    me, plane = lax.axis_index("chan"), lax.axis_index("batch")
    core, chip = me % 2, me // 2
    as_scalar = lambda value: value.reshape(1).astype(jnp.int32)
    core_at, chip_at, plane_at = as_scalar(core), as_scalar(chip), as_scalar(plane)
    swap = lambda value: trade(value, "chan", 1)
    per_core, side, width_in = images.shape[0], images.shape[2], images.shape[-1]
    shard = conv_weight.shape[-1]
    units = fc_weight.shape[-1]
    half = planes // 2

    as_rows = lambda value: jnp.transpose(value, (0, 1, 2, 4, 3)).reshape(2, TAPS * shard, width_in)
    keep, give = pack_kernels(as_rows(conv_weight), conv_bias, stitch_conv, core_at)
    starts = [(plane ^ k).astype(jnp.uint32) * jnp.uint32(PORTION) for k in range(planes)]
    keep, give, core_at, chip_at, plane_at, first_core, starts = tie(
        keep, give, core_at, chip_at, plane_at, core == 0, starts
    )
    mine = lambda a, b: jnp.where(first_core, a, b)
    fc_own, fc_give = (fc_prepare(fc_weight, core_at, which, keep) for which in range(2))
    images, fc_own, fc_give = tie(images, fc_own, fc_give)
    images = with_layout_constraint(images, Layout(major_to_minor=(0, 2, 3, 1, 4)))
    towers = lax.optimization_barrier(jnp.transpose(images, (1, 2, 3, 0, 4)))
    own_images, given = (jnp.where(first_core, towers[a], towers[1 - a]) for a in range(2))
    got, keep_y, give_x, keep_x, give_y, own_images, given = tie(
        swap(give),
        trade(keep, "chan", 4),
        trade(give, "chan", 3),
        trade(keep, "chan", 2),
        trade(give, "chan", 5),
        own_images,
        given,
    )
    tower_images = jnp.concatenate([own_images, swap(given)], axis=2)
    tower_images = jnp.pad(tower_images, ((1, 1), (1, 1), (0, 0), (0, 0)))
    keep_d, give_d, tower_images = tie(trade(keep_y, "chan", 2), trade(give_x, "chan", 4), tower_images)
    kernel_parts = [keep, got, keep_x, give_x, keep_y, give_y, keep_d, give_d]

    pooled, pooled_low, slope, small_all, joined = conv_forward(tower_images, kernel_parts, core_at, chip_at)
    pooled_other = swap(pooled_low)
    pieces = mix_pieces(pooled, pooled_other, small_all, core_at, plane_at, planes)
    got = exchange_planes(pieces)
    fc_cross = swap(fc_give)
    gathered = gather_chips(jnp.stack(got[:half]), jnp.stack(got[half:]), chips)
    tower_rows, *partial = fc_forward(
        [part for pair in gathered for part in pair], (fc_own, fc_cross), chip_at, chips, planes
    )
    other_rows = swap(tower_rows)

    crossed, own = reduce_planes(partial[planes:], partial[:planes])
    fc_out = [total(own), swap(total(crossed))]
    fc_out = [fc_out[a] + mine(fc_bias[a], fc_bias[1 - a]) for a in range(2)]
    acts, slopes = zip(*[silu_and_slope(value) for value in fc_out])
    mix = [[mine(stitch_fc[a, b], stitch_fc[1 - a, 1 - b]) for b in range(2)] for a in range(2)]
    features = [mix[a][0] * acts[0] + mix[a][1] * acts[1] for a in range(2)]
    features_out = jnp.stack([mine(features[0], features[1]), mine(features[1], features[0])], axis=1)
    features_out = features_out.astype(LOW)
    masked = [cotangent[:, t].astype(WIDE) * task_mask[:, t].astype(WIDE)[:, None] for t in range(2)]
    out_grad = [mine(masked[a], masked[1 - a]) for a in range(2)]
    grad_low = [(slopes[b] * (mix[0][b] * out_grad[0] + mix[1][b] * out_grad[1])).astype(LOW) for b in range(2)]
    stitch_fc_grad = jnp.concatenate(
        [jnp.sum(out_grad[a] * acts[b], axis=0, keepdims=True) for a in range(2) for b in range(2)]
    )
    packed = jnp.concatenate(
        [
            jnp.pad(stitch_fc_grad[:, at : at + width_in], ((0, 0), (0, max(0, at + width_in - units))))
            for at in range(0, units, width_in)
        ]
    ).astype(LOW)
    grads_other, grads_own = spread_planes(grad_low[1], grad_low[0])
    grads_own[1], packed = tie(grads_own[1], packed)
    grads_cross = swap(jnp.stack(grads_other))

    step = done = None

    def update_own(gate, first_x, second_y, first_y):
        nonlocal step, done
        *step, done = fc_update(fc_weight, fc_moment, tower_rows, grads_own, core_at, 0, 0, None, gate)
        first_y, done = tie(first_y, done)
        return first_x, second_y, first_y

    *blocks, features_out = fc_backward(features_out, grads_own, grads_cross, (fc_own, fc_cross), chip_at, chips, planes)
    first, second = scatter_chips(
        [blocks[2 * j : 2 * j + 2] for j in range(chips)], chips, later=update_own
    )
    sums = [total([value[i] for value in part]).astype(LOW) for part in (first, second) for i in range(half)]
    mixed_grad = exchange_planes(sums)
    *step, token = fc_update(fc_weight, fc_moment, tower_rows, grads_own, core_at, 0, 1, step, sums[-1])
    mixed_grad[1], done, token = tie(mixed_grad[1], done, token)
    done = done + token
    mixed_grad_other = swap(jnp.stack(mixed_grad))

    *blocks, conv_grad = conv_backward(
        done, mixed_grad, mixed_grad_other, pooled, pooled_other, slope, tower_images, small_all, core_at, chip_at, plane_at
    )

    def turned_conv(grad):
        return lax.conv_general_dilated(
            grad,
            kernel[::-1, ::-1],
            (1, 1),
            "SAME",
            dimension_numbers=("HWNC", "HWIO", "HWNC"),
            preferred_element_type=WIDE,
        ).astype(LOW)

    kernel = joined.reshape(3, 3, -1, width_in)
    def update_early(*values):
        nonlocal step, done
        *step, done = fc_update(fc_weight, fc_moment, other_rows, grads_other, core_at, 1, 0, step, blocks[0])
        *values, done = tie(*values, done)
        return values

    def update_late(gate, first_x, second_y, first_y):
        nonlocal step, done
        gate, first_x, second_y = tie(gate, first_x, second_y)
        *step, token = fc_update(fc_weight, fc_moment, other_rows, grads_other, core_at, 1, 1, step, gate)
        first_y, done, token = tie(first_y, done, token)
        done = done + token
        return first_x, second_y, first_y

    other, own = scatter_chips(
        [(blocks[2 * j + 1], blocks[2 * j]) for j in range(chips)], chips, update_early, update_late
    )
    lines = TAPS * shard + EXTRA

    fill = lambda count: jnp.zeros((count, width_in), LOW)
    spare = planes * PORTION - lines
    flats = (
        jnp.concatenate([total(own).astype(LOW), packed, fill(spare - packed.shape[0])]),
        jnp.concatenate([swap(total(other).astype(LOW)), fill(spare)]),
    )
    nothing = jnp.uint32(0)
    quarters = [
        [lax.dynamic_slice(flat, (start, nothing), (PORTION, width_in)) for start in starts] for flat in flats
    ]
    quarters = exchange_planes([jnp.concatenate(pair) for pair in zip(*quarters)])
    quarters[0], conv_grad = tie(quarters[0], conv_grad)
    quarters[1], images_grad = tie(quarters[1], turned_conv(conv_grad))
    quarter = total(quarters).astype(LOW)
    quarters = exchange_planes([quarter] * planes)

    images_grad, quarters[0] = tie(images_grad, quarters[0])
    keep, got = images_grad[:, :, :per_core], swap(images_grad[:, :, per_core:])
    images_grad = order_towers(keep, got, core_at)
    images_grad = jnp.transpose(images_grad, (3, 1, 2, 0, 4))

    *new_small, images_grad = small_update(
        done,
        images_grad,
        quarters,
        lines,
        (as_rows(conv_weight), conv_bias, stitch_conv, stitch_fc),
        (as_rows(conv_moment), bias_moment, stitch_conv_moment, stitch_fc_moment),
        core_at,
        plane_at,
    )

    fc_bias_grad = [sum(jnp.sum(value.astype(WIDE), axis=0) for value in grads) for grads in (grads_own, grads_other)]
    fc_bias_grad = jnp.stack([mine(fc_bias_grad[a], fc_bias_grad[1 - a]) for a in range(2)])
    new_fc_bias_moment = MOMENTUM * fc_bias_moment + fc_bias_grad
    new_fc_bias = fc_bias - BIAS_RATE * new_fc_bias_moment

    as_given = lambda value: jnp.swapaxes(value.reshape(2, 3, 3, shard, width_in), 3, 4)
    params, fresh = new_small[:4], new_small[4:]
    params[0], fresh[0] = as_given(params[0]), as_given(fresh[0])
    params[3:3], fresh[3:3] = (step[0], new_fc_bias), (step[1], new_fc_bias_moment)
    images_grad = jnp.transpose(images_grad, (0, 3, 1, 2, 4))
    return (features_out, images_grad, *params, *fresh)


def solution(mesh):
    chan_last = P(None, None, None, None, "chan")
    fc_spec = P(None, "batch", "chan")
    params = (chan_last, P(None, "chan"), P(None, None, "chan"), fc_spec, P(None, "chan"), P(None, None, "chan"))
    image_spec = P(("batch", "chan"), None, None, None, None)
    feature_spec = P("batch", None, "chan")
    in_specs = (image_spec, *params, *params, feature_spec, P("batch", None))
    out_specs = (feature_spec, image_spec, *params, *params)
    body = four_by_four if dict(mesh.shape) == {"chan": 8, "batch": 4} else any_mesh
    return jax.shard_map(body, mesh=mesh, in_specs=in_specs, out_specs=out_specs, check_vma=False)
```

```python
import functools

import jax
import jax.numpy as jnp
from jax import lax
from jax.experimental.layout import Layout, with_layout_constraint
from jax.experimental import pallas as pl
from jax.experimental.pallas import tpu as pltpu
from jax.sharding import PartitionSpec as P

MOMENTUM = 0.9
LEARN_RATE = 0.002
BIAS_RATE = 0.02
STITCH_RATE = 0.02
LOW = jnp.bfloat16
WIDE = jnp.float32
TAPS = 9
CELLS = 36
EXTRA = 8
PORTION = 80
LANES = 128
WHOLE = pl.BlockSpec(memory_space=pltpu.VMEM)
SCALARS = pl.BlockSpec(memory_space=pltpu.SMEM)
BRIEF = pl.CostEstimate(flops=0, bytes_accessed=0, transcendentals=0)
NN = (((1,), (0,)), ((), ()))
NT = (((1,), (1,)), ((), ()))
TN = (((0,), (0,)), ((), ()))


def like(shape, dtype):
    return jax.ShapeDtypeStruct(shape, dtype)


def dot(a, b, dims):
    return lax.dot_general(a, b, dims, preferred_element_type=WIDE)


def trade(value, axis, bit):
    size = lax.axis_size(axis)
    return lax.ppermute(value, axis, [(i, i ^ bit) for i in range(size)])


def tie(*values):
    return lax.optimization_barrier(values)


def gather_chips(first, second, chips):
    if chips == 4:
        first_y = trade(first, "chan", 4)
        second_x = trade(second, "chan", 2)
        first_x = trade(first, "chan", 2)
        second_y = trade(second, "chan", 4)
        first_d = trade(first_y, "chan", 2)
        second_d = trade(second_x, "chan", 4)
        return [(first, second), (first_x, second_x), (first_y, second_y), (first_d, second_d)]
    return [(first, second)] + [
        (trade(first, "chan", 2 * j), trade(second, "chan", 2 * j)) for j in range(1, chips)
    ]


def add_low(a, b):
    return (a.astype(WIDE) + b.astype(WIDE)).astype(LOW)


def scatter_chips(parts, chips, early=lambda *values: values, later=lambda gate, *values: values):
    if chips == 4:
        from_x = trade(parts[3][0], "chan", 2)
        from_y = trade(parts[3][1], "chan", 4)
        first_x, second_y = trade(parts[1][0], "chan", 2), trade(parts[2][1], "chan", 4)
        from_x, from_y = early(from_x, from_y)
        to_y = add_low(parts[2][0], from_x)
        first_y = trade(to_y, "chan", 4)
        to_x = add_low(parts[1][1], from_y)
        second_x = trade(to_x, "chan", 2)
        first_x, second_y, first_y = later(to_x, first_x, second_y, first_y)
        return (parts[0][0], first_x, first_y), (parts[0][1], second_x, second_y)
    got = [(trade(parts[j][0], "chan", 2 * j), trade(parts[j][1], "chan", 2 * j)) for j in range(1, chips)]
    return (
        (parts[0][0],) + tuple(pair[0] for pair in got),
        (parts[0][1],) + tuple(pair[1] for pair in got),
    )


def total(values):
    out = values[0].astype(WIDE)
    for value in values[1:]:
        out = out + value.astype(WIDE)
    return out


def exchange_planes(parts):
    got = {k: trade(parts[k], "batch", k) for k in range(len(parts) - 1, 0, -1)}
    return [parts[0]] + [got[k] for k in range(1, len(parts))]


def reduce_planes(*lists):
    passed = [trade(parts[3], "batch", 1) for parts in lists]
    near = [trade(parts[1], "batch", 1) for parts in lists]
    far = [trade(add_low(parts[2], term), "batch", 2) for parts, term in zip(lists, passed)]
    return [[parts[0], a, b] for parts, a, b in zip(lists, near, far)]


def spread_planes(first, second):
    far = [trade(value, "batch", 2) for value in (first, second)]
    near = [trade(value, "batch", 1) for value in (first, second)]
    passed = [trade(value, "batch", 1) for value in far]
    return [list(values) for values in zip((first, second), near, far, passed)]


def gate_of(value):
    return 1.0 / (1.0 + jnp.exp(-value))


def silu_and_slope(value):
    gate = gate_of(value)
    act = value * gate
    return act, gate + act * (1.0 - gate)


def lane_place(width):
    return lax.broadcasted_iota(jnp.int32, (1, LANES), 1) // width


def shift_slots(value, width, source, target):
    if source == target:
        return value
    return pltpu.roll(value, ((target - source) * width) % LANES, 1)


def pack_kernels(conv_weight, conv_bias, stitch_conv, core):
    _, lines, width_in = conv_weight.shape
    shard = conv_bias.shape[-1]

    def kernel(core_ref, w_hbm, bias_hbm, mix_hbm, keep_ref, give_ref, w_ref, bias_ref, mix_ref, sems):
        pairs = ((bias_hbm, bias_ref), (mix_hbm, mix_ref), (w_hbm, w_ref))
        copies = [pltpu.make_async_copy(source, held, sems.at[i]) for i, (source, held) in enumerate(pairs)]
        for copy in copies:
            copy.start()
        first = core_ref[0] == 0
        for copy in copies:
            copy.wait()
        for a, out in enumerate((keep_ref, give_ref)):
            out[:lines, :] = w_ref[core_ref[0] ^ a].astype(LOW)
            choose = lambda p, q: jnp.where(first, *((q, p) if a else (p, q)))
            rows = [
                choose(bias_ref[0:1, :], bias_ref[1:2, :]),
                choose(mix_ref[0, 0:1, :], mix_ref[1, 1:2, :]),
                choose(mix_ref[0, 1:2, :], mix_ref[1, 0:1, :]),
                choose(mix_ref[1, 0:1, :], mix_ref[0, 1:2, :]),
                jnp.zeros((EXTRA - 4, shard), WIDE),
            ]
            out[lines:, :] = jnp.zeros((EXTRA, width_in), LOW)
            out[lines:, :shard] = jnp.concatenate(rows, axis=0).astype(LOW)

    sources = (conv_weight, conv_bias, stitch_conv)
    return pl.pallas_call(
        kernel,
        in_specs=[SCALARS] + [pl.BlockSpec(memory_space=pltpu.HBM)] * 3,
        out_specs=[WHOLE] * 2,
        out_shape=[like((lines + EXTRA, width_in), LOW)] * 2,
        scratch_shapes=[pltpu.VMEM(value.shape, WIDE) for value in sources] + [pltpu.SemaphoreType.DMA((3,))],
        compiler_params=pltpu.CompilerParams(vmem_limit_bytes=8 << 20),
        cost_estimate=BRIEF,
    )(core, *(pltpu.with_memory_space_constraint(value, pltpu.HBM) for value in sources))


def fc_prepare(fc_weight, core, which, gate):
    _, rows, units = fc_weight.shape
    width = rows // CELLS
    fc_weight = pltpu.with_memory_space_constraint(fc_weight, pltpu.HBM)

    def kernel(core_ref, source, _, out):
        for cell in range(CELLS):
            out[pl.ds(cell * width, width), :] = source[0, pl.ds(cell, width, stride=CELLS), :].astype(LOW)

    return pl.pallas_call(
        kernel,
        grid_spec=pltpu.PrefetchScalarGridSpec(
            num_scalar_prefetch=1,
            grid=(units // LANES,),
            in_specs=[
                pl.BlockSpec((1, rows, LANES), lambda j, core: (core[0] ^ which, 0, j)),
                pl.BlockSpec(memory_space=pl.ANY),
            ],
            out_specs=pl.BlockSpec((rows, LANES), lambda j, core: (0, j)),
        ),
        out_shape=like((rows, units), LOW),
        compiler_params=pltpu.CompilerParams(vmem_limit_bytes=6 << 20),
        cost_estimate=pl.CostEstimate(flops=0, bytes_accessed=6 * rows * units, transcendentals=0),
    )(core, fc_weight, gate)


def conv_forward(images, parts, core, chip):
    high, wide, group, width_in = images.shape
    side = high - 2
    count = len(parts)
    shard = (parts[0].shape[0] - EXTRA) // TAPS
    full = shard * count
    slots = LANES // shard

    def kernel(core_ref, chip_ref, x_ref, *refs):
        pieces = refs[:count]
        pooled_ref, low_ref, slope_out, small_ref, weights_out = refs[count : count + 5]
        weights, acc, slope_ref, sems = refs[count + 5 :]
        copies = [pltpu.make_async_copy(slope_ref.at[h], slope_out.at[h], sems.at[h]) for h in range(side)]
        copies += [
            pltpu.make_async_copy(
                weights.at[:, pl.ds(tap * width_in, width_in)], weights_out.at[tap], sems.at[side + tap]
            )
            for tap in range(TAPS)
        ]
        lane = lax.broadcasted_iota(jnp.int32, (EXTRA, LANES), 1) // shard
        smalls = [jnp.zeros((EXTRA, LANES), WIDE) for _ in range(full // LANES)]
        for j in range(count // 2):
            for r in range(2):
                piece = pieces[2 * j + r]
                where = (chip_ref[0] ^ j) * 2 + (core_ref[0] ^ r)
                at = pl.ds(pl.multiple_of(where * shard, shard), shard)
                for tap in range(TAPS):
                    weights[at, tap * width_in : (tap + 1) * width_in] = piece[tap * shard : (tap + 1) * shard, :]
                row = piece[TAPS * shard :, :LANES].astype(WIDE)
                spread = row
                for s in range(1, slots):
                    spread = spread + pltpu.roll(row, s * shard, 1)
                for v in range(len(smalls)):
                    smalls[v] = jnp.where(lane + v * slots == where, spread, smalls[v])
        for v, value in enumerate(smalls):
            small_ref[:, v * LANES : (v + 1) * LANES] = value
        for copy in copies[side:]:
            copy.start()
        line = side * group
        bias = small_ref[0:1, :]
        def products(low, high_row):
            tall = high_row - low
            windows = [
                x_ref[tap // 3 + low : tap // 3 + high_row, tap % 3 : tap % 3 + side].reshape(tall * line, width_in)
                for tap in range(TAPS)
            ]
            acc[low * line : high_row * line, :] = dot(jnp.concatenate(windows, axis=1), weights[...], NT)

        def activate(low, high_row):
            for h in range(low, high_row):
                value, slope = silu_and_slope(acc[h * line : (h + 1) * line, :] + bias)
                slope_ref[h] = slope.reshape(side, group, full).astype(LOW)
                acc[h * line : (h + 1) * line, :] = value
                copies[h].start()

        blocks = [(low, min(low + 2, side)) for low in range(0, side, 2)]
        for n, block in enumerate(blocks):
            products(*block)
            if n:
                activate(*blocks[n - 1])
        activate(*blocks[-1])
        cell = lambda h, w: acc[(h * side + w) * group : (h * side + w + 1) * group, :]
        for r in range(6):
            rows = [cell(2 * r, w) + cell(2 * r + 1, w) + cell(2 * r + 2, w) for w in range(side)]
            for c in range(6):
                value = (rows[2 * c] + rows[2 * c + 1] + rows[2 * c + 2]) * (1.0 / 9.0)
                pooled_ref[6 * r + c] = value
                low_ref[6 * r + c] = value.astype(LOW)
        for copy in copies:
            copy.wait()

    area = side * side * group
    return pl.pallas_call(
        kernel,
        in_specs=[SCALARS] * 2 + [WHOLE] * (1 + count),
        out_specs=[WHOLE, WHOLE, pl.BlockSpec(memory_space=pltpu.HBM), WHOLE, pl.BlockSpec(memory_space=pltpu.HBM)],
        out_shape=[
            like((CELLS, group, full), WIDE),
            like((CELLS, group, full), LOW),
            pltpu.HBM((side, side, group, full), LOW),
            like((EXTRA, full), WIDE),
            pltpu.HBM((TAPS, full, width_in), LOW),
        ],
        scratch_shapes=[
            pltpu.VMEM((full, TAPS * width_in), LOW),
            pltpu.VMEM((area, full), WIDE),
            pltpu.VMEM((side, side, group, full), LOW),
            pltpu.SemaphoreType.DMA((side + TAPS,)),
        ],
        compiler_params=pltpu.CompilerParams(vmem_limit_bytes=16 << 20),
        cost_estimate=BRIEF,
    )(core, chip, images, *parts)


def turn(value):
    half = value.shape[0] // 2
    return jnp.concatenate([value[half:], value[:half]], axis=0)


def mix_pieces(pooled, other, small, core, plane, planes):
    cells, group, full = pooled.shape
    width = full // planes
    per = LANES // width

    def kernel(core_ref, plane_ref, a_ref, b_ref, small_ref, *refs):
        outs, held = refs[:planes], refs[planes]
        first = core_ref[0] == 0
        place = lane_place(width)
        one, two = small_ref[1:2, :], small_ref[2:3, :]
        for start in range(0, cells, per):
            mixed = [
                one * a_ref[start + i] + two * turn(b_ref[start + i].astype(WIDE)) for i in range(per)
            ]
            mixed = [jnp.where(first, value, turn(value)) for value in mixed]
            for p in range(planes):
                column, source = divmod(p * width, LANES)
                out = None
                for i in range(per):
                    moved = shift_slots(
                        mixed[i][:, column * LANES : (column + 1) * LANES], width, source // width, i
                    )
                    out = moved if out is None else jnp.where(place == i, moved, out)
                held[p, :, start * width : (start + per) * width] = out.astype(LOW)
        for k in range(planes):
            outs[k][...] = held[plane_ref[0] ^ k]

    rows = cells * width
    return pl.pallas_call(
        kernel,
        in_specs=[SCALARS] * 2 + [WHOLE] * 3,
        out_specs=[WHOLE] * planes,
        out_shape=[like((group, rows), LOW)] * planes,
        scratch_shapes=[pltpu.VMEM((planes, group, rows), LOW)],
        compiler_params=pltpu.CompilerParams(vmem_limit_bytes=8 << 20),
        cost_estimate=BRIEF,
    )(core, plane, pooled, other, small)


def fc_forward(gathered, weights, chip, chips, planes):
    half, group, rows = gathered[0].shape
    units = weights[0].shape[-1]
    count = 2 * chips
    block = chips * group

    def kernel(chip_ref, *refs):
        pieces, (own, cross) = refs[:count], refs[count : count + 2]
        rows_ref, outs = refs[count + 2], refs[count + 3 :]
        for j in range(chips):
            for h in range(2):
                for i in range(half):
                    start = ((h * half + i) * chips + (chip_ref[0] ^ j)) * group
                    rows_ref[pl.ds(pl.multiple_of(start, group), group), :] = pieces[2 * j + h][i]
        for n, weight in enumerate((own, cross)):
            part = dot(rows_ref[...], weight[...], NN)
            for k in range(planes):
                out = outs[n * planes + k]
                out[...] = part[k * block : (k + 1) * block].astype(out.dtype)

    n_images = planes * block
    return pl.pallas_call(
        kernel,
        in_specs=[SCALARS] + [WHOLE] * (count + 2),
        out_specs=[WHOLE] * (1 + 2 * planes),
        out_shape=[like((n_images, rows), LOW)]
        + [like((block, units), LOW if k else WIDE) for k in range(planes)] * 2,
        compiler_params=pltpu.CompilerParams(vmem_limit_bytes=16 << 20),
        cost_estimate=BRIEF,
    )(chip, *gathered, *weights)


def fc_backward(ready, grads, crossed, weights, chip, chips, planes):
    block, units = grads[0].shape
    rows = weights[0].shape[0]
    group = block // chips
    half = planes // 2
    n_images = planes * block

    def kernel(chip_ref, _, *refs):
        pieces, got = refs[:planes], refs[planes]
        own, cross = refs[planes + 1 : planes + 3]
        outs = refs[planes + 3 : planes + 3 + 2 * chips]
        held_own, held_cross, held = refs[planes + 4 + 2 * chips :]
        for k in range(planes):
            held_own[pl.ds(k * block, block), :] = pieces[k][...]
            held_cross[pl.ds(k * block, block), :] = got[k]
        step = rows // 3
        for s in range(3):
            at = pl.ds(s * step, step)
            value = dot(held_own[...], own[at, :], NT) + dot(held_cross[...], cross[at, :], NT)
            held[:, at] = value.astype(LOW)
        for j in range(chips):
            for h in range(2):
                for i in range(half):
                    start = ((h * half + i) * chips + (chip_ref[0] ^ j)) * group
                    outs[2 * j + h][i] = held[pl.ds(pl.multiple_of(start, group), group), :]

    return pl.pallas_call(
        kernel,
        in_specs=[SCALARS, pl.BlockSpec(memory_space=pltpu.HBM)] + [WHOLE] * (planes + 3),
        out_specs=[WHOLE] * (2 * chips) + [pl.BlockSpec(memory_space=pltpu.HBM)],
        out_shape=[like((half, group, rows), LOW)] * (2 * chips) + [pltpu.HBM(ready.shape, ready.dtype)],
        input_output_aliases={1: 2 * chips},
        scratch_shapes=[
            pltpu.VMEM((n_images, units), LOW),
            pltpu.VMEM((n_images, units), LOW),
            pltpu.VMEM((n_images, rows), LOW),
        ],
        compiler_params=pltpu.CompilerParams(vmem_limit_bytes=20 << 20),
        cost_estimate=BRIEF,
    )(chip, ready, *grads, crossed, *weights)


def conv_backward(gate, own, other, pooled, pooled_other, slope, images, small, core, chip, plane):
    planes = len(own)
    cells, group, full = pooled.shape
    high, _, _, width_in = images.shape
    side = high - 2
    width = full // planes
    per = LANES // width
    columns = full // LANES
    shards = lax.axis_size("chan")
    shard = full // shards
    slots = LANES // shard
    area = side * side * group

    def covering(h):
        return [r for r in range(6) if 2 * r <= h <= 2 * r + 2]

    def kernel(core_ref, chip_ref, plane_ref, gate_ref, *refs):
        own_refs, other_ref = refs[:planes], refs[planes]
        a_ref, b_ref, slope_ref, x_ref, small_ref = refs[planes + 1 : planes + 6]
        outs = refs[planes + 6 : planes + 6 + shards]
        grad_out = refs[planes + 6 + shards]
        flat, pool_grad, turned, taps, smalls, grad_ref, sem = refs[planes + 7 + shards :]
        copy = pltpu.make_async_copy(grad_ref, grad_out, sem)
        place = lane_place(width)
        first = core_ref[0] == 0
        for k in range(planes):
            for t, value in enumerate((own_refs[k][...], other_ref[k])):
                value = value.astype(WIDE)
                flat[t, plane_ref[0] ^ k] = jnp.where(first, value, turn(value))
        one, back = small_ref[1:2, :] * (1.0 / 9.0), small_ref[3:4, :] * (1.0 / 9.0)
        sum_one = jnp.zeros((group, full), WIDE)
        sum_two = jnp.zeros((group, full), WIDE)
        for cell in range(cells):
            column, source = divmod(cell * width, LANES)
            both = []
            for t in range(2):
                blocks = []
                for v in range(columns):
                    out = None
                    for i in range(per):
                        piece = flat[t, v * per + i, :, column * LANES : (column + 1) * LANES]
                        moved = shift_slots(piece, width, source // width, i)
                        out = moved if out is None else jnp.where(place == i, moved, out)
                    blocks.append(out)
                both.append(jnp.concatenate(blocks, axis=1))
            sum_one += both[0] * a_ref[cell]
            sum_two += both[0] * turn(b_ref[cell].astype(WIDE))
            pool_grad[cell] = one * both[0] + back * both[1]
        sum_bias = jnp.zeros((group, full), WIDE)
        for h in range(side):
            line = [sum(pool_grad[6 * r + c] for r in covering(h)) for c in range(6)]
            for w in range(side):
                value = sum(line[c] for c in covering(w))
                value = (value * slope_ref[h, w].astype(WIDE)).astype(LOW)
                grad_ref[h, w] = value
                sum_bias += value.astype(WIDE)
        copy.start()
        turned[...] = grad_ref[...].reshape(area, full).T
        for start in range(0, TAPS, 2):
            some = range(start, min(start + 2, TAPS))
            windows = [
                x_ref[tap // 3 : tap // 3 + side, tap % 3 : tap % 3 + side].reshape(area, width_in) for tap in some
            ]
            part = dot(turned[...], jnp.concatenate(windows, axis=1), NN)
            for n, tap in enumerate(some):
                taps[tap] = part[:, n * width_in : (n + 1) * width_in].astype(LOW)
        sums = [jnp.sum(value, axis=0, keepdims=True) for value in (sum_bias, sum_one, sum_two)]
        sums = jnp.concatenate(sums + [jnp.zeros((EXTRA - 3, full), WIDE)], axis=0)
        for v in range(columns):
            smalls[v] = sums[:, v * LANES : (v + 1) * LANES]
        lane = lax.broadcasted_iota(jnp.int32, (EXTRA, LANES), 1)
        for j in range(shards // 2):
            for r in range(2):
                where = (chip_ref[0] ^ j) * 2 + (core_ref[0] ^ r)
                at = pl.ds(pl.multiple_of(where * shard, shard), shard)
                out = outs[2 * j + r]
                for tap in range(TAPS):
                    out[tap * shard : (tap + 1) * shard, :] = taps[tap, at, :]
                row = smalls[where // slots]
                value = jnp.zeros((EXTRA, LANES), WIDE)
                for s in range(slots):
                    moved = row if s == 0 else pltpu.roll(row, LANES - s * shard, 1)
                    value = jnp.where(where % slots == s, moved, value)
                out[TAPS * shard :, :] = jnp.zeros((EXTRA, width_in), LOW)
                out[TAPS * shard :, :LANES] = jnp.where(lane < shard, value, 0.0).astype(LOW)
        copy.wait()

    return pl.pallas_call(
        kernel,
        in_specs=[SCALARS] * 3 + [pl.BlockSpec(memory_space=pl.ANY)] + [WHOLE] * (planes + 6),
        out_specs=[WHOLE] * shards + [pl.BlockSpec(memory_space=pltpu.HBM)],
        out_shape=[like((TAPS * shard + EXTRA, width_in), LOW)] * shards
        + [pltpu.HBM((side, side, group, full), LOW)],
        scratch_shapes=[
            pltpu.VMEM((2, planes, group, cells * width), WIDE),
            pltpu.VMEM((cells, group, full), WIDE),
            pltpu.VMEM((full, area), LOW),
            pltpu.VMEM((TAPS, full, width_in), LOW),
            pltpu.VMEM((columns, EXTRA, LANES), WIDE),
            pltpu.VMEM((side, side, group, full), LOW),
            pltpu.SemaphoreType.DMA(()),
        ],
        compiler_params=pltpu.CompilerParams(vmem_limit_bytes=14 << 20),
        cost_estimate=BRIEF,
    )(core, chip, plane, gate, *own, other, pooled, pooled_other, slope, images, small)


def fc_update(weight, moment, rows, grads, core, which, part, previous, gate):
    _, depth, units = weight.shape
    width = depth // CELLS
    n_images = rows.shape[0]
    planes = len(grads)
    block = n_images // planes
    columns = units // LANES
    steps = 4
    few = width // 2
    tall = depth // 2 // steps
    hbm = pl.BlockSpec(memory_space=pltpu.HBM)

    def kernel(core_ref, w_ref, m_ref, rows_ref, *refs):
        grad_refs = refs[:planes]
        new_w, new_m, token, joined, product, held_w, held_m, sems = refs[-8:]
        tower = core_ref[0] ^ which
        token[...] = jnp.zeros_like(token)
        for k in range(planes):
            joined[pl.ds(k * block, block), :] = grad_refs[k][...]
        for v in range(columns):
            grad = dot(rows_ref[...], joined[:, v * LANES : (v + 1) * LANES], TN)
            for cell in range(CELLS):
                start = cell * width + part * few
                product[v, pl.ds(cell, few, stride=CELLS), :] = grad[start : start + few]
        stores = []
        for s in range(steps):
            at = pl.ds((part * steps + s) * tall, tall)
            for v in range(columns):
                lanes = slice(v * LANES, (v + 1) * LANES)
                fresh = MOMENTUM * m_ref[tower, at, lanes] + product[v, s * tall : (s + 1) * tall, :]
                held_m[s, :, lanes] = fresh
                held_w[s, :, lanes] = w_ref[tower, at, lanes] - LEARN_RATE * fresh
            for i, (held, out) in enumerate(((held_w, new_w), (held_m, new_m))):
                stores.append(pltpu.make_async_copy(held.at[s], out.at[tower, at, :], sems.at[s, i]))
                stores[-1].start()
        for copy in stores:
            copy.wait()

    anywhere = pl.BlockSpec(memory_space=pl.ANY)
    extra = [] if previous is None else list(previous)
    return pl.pallas_call(
        kernel,
        in_specs=[SCALARS] + [WHOLE] * (3 + planes) + [hbm] * len(extra) + [anywhere],
        out_specs=[hbm, hbm, WHOLE],
        out_shape=[pltpu.HBM(weight.shape, WIDE)] * 2 + [like((8, LANES), WIDE)],
        scratch_shapes=[
            pltpu.VMEM((n_images, units), LOW),
            pltpu.VMEM((columns, depth // 2, LANES), WIDE),
            pltpu.VMEM((steps, tall, units), WIDE),
            pltpu.VMEM((steps, tall, units), WIDE),
            pltpu.SemaphoreType.DMA((steps, 2)),
        ],
        input_output_aliases={} if previous is None else {4 + planes: 0, 5 + planes: 1},
        compiler_params=pltpu.CompilerParams(vmem_limit_bytes=12 << 20),
        cost_estimate=pl.CostEstimate(flops=0, bytes_accessed=8 * depth * units, transcendentals=0),
    )(core, weight, moment, rows, *grads, *extra, gate)


def order_towers(own, other, core):
    def kernel(core_ref, own_ref, other_ref, out_ref):
        out_ref[core_ref[0]] = own_ref[...]
        out_ref[1 - core_ref[0]] = other_ref[...]

    return pl.pallas_call(
        kernel,
        in_specs=[SCALARS, WHOLE, WHOLE],
        out_specs=WHOLE,
        out_shape=like((2, *own.shape), own.dtype),
        compiler_params=pltpu.CompilerParams(vmem_limit_bytes=8 << 20),
        cost_estimate=BRIEF,
    )(core, own, other)


def small_update(gate, ready, pieces, lines, params, moments, core, plane):
    planes = len(pieces)
    height, width_in = pieces[0].shape
    height = height // 2
    shard = params[1].shape[-1]
    units = params[3].shape[-1]
    count = lines - EXTRA
    rates = (LEARN_RATE, BIAS_RATE, STITCH_RATE, STITCH_RATE)

    def kernel(core_ref, plane_ref, gate_ref, ready_ref, *refs):
        piece_refs, refs = refs[:planes], refs[planes:]
        p_refs, m_refs, new_p, new_m, whole = refs[:4], refs[4:8], refs[8:12], refs[12:16], refs[17]
        for a in range(2):
            for k in range(planes):
                at = pl.ds(pl.multiple_of((plane_ref[0] ^ k) * height, height), height)
                whole[a, at, :] = piece_refs[k][a * height : (a + 1) * height, :].astype(WIDE)

        def advance(which, at, grad):
            fresh = MOMENTUM * m_refs[which][at] + grad
            new_m[which][at] = fresh
            new_p[which][at] = p_refs[which][at] - rates[which] * fresh

        first = core_ref[0] == 0
        for a in range(2):
            advance(0, core_ref[0] ^ a, whole[a, :count, :])
        rows = [[whole[a, count + i : count + i + 1, :shard] for i in range(3)] for a in range(2)]
        rows = [[jnp.where(first, rows[a][i], rows[1 - a][i]) for i in range(3)] for a in range(2)]
        for t in range(2):
            advance(1, (slice(t, t + 1), slice(None)), rows[t][0])
            advance(2, (t, slice(t, t + 1), slice(None)), rows[t][1])
            advance(2, (t, slice(1 - t, 2 - t), slice(None)), rows[t][2])
        base = lines
        parts, start = [], 0
        while start < units:
            step = min(width_in, units - start)
            parts.append(whole[0, base : base + 4, :step])
            base, start = base + 4, start + step
        packed = jnp.concatenate(parts, axis=1) if len(parts) > 1 else parts[0]
        for i in range(4):
            row = jnp.where(first, packed[i : i + 1, :], packed[3 - i : 4 - i, :])
            advance(3, (i // 2, slice(i % 2, i % 2 + 1), slice(None)), row)

    out_shape = [like(value.shape, WIDE) for value in (*params, *moments)]
    return pl.pallas_call(
        kernel,
        in_specs=[SCALARS] * 2
        + [pl.BlockSpec(memory_space=pl.ANY), pl.BlockSpec(memory_space=pltpu.HBM)]
        + [WHOLE] * (planes + 8),
        out_specs=[WHOLE] * 8 + [pl.BlockSpec(memory_space=pltpu.HBM)],
        out_shape=out_shape + [pltpu.HBM(ready.shape, ready.dtype)],
        input_output_aliases={3: 8},
        scratch_shapes=[pltpu.VMEM((2, planes * height, width_in), WIDE)],
        compiler_params=pltpu.CompilerParams(vmem_limit_bytes=12 << 20),
        cost_estimate=BRIEF,
    )(core, plane, gate, ready, *pieces, *params, *moments)


def reorder(parts, place):
    bit = 1
    while bit < len(parts):
        flip = (place & bit) != 0
        parts = [
            jax.tree.map(lambda a, b: jnp.where(flip, b, a), parts[j], parts[j ^ bit])
            for j in range(len(parts))
        ]
        bit *= 2
    return parts


def pick(stacked, place, count):
    return [lax.dynamic_index_in_dim(stacked, place ^ j, 0, keepdims=False) for j in range(count)]


def pool(values):
    rows = values[0:11:2] + values[1:12:2] + values[2:13:2]
    return (rows[:, 0:11:2] + rows[:, 1:12:2] + rows[:, 2:13:2]) * (1.0 / 9.0)


def spread(values, axis):
    values = jnp.moveaxis(values, axis, 0)
    zero = jnp.zeros_like(values[:1])
    even = jnp.concatenate([values, zero]) + jnp.concatenate([zero, values])
    inter = jnp.stack([even[:-1], values], axis=1).reshape((12,) + values.shape[1:])
    return jnp.moveaxis(jnp.concatenate([inter, even[-1:]]), 0, axis)


def any_mesh(
    images,
    conv_weight,
    conv_bias,
    stitch_conv,
    fc_weight,
    fc_bias,
    stitch_fc,
    conv_moment,
    bias_moment,
    stitch_conv_moment,
    fc_moment,
    fc_bias_moment,
    stitch_fc_moment,
    cotangent,
    task_mask,
):
    chan_size, planes = lax.axis_size("chan"), lax.axis_size("batch")
    chips = chan_size // 2
    me, plane = lax.axis_index("chan"), lax.axis_index("batch")
    core, chip = me % 2, me // 2
    swap = lambda value: trade(value, "chan", 1)
    mine = lambda a, b: jnp.where(core == 0, a, b)
    per_core, side, width_in = images.shape[0], images.shape[2], images.shape[-1]
    chan_width = conv_weight.shape[-1]
    full_chan = chan_width * chan_size
    units = fc_weight.shape[-1]
    rows = fc_weight.shape[1]
    cells = 36
    plane_chan = rows // cells
    group = 2 * per_core

    kernel_rows = jnp.transpose(conv_weight, (0, 1, 2, 4, 3)).astype(LOW)
    kernel_rows = kernel_rows.reshape(2, 9 * chan_width, width_in)
    cross = stitch_conv[:, ::-1]
    small = jnp.stack(
        [
            conv_bias,
            jnp.stack([stitch_conv[0, 0], stitch_conv[1, 1]]),
            jnp.stack([stitch_conv[0, 1], stitch_conv[1, 0]]),
            jnp.stack([stitch_conv[1, 0], stitch_conv[0, 1]]),
        ],
        axis=1,
    ).astype(LOW)
    small = jnp.pad(small, ((0, 0), (0, 12), (0, width_in - chan_width)))
    kernel_rows = jnp.concatenate([kernel_rows, small], axis=1)
    keep = mine(kernel_rows[0], kernel_rows[1])
    got = swap(mine(kernel_rows[1], kernel_rows[0]))
    halves = mine(keep, got), mine(got, keep)
    kernel_parts = gather_chips(halves[0], halves[1], chips)

    keep = mine(images[:, 0], images[:, 1])
    got = swap(mine(images[:, 1], images[:, 0]))
    tower_images = jnp.concatenate([mine(keep, got), mine(got, keep)], axis=0)
    tower_images = jnp.transpose(tower_images, (1, 2, 0, 3))

    fc_low = fc_weight.astype(LOW).reshape(2, plane_chan, cells, units)
    fc_low = jnp.swapaxes(fc_low, 1, 2).reshape(2, rows, units)
    fc_keep = mine(fc_low[0], fc_low[1])
    fc_got = swap(mine(fc_low[1], fc_low[0]))
    fc_halves = mine(fc_keep, fc_got), mine(fc_got, fc_keep)

    ordered = reorder(kernel_parts, chip)
    kernel = jnp.concatenate(
        [half[: 9 * chan_width].reshape(9, chan_width, width_in) for pair in ordered for half in pair],
        axis=1,
    )
    small_all = jnp.concatenate(
        [half[9 * chan_width :, :chan_width] for pair in ordered for half in pair], axis=1
    ).astype(WIDE)
    bias_all, self_mix, cross_mix, back_mix = (small_all[i] for i in range(4))

    conv_out = lax.conv_general_dilated(
        tower_images,
        kernel.reshape(3, 3, full_chan, width_in),
        (1, 1),
        "SAME",
        dimension_numbers=("HWNC", "HWOI", "HWNC"),
        preferred_element_type=WIDE,
    )
    act, slope = silu_and_slope(conv_out + bias_all)
    pooled = pool(act)
    pooled_other = swap(pooled)
    mixed = (self_mix * pooled + cross_mix * pooled_other).astype(LOW)
    mixed = mixed.reshape(cells, group, planes, plane_chan)
    pieces = jnp.transpose(mixed, (2, 1, 0, 3)).reshape(planes, group, rows)
    got = exchange_planes(pick(pieces, plane, planes))
    half = planes // 2
    gathered = reorder(
        gather_chips(jnp.stack(got[:half]), jnp.stack(got[half:]), chips), chip
    )
    tower_rows = jnp.concatenate(
        [jnp.stack([pair[h] for pair in gathered], axis=1) for h in range(2)], axis=0
    )
    tower_rows = tower_rows.reshape(planes * chips * group, rows)
    other_rows = swap(tower_rows)

    fc_tower = jnp.concatenate(fc_halves, axis=1)
    partial = jnp.dot(tower_rows, fc_tower, preferred_element_type=WIDE).astype(LOW)
    partial = partial.reshape(planes, chips * group, 2 * units)
    fc_sum = total(exchange_planes([partial[k] for k in range(planes)]))
    fc_keep = mine(fc_sum[:, :units], fc_sum[:, units:])
    fc_got = swap(mine(fc_sum[:, units:], fc_sum[:, :units]))
    fc_out = [mine(fc_keep, fc_got) + fc_bias[0], mine(fc_got, fc_keep) + fc_bias[1]]

    acts, slopes = zip(*[silu_and_slope(value) for value in fc_out])
    features_out = jnp.stack(
        [stitch_fc[t, 0] * acts[0] + stitch_fc[t, 1] * acts[1] for t in range(2)], axis=1
    ).astype(LOW)
    out_grad = [
        cotangent[:, t].astype(WIDE) * task_mask[:, t].astype(WIDE)[:, None] for t in range(2)
    ]
    stitch_fc_grad = jnp.stack(
        [jnp.stack([jnp.sum(out_grad[t] * acts[s], axis=0) for s in range(2)]) for t in range(2)]
    )
    grad_low = jnp.stack(
        [
            (slopes[s] * (stitch_fc[0, s] * out_grad[0] + stitch_fc[1, s] * out_grad[1])).astype(LOW)
            for s in range(2)
        ]
    )
    grad_all = exchange_planes([grad_low] * planes)
    grad_all = jnp.stack(grad_all, axis=1).reshape(2, planes * chips * group, units)
    grad_keep = mine(grad_all[0], grad_all[1])
    grad_got = swap(mine(grad_all[1], grad_all[0]))
    grad_tower = jnp.concatenate([mine(grad_keep, grad_got), mine(grad_got, grad_keep)], axis=1)

    flat_grad = lax.dot_general(
        grad_tower, fc_tower, (((1,), (1,)), ((), ())), preferred_element_type=WIDE
    ).astype(LOW)
    flat_grad = flat_grad.reshape(2, half, chips, group, rows)
    by_chip = reorder([(flat_grad[0, :, m], flat_grad[1, :, m]) for m in range(chips)], chip)
    first, second = scatter_chips(by_chip, chips)
    sums = jnp.concatenate([total(first), total(second)]).astype(LOW)
    got = reorder(exchange_planes([sums[k] for k in range(planes)]), plane)
    mixed_grad = jnp.stack(got)
    mixed_grad_other = swap(mixed_grad)

    def unflatten(value):
        value = value.astype(WIDE).reshape(planes, group, cells, plane_chan)
        return jnp.transpose(value, (2, 1, 0, 3)).reshape(6, 6, group, full_chan)

    own_grad, other_grad = unflatten(mixed_grad), unflatten(mixed_grad_other)
    self_stitch = jnp.sum(own_grad * pooled, axis=(0, 1, 2))
    cross_stitch = jnp.sum(own_grad * pooled_other, axis=(0, 1, 2))
    pooled_grad = (self_mix * own_grad + back_mix * other_grad) * (1.0 / 9.0)
    conv_grad = (slope * spread(spread(pooled_grad, 0), 1)).astype(LOW)
    bias_grad = jnp.sum(conv_grad.astype(WIDE), axis=(0, 1, 2))

    padded = jnp.pad(tower_images, ((1, 1), (1, 1), (0, 0), (0, 0)))
    taps = []
    for down in range(3):
        for right in range(3):
            window = padded[down : down + side, right : right + side]
            taps.append(
                lax.dot_general(
                    conv_grad.reshape(-1, full_chan),
                    window.reshape(-1, width_in),
                    (((0,), (0,)), ((), ())),
                    preferred_element_type=WIDE,
                ).astype(LOW)
            )
    kernel_grad = jnp.stack(taps).reshape(9, chips, 2, chan_width, width_in)
    smalls = jnp.stack([bias_grad, self_stitch, cross_stitch]).astype(LOW)
    smalls = jnp.pad(
        smalls.reshape(3, chips, 2, chan_width), ((0, 13), (0, 0), (0, 0), (0, width_in - chan_width))
    )
    blocks = [
        tuple(
            jnp.concatenate([kernel_grad[:, m, c].reshape(9 * chan_width, width_in), smalls[:, m, c]])
            for c in range(2)
        )
        for m in range(chips)
    ]
    first, second = scatter_chips(reorder(blocks, chip), chips)
    sums = [total(first).astype(LOW), total(second).astype(LOW)]
    keep = mine(sums[0], sums[1])
    got = swap(mine(sums[1], sums[0]))
    towers = jnp.stack([mine(keep, got), mine(got, keep)])
    towers = lax.psum(towers, "batch").astype(WIDE)
    stitch_fc_grad = lax.psum(stitch_fc_grad.astype(LOW), "batch").astype(WIDE)

    images_grad = lax.conv_general_dilated(
        conv_grad,
        kernel.reshape(3, 3, full_chan, width_in)[::-1, ::-1],
        (1, 1),
        "SAME",
        dimension_numbers=("HWNC", "HWIO", "HWNC"),
        preferred_element_type=WIDE,
    ).astype(LOW)
    images_grad = jnp.transpose(images_grad, (2, 0, 1, 3))
    keep = mine(images_grad[:per_core], images_grad[per_core:])
    got = swap(mine(images_grad[per_core:], images_grad[:per_core]))
    images_grad = jnp.stack([mine(keep, got), mine(got, keep)], axis=1)

    both_rows = [mine(tower_rows, other_rows), mine(other_rows, tower_rows)]
    fc_weight_grad = jnp.stack(
        [
            lax.dot_general(
                jnp.swapaxes(both_rows[t].reshape(-1, cells, plane_chan), 1, 2).reshape(-1, rows),
                grad_all[t],
                (((0,), (0,)), ((), ())),
                preferred_element_type=WIDE,
            )
            for t in range(2)
        ]
    )
    fc_bias_grad = jnp.sum(grad_all.astype(WIDE), axis=1)

    conv_weight_grad = jnp.swapaxes(
        towers[:, : 9 * chan_width].reshape(2, 3, 3, chan_width, width_in), 3, 4
    )
    conv_bias_grad = towers[:, 9 * chan_width, :chan_width]
    straight = towers[:, 9 * chan_width + 1, :chan_width]
    crossed = towers[:, 9 * chan_width + 2, :chan_width]
    stitch_conv_grad = jnp.stack(
        [jnp.stack([straight[0], crossed[0]]), jnp.stack([crossed[1], straight[1]])]
    )
    grads = (
        conv_weight_grad,
        conv_bias_grad,
        stitch_conv_grad,
        fc_weight_grad,
        fc_bias_grad,
        stitch_fc_grad,
    )
    params = (conv_weight, conv_bias, stitch_conv, fc_weight, fc_bias, stitch_fc)
    moments = (
        conv_moment,
        bias_moment,
        stitch_conv_moment,
        fc_moment,
        fc_bias_moment,
        stitch_fc_moment,
    )
    rates = (LEARN_RATE, BIAS_RATE, STITCH_RATE, LEARN_RATE, BIAS_RATE, STITCH_RATE)
    fresh = [MOMENTUM * moments[place] + grads[place] for place in range(6)]
    updated = [params[place] - rates[place] * fresh[place] for place in range(6)]
    return (features_out, images_grad, *updated, *fresh)


def four_by_four(
    images,
    conv_weight,
    conv_bias,
    stitch_conv,
    fc_weight,
    fc_bias,
    stitch_fc,
    conv_moment,
    bias_moment,
    stitch_conv_moment,
    fc_moment,
    fc_bias_moment,
    stitch_fc_moment,
    cotangent,
    task_mask,
):
    chips, planes = lax.axis_size("chan") // 2, lax.axis_size("batch")
    me, plane = lax.axis_index("chan"), lax.axis_index("batch")
    core, chip = me % 2, me // 2
    as_scalar = lambda value: value.reshape(1).astype(jnp.int32)
    core_at, chip_at, plane_at = as_scalar(core), as_scalar(chip), as_scalar(plane)
    swap = lambda value: trade(value, "chan", 1)
    per_core, side, width_in = images.shape[0], images.shape[2], images.shape[-1]
    shard = conv_weight.shape[-1]
    units = fc_weight.shape[-1]
    half = planes // 2

    as_rows = lambda value: jnp.transpose(value, (0, 1, 2, 4, 3)).reshape(2, TAPS * shard, width_in)
    keep, give = pack_kernels(as_rows(conv_weight), conv_bias, stitch_conv, core_at)
    starts = [(plane ^ k).astype(jnp.uint32) * jnp.uint32(PORTION) for k in range(planes)]
    keep, give, core_at, chip_at, plane_at, first_core, starts = tie(
        keep, give, core_at, chip_at, plane_at, core == 0, starts
    )
    mine = lambda a, b: jnp.where(first_core, a, b)
    fc_own, fc_give = (fc_prepare(fc_weight, core_at, which, keep) for which in range(2))
    images, fc_own, fc_give = tie(images, fc_own, fc_give)
    images = with_layout_constraint(images, Layout(major_to_minor=(0, 2, 3, 1, 4)))
    towers = lax.optimization_barrier(jnp.transpose(images, (1, 2, 3, 0, 4)))
    own_images, given = (jnp.where(first_core, towers[a], towers[1 - a]) for a in range(2))
    got, keep_y, give_x, keep_x, give_y, own_images, given = tie(
        swap(give),
        trade(keep, "chan", 4),
        trade(give, "chan", 3),
        trade(keep, "chan", 2),
        trade(give, "chan", 5),
        own_images,
        given,
    )
    tower_images = jnp.concatenate([own_images, swap(given)], axis=2)
    tower_images = jnp.pad(tower_images, ((1, 1), (1, 1), (0, 0), (0, 0)))
    keep_d, give_d, tower_images = tie(trade(keep_y, "chan", 2), trade(give_x, "chan", 4), tower_images)
    kernel_parts = [keep, got, keep_x, give_x, keep_y, give_y, keep_d, give_d]

    pooled, pooled_low, slope, small_all, joined = conv_forward(tower_images, kernel_parts, core_at, chip_at)
    pooled_other = swap(pooled_low)
    pieces = mix_pieces(pooled, pooled_other, small_all, core_at, plane_at, planes)
    got = exchange_planes(pieces)
    fc_cross = swap(fc_give)
    gathered = gather_chips(jnp.stack(got[:half]), jnp.stack(got[half:]), chips)
    tower_rows, *partial = fc_forward(
        [part for pair in gathered for part in pair], (fc_own, fc_cross), chip_at, chips, planes
    )
    other_rows = swap(tower_rows)

    crossed, own = reduce_planes(partial[planes:], partial[:planes])
    fc_out = [total(own), swap(total(crossed))]
    fc_out = [fc_out[a] + mine(fc_bias[a], fc_bias[1 - a]) for a in range(2)]
    acts, slopes = zip(*[silu_and_slope(value) for value in fc_out])
    mix = [[mine(stitch_fc[a, b], stitch_fc[1 - a, 1 - b]) for b in range(2)] for a in range(2)]
    features = [mix[a][0] * acts[0] + mix[a][1] * acts[1] for a in range(2)]
    features_out = jnp.stack([mine(features[0], features[1]), mine(features[1], features[0])], axis=1)
    features_out = features_out.astype(LOW)
    masked = [cotangent[:, t].astype(WIDE) * task_mask[:, t].astype(WIDE)[:, None] for t in range(2)]
    out_grad = [mine(masked[a], masked[1 - a]) for a in range(2)]
    grad_low = [(slopes[b] * (mix[0][b] * out_grad[0] + mix[1][b] * out_grad[1])).astype(LOW) for b in range(2)]
    stitch_fc_grad = jnp.concatenate(
        [jnp.sum(out_grad[a] * acts[b], axis=0, keepdims=True) for a in range(2) for b in range(2)]
    )
    packed = jnp.concatenate(
        [
            jnp.pad(stitch_fc_grad[:, at : at + width_in], ((0, 0), (0, max(0, at + width_in - units))))
            for at in range(0, units, width_in)
        ]
    ).astype(LOW)
    grads_other, grads_own = spread_planes(grad_low[1], grad_low[0])
    grads_own[1], packed = tie(grads_own[1], packed)
    grads_cross = swap(jnp.stack(grads_other))

    step = done = None

    def update_own(gate, first_x, second_y, first_y):
        nonlocal step, done
        *step, done = fc_update(fc_weight, fc_moment, tower_rows, grads_own, core_at, 0, 0, None, gate)
        first_y, done = tie(first_y, done)
        return first_x, second_y, first_y

    *blocks, features_out = fc_backward(features_out, grads_own, grads_cross, (fc_own, fc_cross), chip_at, chips, planes)
    first, second = scatter_chips(
        [blocks[2 * j : 2 * j + 2] for j in range(chips)], chips, later=update_own
    )
    sums = [total([value[i] for value in part]).astype(LOW) for part in (first, second) for i in range(half)]
    mixed_grad = exchange_planes(sums)
    *step, token = fc_update(fc_weight, fc_moment, tower_rows, grads_own, core_at, 0, 1, step, sums[-1])
    mixed_grad[1], done, token = tie(mixed_grad[1], done, token)
    done = done + token
    mixed_grad_other = swap(jnp.stack(mixed_grad))

    *blocks, conv_grad = conv_backward(
        done, mixed_grad, mixed_grad_other, pooled, pooled_other, slope, tower_images, small_all, core_at, chip_at, plane_at
    )

    def turned_conv(grad):
        return lax.conv_general_dilated(
            grad,
            kernel[::-1, ::-1],
            (1, 1),
            "SAME",
            dimension_numbers=("HWNC", "HWIO", "HWNC"),
            preferred_element_type=WIDE,
        ).astype(LOW)

    kernel = joined.reshape(3, 3, -1, width_in)
    def update_early(*values):
        nonlocal step, done
        *step, done = fc_update(fc_weight, fc_moment, other_rows, grads_other, core_at, 1, 0, step, blocks[0])
        *values, done = tie(*values, done)
        return values

    def update_late(gate, first_x, second_y, first_y):
        nonlocal step, done
        gate, first_x, second_y = tie(gate, first_x, second_y)
        *step, token = fc_update(fc_weight, fc_moment, other_rows, grads_other, core_at, 1, 1, step, gate)
        first_y, done, token = tie(first_y, done, token)
        done = done + token
        return first_x, second_y, first_y

    other, own = scatter_chips(
        [(blocks[2 * j + 1], blocks[2 * j]) for j in range(chips)], chips, update_early, update_late
    )
    lines = TAPS * shard + EXTRA

    fill = lambda count: jnp.zeros((count, width_in), LOW)
    spare = planes * PORTION - lines
    flats = (
        jnp.concatenate([total(own).astype(LOW), packed, fill(spare - packed.shape[0])]),
        jnp.concatenate([swap(total(other).astype(LOW)), fill(spare)]),
    )
    nothing = jnp.uint32(0)
    quarters = [
        [lax.dynamic_slice(flat, (start, nothing), (PORTION, width_in)) for start in starts] for flat in flats
    ]
    quarters = exchange_planes([jnp.concatenate(pair) for pair in zip(*quarters)])
    quarters[0], conv_grad = tie(quarters[0], conv_grad)
    quarters[1], images_grad = tie(quarters[1], turned_conv(conv_grad))
    quarter = total(quarters).astype(LOW)
    quarters = exchange_planes([quarter] * planes)

    images_grad, quarters[0] = tie(images_grad, quarters[0])
    keep, got = images_grad[:, :, :per_core], swap(images_grad[:, :, per_core:])
    images_grad = order_towers(keep, got, core_at)
    images_grad = jnp.transpose(images_grad, (3, 1, 2, 0, 4))

    *new_small, images_grad = small_update(
        done,
        images_grad,
        quarters,
        lines,
        (as_rows(conv_weight), conv_bias, stitch_conv, stitch_fc),
        (as_rows(conv_moment), bias_moment, stitch_conv_moment, stitch_fc_moment),
        core_at,
        plane_at,
    )

    fc_bias_grad = [sum(jnp.sum(value.astype(WIDE), axis=0) for value in grads) for grads in (grads_own, grads_other)]
    fc_bias_grad = jnp.stack([mine(fc_bias_grad[a], fc_bias_grad[1 - a]) for a in range(2)])
    new_fc_bias_moment = MOMENTUM * fc_bias_moment + fc_bias_grad
    new_fc_bias = fc_bias - BIAS_RATE * new_fc_bias_moment

    as_given = lambda value: jnp.swapaxes(value.reshape(2, 3, 3, shard, width_in), 3, 4)
    params, fresh = new_small[:4], new_small[4:]
    params[0], fresh[0] = as_given(params[0]), as_given(fresh[0])
    params[3:3], fresh[3:3] = (step[0], new_fc_bias), (step[1], new_fc_bias_moment)
    images_grad = jnp.transpose(images_grad, (0, 3, 1, 2, 4))
    return (features_out, images_grad, *params, *fresh)


def solution(mesh):
    chan_last = P(None, None, None, None, "chan")
    fc_spec = P(None, "batch", "chan")
    params = (chan_last, P(None, "chan"), P(None, None, "chan"), fc_spec, P(None, "chan"), P(None, None, "chan"))
    image_spec = P(("batch", "chan"), None, None, None, None)
    feature_spec = P("batch", None, "chan")
    in_specs = (image_spec, *params, *params, feature_spec, P("batch", None))
    out_specs = (feature_spec, image_spec, *params, *params)
    body = four_by_four if dict(mesh.shape) == {"chan": 8, "batch": 4} else any_mesh
    return jax.shard_map(body, mesh=mesh, in_specs=in_specs, out_specs=out_specs, check_vma=False)
```
